256 devices in a mesh: member: 8 (over x, y_lo), tile: 32 (over z, y_hi, core).
Axes of the slice: x: 4, y: 4 (y_hi: 2, y_lo: 2; y = y_hi * 2 + y_lo), z: 8, core: 2. Of those that a mesh axis runs over, the one named last changes fastest.
Arguments:
- members: float32 [8, 6, 256, 512], P('member', None, 'tile'), may hold values from -6 to 6
- condition: float32 [6, 256, 512], P(None, 'tile'), may hold values from -6 to 6
- observed: float32 [6, 256, 512], P(None, 'tile'), may hold values from -6 to 6
- kernel_in: bfloat16 [9, 64, 9], replicated, may hold values from -0.625 to 0.625
- kernel_mid: bfloat16 [9, 64, 64], replicated, may hold values from -0.25 to 0.25
- kernel_out: bfloat16 [9, 6, 64], replicated, may hold values from -0.25 to 0.25
Outputs:
- pushed: float32 [8, 6, 256, 512], P('member', None, 'tile')
- energy: float32 [], replicated
- grad_in: float32 [9, 64, 9], replicated
- grad_mid: float32 [9, 64, 64], replicated
- grad_out: float32 [9, 6, 64], replicated
The draws below stay inside these ranges and needn't reach their ends.
All inputs are finite; a program needn't handle non-finite values.
Results may differ from the reference program's by a relative error of at most 0.0004.
The reference program's roundings to bfloat16 on the way (of `inputs`, `hidden_first`, `hidden_second`, `grad_coupling` and `grad_pre_first`) count: a program that leaves them out, or rounds other values in their place, can miss the bound.
Values may be sent and summed in bfloat16 or wider, within the bound.
No kernel may reach another device: no remote copies, remote signals or barrier semaphores. Data moves between devices by JAX's collectives and lax.ppermute only.
A program may use at most 64 MiB of HBM per device.

```python
import math
import jax
import jax.numpy as jnp

VARS = 6
COND = 6
HALF = 3
CH = 64
LON = 512
NLAT = 256
MEMBERS = 8


def draw_members(key, part):
    key = jax.random.fold_in(key, 11)
    base_key, noise_key, common_key, gain_key, weight_key = jax.random.split(key, 5)
    whole_shape = (MEMBERS, VARS, NLAT, LON)
    field_shape = (1, VARS, NLAT, LON)
    base = jax.random.normal(base_key, field_shape, jnp.float32)
    noise = jax.random.normal(noise_key, whole_shape, jnp.float32)
    common = jax.random.normal(common_key, field_shape, jnp.float32)
    gains = 0.12 * jnp.exp(jax.random.uniform(gain_key, (MEMBERS, 1, 1, 1), jnp.float32, -1.2, 1.2))
    weights = jax.random.uniform(weight_key, (MEMBERS, 1, 1, 1), jnp.float32, -1.0, 1.0)
    spread = gains * (noise + weights * common)
    return jnp.clip(base + spread, -6.0, 6.0)


def levels(key, extent, shards, low, top_value):
    factor_of, own = 1.0, jax.random.fold_in(key, 6)
    for dim, shards_of in shards:
        draws = jnp.exp(jax.random.uniform(jax.random.fold_in(own, dim), (shards_of,), jnp.float32, low / len(shards), top_value / len(shards)))
        factor_of = factor_of * jnp.repeat(draws, extent[dim] // shards_of).reshape([-1 if axis == dim else 1 for axis in range(len(extent))])
    return factor_of


def bell_draw(key, shape, scale, bound, shards=(), dtype=jnp.bfloat16):
    values = jax.random.normal(key, shape, jnp.float32) * scale
    if len(shards) > 0:
        values = levels(key, shape, shards, -0.22, 0.18) * values
    return jnp.clip(values, min=-bound, max=bound).astype(dtype)


def setup_inputs(seed: int = 0) -> dict:
    arg_keys = jax.random.split(jax.random.key(seed), 7)
    return {
        "members": draw_members(jax.random.fold_in(arg_keys[6], 71), 0),
        "condition": bell_draw(arg_keys[1], (COND, NLAT, LON), 1.0, 6.0, ((1, 32),), jnp.float32),
        "observed": bell_draw(arg_keys[2], (VARS, NLAT, LON), 1.0, 6.0, ((1, 32),), jnp.float32),
        "kernel_in": bell_draw(arg_keys[3], (9, CH, HALF + COND), (9 * (HALF + COND)) ** -0.5, 0.625),
        "kernel_mid": bell_draw(arg_keys[4], (9, CH, CH), (9 * CH) ** -0.5, 0.25),
        "kernel_out": bell_draw(arg_keys[5], (9, VARS, CH), (9 * CH) ** -0.5, 0.25),
    }


EPSILON = 1e-06

def lat_weights(total_rows):
    position = jnp.arange(total_rows).astype(jnp.float32)
    radians = (-90.0 + 180.0 * (position + 0.5) / total_rows) * (jnp.pi / 180.0)
    cosine = jnp.cos(radians)
    return cosine / jnp.mean(cosine)

def silu_slope(pre_act):
    sigmoid = jax.nn.sigmoid(pre_act)
    return sigmoid * (1.0 + pre_act * (1.0 - sigmoid))

def window_at(padded, tap_index, row_count):
    row_step = tap_index // 3
    col_step = tap_index % 3
    return jnp.roll(padded[:, row_step:row_step + row_count, :], 1 - col_step, axis=2)

def convolve(padded, kernel, row_count):
    summed = None
    for tap_index in range(9):
        product = jnp.einsum('oc,crl->orl', kernel[tap_index].astype(jnp.float32), window_at(padded, tap_index, row_count).astype(jnp.float32))
        summed = product if summed is None else summed + product
    return summed

def kernel_grad(grad_field, padded, row_count):
    return jnp.stack([jnp.einsum('orl,crl->oc', grad_field.astype(jnp.float32), window_at(padded, tap_index, row_count).astype(jnp.float32)) for tap_index in range(9)])

def flipped(kernel):
    return jnp.transpose(kernel[::-1], (0, 2, 1))

def pad_rows(field):
    return jnp.pad(field, ((0, 0), (1, 1), (0, 0)))

def forward(member_state, condition, kernel_in, kernel_mid, kernel_out, row_count):
    half_vars = member_state.shape[0] // 2
    inputs = jnp.concatenate([member_state[:half_vars], condition], 0).astype(jnp.bfloat16)
    padded_in = pad_rows(inputs)
    pre_first = convolve(padded_in, kernel_in, row_count)
    hidden_first = jax.nn.silu(pre_first).astype(jnp.bfloat16)
    padded_first = pad_rows(hidden_first)
    pre_second = convolve(padded_first, kernel_mid, row_count)
    hidden_second = jax.nn.silu(pre_second).astype(jnp.bfloat16)
    padded_second = pad_rows(hidden_second)
    coupling = convolve(padded_second, kernel_out, row_count)
    log_scale = jnp.tanh(coupling[:half_vars])
    moved = member_state[half_vars:] * jnp.exp(log_scale) + coupling[half_vars:]
    pushed = jnp.concatenate([member_state[:half_vars], moved], 0)
    saved = (padded_in, pre_first, padded_first, pre_second, padded_second, log_scale)
    return (pushed, saved)

def backward(member_state, grad_pushed, saved, kernel_mid, kernel_out, row_count):
    half_vars = member_state.shape[0] // 2
    padded_in, pre_first, padded_first, pre_second, padded_second, log_scale = saved
    moving = member_state[half_vars:]
    upper_grad = grad_pushed[half_vars:]
    grad_scale = upper_grad * moving * jnp.exp(log_scale) * (1.0 - log_scale * log_scale)
    grad_coupling = jnp.concatenate([grad_scale, upper_grad], 0).astype(jnp.bfloat16)
    grad_last = kernel_grad(grad_coupling, padded_second, row_count)
    back_second = convolve(pad_rows(grad_coupling), flipped(kernel_out), row_count)
    grad_pre_second = (back_second * silu_slope(pre_second)).astype(jnp.bfloat16)
    grad_middle = kernel_grad(grad_pre_second, padded_first, row_count)
    back_first = convolve(pad_rows(grad_pre_second), flipped(kernel_mid), row_count)
    grad_pre_first = (back_first * silu_slope(pre_first)).astype(jnp.bfloat16)
    grad_first = kernel_grad(grad_pre_first, padded_in, row_count)
    return (grad_first, grad_middle, grad_last)

def reference(members, condition, observed, kernel_in, kernel_mid, kernel_out):
    member_count = members.shape[0]
    row_count = members.shape[2]
    entries = members.shape[1] * row_count * members.shape[3]
    lat = lat_weights(row_count)[None, :, None]
    fields = []
    for member_index in range(member_count):
        pushed_one, unused = forward(members[member_index], condition, kernel_in, kernel_mid, kernel_out, row_count)
        fields.append(pushed_one)
    to_obs = [jnp.sqrt(jnp.sum(lat * (fields[mm] - observed) ** 2) / entries + EPSILON) for mm in range(member_count)]
    between = {}
    for first_index in range(member_count):
        for second_index in range(first_index + 1, member_count):
            value = jnp.sqrt(jnp.sum(lat * (fields[first_index] - fields[second_index]) ** 2) / entries + EPSILON)
            between[first_index, second_index] = value
            between[second_index, first_index] = value
    energy = sum(to_obs) / member_count
    energy = energy - sum(between.values()) / (2.0 * member_count * member_count)
    grad_first = jnp.zeros(kernel_in.shape, jnp.float32)
    grad_middle = jnp.zeros(kernel_mid.shape, jnp.float32)
    grad_last = jnp.zeros(kernel_out.shape, jnp.float32)
    root = math.sqrt(entries)
    for member_index in range(member_count):
        pushed_one, saved = forward(members[member_index], condition, kernel_in, kernel_mid, kernel_out, row_count)
        inner = (pushed_one - observed) / (member_count * to_obs[member_index])
        for other_index in range(member_count):
            if other_index != member_index:
                inner = inner - (pushed_one - fields[other_index]) / (member_count * member_count * between[member_index, other_index])
        grad_pushed = lat * inner / root
        parts = backward(members[member_index], grad_pushed, saved, kernel_mid, kernel_out, row_count)
        grad_first = grad_first + parts[0]
        grad_middle = grad_middle + parts[1]
        grad_last = grad_last + parts[2]
    return (jnp.stack(fields), energy, grad_first, grad_middle, grad_last)
```

```python
import math

import jax
import jax.numpy as jnp
from jax import lax
from jax.sharding import Mesh, PartitionSpec as P

EPSILON = 1e-06


HALO = 5
LANES = 128
CHUNK_ROWS = 24
TILE = ("ring", "core")


def spread(value, axes, count):
    copies = jnp.broadcast_to(value[None], (count,) + value.shape)
    return lax.all_to_all(copies, axes, 0, 0)


def lat_weights(total_rows):
    position = jnp.arange(total_rows).astype(jnp.float32)
    radians = (-90.0 + 180.0 * (position + 0.5) / total_rows) * (jnp.pi / 180.0)
    cosine = jnp.cos(radians)
    return cosine / jnp.mean(cosine)


def silu_slope(pre_act):
    sigmoid = jax.nn.sigmoid(pre_act)
    return sigmoid * (1.0 + pre_act * (1.0 - sigmoid))


def window_at(padded, tap_index, row_count):
    row_step = tap_index // 3
    col_step = tap_index % 3
    return jnp.roll(padded[:, row_step : row_step + row_count, :], 1 - col_step, axis=2)


def convolve(padded, kernel, row_count):
    summed = None
    for tap_index in range(9):
        product = jnp.einsum(
            "oc,crl->orl",
            kernel[tap_index],
            window_at(padded, tap_index, row_count),
            preferred_element_type=jnp.float32,
        )
        summed = product if summed is None else summed + product
    return summed


def kernel_grad(grad_field, padded, row_count):
    return jnp.stack(
        [
            jnp.einsum(
                "orl,crl->oc",
                grad_field,
                window_at(padded, tap_index, row_count),
                preferred_element_type=jnp.float32,
            )
            for tap_index in range(9)
        ]
    )


def flipped(kernel):
    return jnp.transpose(kernel[::-1], (0, 2, 1))


def pack(fields):
    return jnp.concatenate([field.reshape(-1, field.shape[-1]) for field in fields], 0)


def unpack(packed, shapes):
    fields, start = [], 0
    for channels, rows in shapes:
        part = packed[start : start + channels * rows]
        fields.append(part.reshape(channels, rows, packed.shape[-1]))
        start += channels * rows
    return fields


def widened(fields, tile_count):
    up = [(i, i + 1) for i in range(tile_count - 1)]
    down = [(i + 1, i) for i in range(tile_count - 1)]
    last = pack([field[:, field.shape[1] - width :] for field, width in fields])
    initial = pack([field[:, :width] for field, width in fields])
    shapes = [(field.shape[0], width) for field, width in fields]
    before = unpack(lax.ppermute(last, TILE, up), shapes)
    after = unpack(lax.ppermute(initial, TILE, down), shapes)
    return [
        jnp.concatenate([first, field, second], 1)
        for first, (field, _), second in zip(before, fields, after)
    ]


def total_over_all(flat, member_count, ring_count):
    size = 2 * member_count * CHUNK_ROWS * LANES
    blocks = jnp.pad(flat, (0, size - flat.shape[0]))
    blocks = blocks.reshape(2, member_count, CHUNK_ROWS, LANES)
    core = lax.axis_index("core")
    swap = [(0, 1), (1, 0)]
    mine = jnp.where(core == 0, blocks[0], blocks[1])
    theirs = jnp.where(core == 0, blocks[1], blocks[0])
    mine = mine + lax.ppermute(theirs, "core", swap)
    chunk = jnp.sum(lax.all_to_all(mine, "member", 0, 0), 0)
    chunk = jnp.sum(spread(chunk, "ring", ring_count), 0)
    half = spread(chunk, "member", member_count)
    other = lax.ppermute(half, "core", swap)
    first = jnp.where(core == 0, half, other)
    second = jnp.where(core == 0, other, half)
    return jnp.concatenate([first.reshape(-1), second.reshape(-1)])[: flat.shape[0]]


def per_device(members, condition, observed, kernel_in, kernel_mid, kernel_out):
    member_state = members[0]
    row_count = member_state.shape[1]
    half_vars = member_state.shape[0] // 2
    member_count = lax.axis_size("member")
    ring_count = lax.axis_size("ring")
    tile_count = ring_count * lax.axis_size("core")
    total_rows = row_count * tile_count
    entries = member_state.shape[0] * total_rows * member_state.shape[2]
    base_row = lax.axis_index(TILE) * row_count
    fixed, moving = member_state[:half_vars], member_state[half_vars:]

    def inside(extra):
        rows = base_row - extra + jnp.arange(row_count + 2 * extra)
        return ((rows >= 0) & (rows < total_rows))[None, :, None]

    lat_all = jnp.pad(lat_weights(total_rows), (2, 2))
    lat_wide = lax.dynamic_slice_in_dim(lat_all, base_row, row_count + 4, 0)[None, :, None]
    lat = lat_wide[:, 2:-2]
    fixed_wide, condition_wide, moving_wide, observed_wide = widened(
        [(fixed, HALO), (condition, HALO), (moving, 2), (observed[half_vars:], 2)], tile_count
    )
    inputs = jnp.concatenate([fixed_wide, condition_wide], 0).astype(jnp.bfloat16)
    pre_first = convolve(inputs, kernel_in, row_count + 8)
    hidden_first = jnp.where(inside(4), jax.nn.silu(pre_first), 0.0).astype(jnp.bfloat16)
    pre_second = convolve(hidden_first, kernel_mid, row_count + 6)
    hidden_second = jnp.where(inside(3), jax.nn.silu(pre_second), 0.0).astype(jnp.bfloat16)
    coupling = convolve(hidden_second, kernel_out, row_count + 4)
    log_scale = jnp.tanh(coupling[:half_vars])
    scale = jnp.exp(log_scale)
    moved = moving_wide * scale + coupling[half_vars:]
    pushed = jnp.concatenate([fixed, moved[:, 2:-2]], 0)
    everyone = spread(pack([moved, fixed]), "member", member_count)
    split = half_vars * (row_count + 4)
    lon = member_state.shape[2]
    moved_all = everyone[:, :split].reshape(member_count, half_vars, row_count + 4, lon)
    fixed_all = everyone[:, split:].reshape(member_count, half_vars, row_count, lon)
    from_moved = jnp.sum(lat * (moved[None, :, 2:-2] - moved_all[:, :, 2:-2]) ** 2, (1, 2, 3))
    from_fixed = jnp.sum(lat * (fixed[None] - fixed_all) ** 2, (1, 2, 3))
    to_observed = jnp.sum(lat * (pushed - observed) ** 2)
    partials = jnp.concatenate([from_moved + from_fixed, to_observed[None]])
    partials = jnp.pad(partials[None], ((0, 7), (0, LANES - partials.shape[0])))
    totals = jnp.sum(spread(partials, TILE, tile_count), 0)[0]
    distances = jnp.sqrt(totals / entries + EPSILON)
    to_others = distances[:member_count]
    is_other = jnp.arange(member_count) != lax.axis_index("member")
    energy_share = distances[member_count] / member_count
    energy_share = energy_share - jnp.sum(jnp.where(is_other, to_others, 0.0)) / (
        2.0 * member_count * member_count
    )
    weights = jnp.where(is_other, 1.0 / (member_count * member_count * to_others), 0.0)
    inner = (moved - observed_wide) / (member_count * distances[member_count])
    inner = inner - jnp.sum(weights[:, None, None, None] * (moved[None] - moved_all), 0)
    upper_grad = lat_wide * inner / math.sqrt(entries)
    grad_scale = upper_grad * moving_wide * scale * (1.0 - log_scale * log_scale)
    grad_coupling = jnp.concatenate([grad_scale, upper_grad], 0).astype(jnp.bfloat16)
    grad_last = kernel_grad(grad_coupling[:, 2:-2], hidden_second[:, 2:-2], row_count)
    back_second = convolve(grad_coupling, flipped(kernel_out), row_count + 2)
    grad_pre_second = back_second * silu_slope(pre_second[:, 2:-2])
    grad_pre_second = jnp.where(inside(1), grad_pre_second, 0.0).astype(jnp.bfloat16)
    grad_middle = kernel_grad(grad_pre_second[:, 1:-1], hidden_first[:, 3:-3], row_count)
    back_first = convolve(grad_pre_second, flipped(kernel_mid), row_count)
    grad_pre_first = (back_first * silu_slope(pre_first[:, 4:-4])).astype(jnp.bfloat16)
    grad_first = kernel_grad(grad_pre_first, inputs[:, 4:-4], row_count)
    parts = [grad_first, grad_middle, grad_last, energy_share[None] / tile_count]
    summed = total_over_all(
        jnp.concatenate([part.reshape(-1) for part in parts]), member_count, ring_count
    )
    results, start = [], 0
    for part in parts:
        results.append(summed[start : start + part.size].reshape(part.shape))
        start += part.size
    grad_first, grad_middle, grad_last, energy = results
    return (pushed[None], energy[0], grad_first, grad_middle, grad_last)


def solution(mesh):
    sizes = (mesh.shape["member"], mesh.shape["tile"] // 2, 2)
    fine = Mesh(mesh.devices.reshape(sizes), ("member",) + TILE)
    in_specs = (
        P("member", None, TILE, None),
        P(None, TILE, None),
        P(None, TILE, None),
        P(),
        P(),
        P(),
    )
    out_specs = (P("member", None, TILE, None), P(), P(), P(), P())
    return jax.shard_map(
        per_device, mesh=fine, in_specs=in_specs, out_specs=out_specs, check_vma=False
    )
```

```python
import functools
import math

import jax
import jax.numpy as jnp
import numpy as np
from jax import lax
from jax.experimental import pallas as pl
from jax.experimental.pallas import tpu as pltpu
from jax.sharding import Mesh, PartitionSpec as P

EPSILON = 1e-06
MEMBERS, NLAT, LON, ROWS = 8, 256, 512, 8
VARS, HALF, COND, CH = 6, 3, 6, 64
TILES, RING = 32, 16
ENTRIES = VARS * NLAT * LON
HALO = 5
FIELDS = 16
INPUTS = HALF + COND
WIDE = (ROWS + 4) * HALF
FIXED_AT = 40
CHUNK = 24
TILE = ("ring", "core")
F32, BF16 = jnp.float32, jnp.bfloat16


def spread(value, axes, count):
    copies = jnp.broadcast_to(value[None], (count,) + value.shape)
    return lax.all_to_all(copies, axes, 0, 0)


def lat_table():
    rows = np.arange(NLAT)
    cosine = np.cos((-90.0 + 180.0 * (rows + 0.5) / NLAT) * (np.pi / 180.0))
    lat = (cosine / cosine.mean()).astype(np.float32)
    padded = np.pad(lat, (2, 2))
    table = np.zeros((TILES, FIXED_AT + ROWS), np.float32)
    for tile in range(TILES):
        wide = padded[tile * ROWS : tile * ROWS + ROWS + 4]
        table[tile, :WIDE] = np.repeat(wide, HALF)
        table[tile, FIXED_AT:] = lat[tile * ROWS : (tile + 1) * ROWS]
    return table


def turned(value, step):
    return value if step == 0 else pltpu.roll(value, step % LON, 1)


def dot(left, right):
    return jnp.dot(left, right, preferred_element_type=F32)


def dot_cells(left, right):
    return lax.dot_general(left, right, (((1,), (1,)), ((), ())), preferred_element_type=F32)


def inside(base, row):
    row = base + row
    return jnp.where((row >= 0) & (row < NLAT), 1.0, 0.0).astype(F32)


def sigmoid(value):
    return 0.5 * jnp.tanh(0.5 * value) + 0.5


def loop(start, stop, body):
    lax.fori_loop(start, stop, lambda row, carry: (body(row), carry)[1], 0, unroll=2)


def forward_kernel(
    place, before, own, after, members, w_in, w_mid, w_out,
    send, pushed, kept, stack, hidden_1, slope_1, hidden_2, slope_2,
):
    base = place[1]
    for row in range(ROWS + 2 * HALO):
        if row < HALO:
            field = before[row]
        elif row < HALO + ROWS:
            field = own[row - HALO]
        else:
            field = after[row - HALO - ROWS]
        for shift in range(3):
            part = turned(field, 1 - shift).astype(BF16)
            stack[row, shift * FIELDS : (shift + 1) * FIELDS, :] = part

    def first(row, keep):
        pre = dot(w_in[...], stack[pl.ds(row, 3)].reshape(9 * FIELDS, LON))
        gate = sigmoid(pre)
        hidden_1[row] = (pre * gate * inside(base, row - 4)).astype(BF16)
        if keep:
            slope_1[row - 4] = gate * (1.0 + pre * (1.0 - gate))

    loop(0, 4, functools.partial(first, keep=False))
    loop(4, 12, functools.partial(first, keep=True))
    loop(12, 16, functools.partial(first, keep=False))

    def second(row, keep):
        part = dot(w_mid[...], hidden_1[pl.ds(row, 3)].reshape(3 * CH, LON))
        pre = turned(part[:CH], 1) + part[CH : 2 * CH] + turned(part[2 * CH :], -1)
        gate = sigmoid(pre)
        hidden_2[row] = (pre * gate * inside(base, row - 3)).astype(BF16)
        if keep:
            slope_2[row - 2] = gate * (1.0 + pre * (1.0 - gate))

    loop(0, 2, functools.partial(second, keep=False))
    loop(2, 12, functools.partial(second, keep=True))
    loop(12, 14, functools.partial(second, keep=False))

    for row in range(ROWS + 4):
        part = dot(w_out[...], hidden_2[row : row + 3].reshape(3 * CH, LON))
        both = turned(part[:16], 1) + part[16:32] + turned(part[32:], -1)
        log_scale = jnp.tanh(both[:HALF])
        if row < 2:
            field = before[row + 3]
        elif row < 2 + ROWS:
            field = own[row - 2]
        else:
            field = after[row - 2 - ROWS]
        moving = field[INPUTS : INPUTS + HALF]
        moved = moving * jnp.exp(log_scale) + both[8 : 8 + HALF]
        here = slice(row * HALF, (row + 1) * HALF)
        kept[0, here, :] = log_scale
        kept[1, here, :] = moving
        kept[2, here, :] = field[INPUTS + HALF : INPUTS + 2 * HALF]
        send[0, here, :] = moved
        if 2 <= row < 2 + ROWS:
            for var in range(HALF):
                pushed[HALF + var, row - 2 : row - 1, :] = moved[var : var + 1]
    pushed[:HALF] = members[:HALF]
    send[0, WIDE:FIXED_AT, :] = jnp.zeros((FIXED_AT - WIDE, LON), F32)
    send[0, FIXED_AT:, :] = members[:HALF].reshape(HALF * ROWS, LON)
    whole = send[0]
    for copy in range(1, MEMBERS):
        send[copy] = whole


def folded(value):
    return sum(value[..., at : at + 128] for at in range(0, LON, 128))


def distance_kernel(place, lat, fields, kept, observed, partials):
    me = place[0]
    spot = lax.broadcasted_iota(jnp.int32, (WIDE, 1), 0)
    wide = jnp.where((spot >= 2 * HALF) & (spot < WIDE - 2 * HALF), lat[:WIDE, :1], 0.0)
    low = jnp.concatenate([lat[FIXED_AT:, :1]] * HALF, 0)
    mine = fields[me]

    def weighed(moved, fixed):
        upper = jnp.sum(folded(wide * (mine[:WIDE] - moved) ** 2), 0, keepdims=True)
        lower = jnp.sum(folded(low * (mine[FIXED_AT:] - fixed) ** 2), 0, keepdims=True)
        return upper + lower

    rows = [weighed(fields[n, :WIDE], fields[n, FIXED_AT:]) for n in range(MEMBERS)]
    to_observed = weighed(kept[2], observed[:HALF].reshape(HALF * ROWS, LON))
    all_rows = jnp.concatenate(rows, 0)
    spot = lax.broadcasted_iota(jnp.int32, (MEMBERS, 128), 0)
    all_rows = jnp.where(spot == me, to_observed, all_rows)
    for tile in range(TILES):
        partials[tile] = all_rows


def backward_kernel(
    place, lat, totals, fields, kept, stack, hidden_1, slope_1, hidden_2, slope_2, w_back_2, w_back_1,
    mine, theirs, coupled, turned_2, sum_out, sum_mid, sum_in, packed,
):
    me, base, core = place[0], place[1], place[2]
    total = totals[0]
    for tile in range(1, TILES):
        total = total + totals[tile]
    distances = jnp.sqrt(jnp.sum(total, 1, keepdims=True) / ENTRIES + EPSILON)
    is_me = lax.broadcasted_iota(jnp.int32, (MEMBERS, 1), 0) == me
    shares = jnp.where(is_me, distances / MEMBERS, -distances / (2.0 * MEMBERS * MEMBERS))
    share = jnp.sum(shares, 0, keepdims=True) / TILES
    weights = 1.0 / (jnp.where(is_me, MEMBERS, MEMBERS * MEMBERS) * distances)
    own_weight = jnp.sum(jnp.where(is_me, weights, 0.0), 0, keepdims=True)
    weights = jnp.where(is_me, 0.0, weights)
    log_scale, moving, observed = kept[0], kept[1], kept[2]
    moved = fields[me, :WIDE]
    inner = (moved - observed) * own_weight
    for n in range(MEMBERS):
        inner = inner - weights[n : n + 1] * (moved - fields[n, :WIDE])
    upper = lat[:WIDE, :1] * inner / math.sqrt(ENTRIES)
    scaled = upper * moving * jnp.exp(log_scale) * (1.0 - log_scale * log_scale)
    blank = jnp.zeros((8 - HALF, LON), F32)
    for row in range(ROWS + 4):
        here = slice(row * HALF, (row + 1) * HALF)
        field = jnp.concatenate([scaled[here], blank, upper[here], blank], 0)
        for shift in range(3):
            part = turned(field, shift - 1).astype(BF16)
            coupled[row, shift * 16 : (shift + 1) * 16, :] = part

    def second(row):
        back = dot(w_back_2[...], coupled[pl.ds(row, 3)].reshape(144, LON))
        grad = back * slope_2[row] * inside(base, row - 1)
        for shift in range(3):
            part = turned(grad, shift - 1).astype(BF16)
            turned_2[row, shift * CH : (shift + 1) * CH, :] = part

    loop(0, ROWS + 2, second)
    sum_out[...] = jnp.zeros_like(sum_out)
    sum_mid[...] = jnp.zeros_like(sum_mid)
    sum_in[...] = jnp.zeros_like(sum_in)

    def last(row):
        near_2 = hidden_2[pl.ds(row + 2, 3)].reshape(3 * CH, LON)
        sum_out[...] += dot_cells(coupled[row + 2], near_2)
        near_1 = hidden_1[pl.ds(row + 3, 3)].reshape(3 * CH, LON)
        sum_mid[...] += dot_cells(turned_2[row + 1], near_1)
        back = dot(w_back_1[...], turned_2[pl.ds(row, 3)].reshape(9 * CH, LON))
        grad = (back * slope_1[row]).astype(BF16)
        near_0 = stack[pl.ds(row + 4, 3)].reshape(9 * FIELDS, LON)
        sum_in[...] += dot_cells(grad, near_0)

    loop(0, ROWS, last)
    packed[4 * CH :, :] = jnp.zeros((2 * CH, 128), F32)
    for tap in range(9):
        a, b = tap // 3, tap % 3
        at = (tap // 2) * CH
        side = slice((tap % 2) * CH, (tap % 2 + 1) * CH)
        packed[at : at + CH, side] = sum_mid[b * CH : (b + 1) * CH, a * CH : (a + 1) * CH]
        at = 4 * CH + tap * VARS
        across = slice(a * CH, (a + 1) * CH)
        packed[at : at + HALF, CH:] = sum_out[b * 16 : b * 16 + HALF, across]
        packed[at + HALF : at + VARS, CH:] = sum_out[b * 16 + 8 : b * 16 + 8 + HALF, across]
        across = slice(tap * INPUTS, (tap + 1) * INPUTS)
        packed[5 * CH :, across] = sum_in[:, tap * FIELDS : tap * FIELDS + INPUTS]
    packed[5 * CH : 5 * CH + 1, 96:97] = share
    half = MEMBERS * CHUNK
    for copy in range(2):

        @pl.when(core == copy)
        def _():
            mine[...] = packed[copy * half : (copy + 1) * half, :]
            theirs[...] = packed[(1 - copy) * half : (2 - copy) * half, :]


def unpack_kernel(place, mine, theirs, grad_in, grad_mid, grad_out, energy, packed):
    half = MEMBERS * CHUNK
    for copy in range(2):

        @pl.when(place[2] == copy)
        def _():
            packed[copy * half : (copy + 1) * half, :] = mine[...]
            packed[(1 - copy) * half : (2 - copy) * half, :] = theirs[...]

    for tap in range(9):
        at = (tap // 2) * CH
        grad_mid[tap] = packed[at : at + CH, (tap % 2) * CH : (tap % 2 + 1) * CH]
        at = 4 * CH + tap * VARS
        grad_out[tap] = packed[at : at + VARS, CH:]
        grad_in[tap] = packed[5 * CH :, tap * INPUTS : (tap + 1) * INPUTS]
    energy[...] = packed[5 * CH : 5 * CH + 1, 96:97]


def call(kernel, outs, scratch=(), flops=10**6):
    vmem = pl.BlockSpec(memory_space=pltpu.VMEM)

    def run(place, *arrays):
        return pl.pallas_call(
            kernel,
            out_shape=[jax.ShapeDtypeStruct(shape, dtype) for shape, dtype in outs],
            in_specs=[pl.BlockSpec(memory_space=pltpu.SMEM)] + [vmem] * len(arrays),
            out_specs=[vmem] * len(outs),
            scratch_shapes=[pltpu.VMEM(shape, dtype) for shape, dtype in scratch],
            compiler_params=pltpu.CompilerParams(vmem_limit_bytes=VMEM_LIMIT),
            cost_estimate=pl.CostEstimate(flops=flops, bytes_accessed=10**6, transcendentals=0),
        )(place, *arrays)

    return run


VMEM_LIMIT = 32 * 2**20


def padded_to(array, axis, size):
    pads = [(0, 0)] * array.ndim
    pads[axis] = (0, size - array.shape[axis])
    return jnp.pad(array, pads)


def weights_of(kernel_in, kernel_mid, kernel_out):
    taps_in = padded_to(kernel_in, 2, FIELDS).reshape(3, 3, CH, FIELDS)
    w_in = taps_in.transpose(2, 0, 1, 3).reshape(CH, 9 * FIELDS)
    taps_mid = kernel_mid.reshape(3, 3, CH, CH)
    w_mid = taps_mid.transpose(1, 2, 0, 3).reshape(3 * CH, 3 * CH)
    w_back_1 = taps_mid[::-1].transpose(3, 0, 1, 2).reshape(CH, 9 * CH)
    taps_out = padded_to(kernel_out.reshape(3, 3, 2, HALF, CH), 3, 8).reshape(3, 3, 16, CH)
    w_out = taps_out.transpose(1, 2, 0, 3).reshape(48, 3 * CH)
    w_back_2 = taps_out[::-1].transpose(3, 0, 1, 2).reshape(CH, 144)
    return w_in, w_mid, w_out, w_back_2, w_back_1


def per_device(members, condition, observed, kernel_in, kernel_mid, kernel_out):
    members = members[0]
    core = lax.axis_index("core")
    tile = lax.axis_index(TILE)
    place = jnp.stack([lax.axis_index("member"), tile * ROWS, core]).astype(jnp.int32)
    table = jnp.asarray(lat_table())
    lat = lax.dynamic_slice_in_dim(table, tile, 1, 0)[0]
    lat = jnp.broadcast_to(lat[:, None], (FIXED_AT + ROWS, 128))
    blank = jnp.zeros((1, ROWS, LON), F32)
    own = jnp.concatenate([members[:HALF], condition, members[HALF:], observed[HALF:], blank], 0)
    own = own.transpose(1, 0, 2)
    up = [(i, i + 1) for i in range(TILES - 1)]
    down = [(i + 1, i) for i in range(TILES - 1)]
    before = lax.ppermute(own[ROWS - HALO :], TILE, up)
    after = lax.ppermute(own[:HALO], TILE, down)
    w_in, w_mid, w_out, w_back_2, w_back_1 = weights_of(kernel_in, kernel_mid, kernel_out)
    send, pushed, kept, stack, hidden_1, slope_1, hidden_2, slope_2 = call(
        forward_kernel,
        [
            ((MEMBERS, FIXED_AT + HALF * ROWS, LON), F32),
            ((VARS, ROWS, LON), F32),
            ((3, WIDE, LON), F32),
            ((ROWS + 10, 3 * FIELDS, LON), BF16),
            ((ROWS + 8, CH, LON), BF16),
            ((ROWS, CH, LON), F32),
            ((ROWS + 6, CH, LON), BF16),
            ((ROWS + 2, CH, LON), F32),
        ],
        flops=10**9,
    )(place, before, own, after, members, w_in, w_mid, w_out)
    fields = lax.all_to_all(send, "member", 0, 0)
    (partials,) = call(distance_kernel, [((TILES, MEMBERS, 128), F32)])(
        place, lat, fields, kept, observed
    )
    totals = lax.all_to_all(partials, TILE, 0, 0)
    mine, theirs = call(
        backward_kernel,
        [((MEMBERS * CHUNK, 128), F32)] * 2,
        [
            ((ROWS + 4, 48, LON), BF16),
            ((ROWS + 2, 3 * CH, LON), BF16),
            ((48, 3 * CH), F32),
            ((3 * CH, 3 * CH), F32),
            ((CH, 9 * FIELDS), F32),
            ((6 * CH, 128), F32),
        ],
        flops=10**9,
    )(
        place, lat, totals, fields, kept, stack, hidden_1, slope_1, hidden_2, slope_2,
        w_back_2, w_back_1,
    )
    swap = [(0, 1), (1, 0)]
    mine = mine + lax.ppermute(theirs, "core", swap)
    chunk = jnp.sum(lax.all_to_all(mine.reshape(MEMBERS, CHUNK, 128), "member", 0, 0), 0)
    chunk = jnp.sum(spread(chunk, "ring", RING), 0)
    half = spread(chunk, "member", MEMBERS).reshape(MEMBERS * CHUNK, 128)
    other = lax.ppermute(half, "core", swap)
    grad_in, grad_mid, grad_out, energy = call(
        unpack_kernel,
        [((9, CH, INPUTS), F32), ((9, CH, CH), F32), ((9, VARS, CH), F32), ((1, 1), F32)],
        [((6 * CH, 128), F32)],
    )(place, half, other)
    return (pushed[None], energy[0, 0], grad_in, grad_mid, grad_out)


def solution(mesh):
    fine = Mesh(mesh.devices.reshape(MEMBERS, -1, 2), ("member",) + TILE)
    in_specs = (
        P("member", None, TILE, None),
        P(None, TILE, None),
        P(None, TILE, None),
        P(),
        P(),
        P(),
    )
    out_specs = (P("member", None, TILE, None), P(), P(), P(), P())
    return jax.shard_map(
        per_device, mesh=fine, in_specs=in_specs, out_specs=out_specs, check_vma=False
    )
```

```python
import functools
import math

import jax
import jax.numpy as jnp
import numpy as np
from jax import lax
from jax.experimental import pallas as pl
from jax.experimental.pallas import tpu as pltpu
from jax.sharding import Mesh, PartitionSpec as P

EPSILON = 1e-06
MEMBERS, NLAT, LON, ROWS = 8, 256, 512, 8
VARS, HALF, COND, CH = 6, 3, 6, 64
TILES, RING = 32, 16
ENTRIES = VARS * NLAT * LON
HALO = 5
FIELDS = 16
INPUTS = HALF + COND
WIDE = (ROWS + 4) * HALF
FIXED_AT = 40
CHUNK = 24
TILE = ("ring", "core")
F32, BF16 = jnp.float32, jnp.bfloat16


def spread(value, axes, count):
    copies = jnp.broadcast_to(value[None], (count,) + value.shape)
    return lax.all_to_all(copies, axes, 0, 0)


def lat_table():
    rows = np.arange(NLAT)
    cosine = np.cos((-90.0 + 180.0 * (rows + 0.5) / NLAT) * (np.pi / 180.0))
    lat = (cosine / cosine.mean()).astype(np.float32)
    padded = np.pad(lat, (2, 2))
    table = np.zeros((TILES, FIXED_AT + ROWS), np.float32)
    for tile in range(TILES):
        wide = padded[tile * ROWS : tile * ROWS + ROWS + 4]
        table[tile, :WIDE] = np.repeat(wide, HALF)
        table[tile, FIXED_AT:] = lat[tile * ROWS : (tile + 1) * ROWS]
    return table


def turned(value, step):
    return value if step == 0 else pltpu.roll(value, step % LON, 1)


def dot(left, right):
    return jnp.dot(left, right, preferred_element_type=F32)


def dot_cells(left, right):
    return lax.dot_general(left, right, (((1,), (1,)), ((), ())), preferred_element_type=F32)


def inside(base, row):
    row = base + row
    return jnp.where((row >= 0) & (row < NLAT), 1.0, 0.0).astype(F32)


def sigmoid(value):
    return 0.5 * jnp.tanh(0.5 * value) + 0.5


def loop(start, stop, body):
    lax.fori_loop(start, stop, lambda row, carry: (body(row), carry)[1], 0, unroll=2)


def pack_kernel(place, members, condition, observed, own, edge_far, edge_near):
    for row in range(ROWS):
        own[row, :HALF, :] = members[:HALF, row, :]
        own[row, HALF:INPUTS, :] = condition[:, row, :]
        own[row, INPUTS : INPUTS + HALF, :] = members[HALF:, row, :]
        own[row, INPUTS + HALF : INPUTS + 2 * HALF, :] = observed[HALF:, row, :]
        own[row, FIELDS - 1 :, :] = jnp.zeros((1, LON), F32)
    odd = place[2] == 1
    for row in range(HALO):
        initial, last = own[row], own[ROWS - HALO + row]
        edge_far[row] = jnp.where(odd, last, initial)
        edge_near[row] = jnp.where(odd, initial, last)


def weights_kernel(
    place, kernel_in, kernel_mid, kernel_out, w_in, w_mid, w_out, w_back_2, w_back_1,
    flat_in, square, flat_out, back_2, back_1, held_2, held_1, sems,
):
    flat_in[...] = jnp.zeros_like(flat_in)
    flat_out[...] = jnp.zeros_like(flat_out)
    back_2[...] = jnp.zeros_like(back_2)
    for tap in range(9):
        a, b = tap // 3, tap % 3
        back = 3 * (2 - a) + b
        flat_in[:, tap * FIELDS : tap * FIELDS + INPUTS] = kernel_in[tap].astype(F32)
        mid = kernel_mid[tap].astype(F32)
        square[b * CH : (b + 1) * CH, a * CH : (a + 1) * CH] = mid
        back_1[:, back * CH : (back + 1) * CH] = mid.T
        out = kernel_out[tap].astype(F32)
        across = slice(a * CH, (a + 1) * CH)
        flat_out[b * 16 : b * 16 + HALF, across] = out[:HALF]
        flat_out[b * 16 + 8 : b * 16 + 8 + HALF, across] = out[HALF:]
        out = jnp.concatenate([out, jnp.zeros((8 - VARS, CH), F32)], 0).T
        back_2[:, back * 16 : back * 16 + HALF] = out[:, :HALF]
        back_2[:, back * 16 + 8 : back * 16 + 8 + HALF] = out[:, HALF:VARS]
    held_2[...] = back_2[...].astype(BF16)
    held_1[...] = back_1[...].astype(BF16)
    copies = [
        pltpu.make_async_copy(held_2, w_back_2, sems.at[0]),
        pltpu.make_async_copy(held_1, w_back_1, sems.at[1]),
    ]
    for copy in copies:
        copy.start()
    w_in[...] = flat_in[...].astype(BF16)
    w_mid[...] = square[...].astype(BF16)
    w_out[...] = flat_out[...].astype(BF16)
    for copy in copies:
        copy.wait()


def forward_kernel(
    place, far, near, own, members, w_in, w_mid, w_out,
    send_out, pushed, kept_out, stack_out, hidden_1_out, slope_1_out, hidden_2_out, slope_2_out,
    send, kept, stack, hidden_1, slope_1, hidden_2, slope_2, edges, sems,
):
    base = place[1]
    odd = place[2] == 1
    copies = []

    def keep(source, target):
        copy = pltpu.make_async_copy(source, target, sems.at[len(copies)])
        copy.start()
        copies.append(copy)

    for row in range(HALO):
        edges[row] = jnp.where(odd, near[row], far[row])
        edges[HALO + row] = jnp.where(odd, far[row], near[row])

    def wide(row):
        if row < HALO:
            return edges[row]
        return own[row - HALO] if row < HALO + ROWS else edges[row - ROWS]

    for row in range(ROWS + 2 * HALO):
        field = wide(row)
        for shift in range(3):
            part = turned(field, 1 - shift).astype(BF16)
            stack[row, shift * FIELDS : (shift + 1) * FIELDS, :] = part
    keep(stack, stack_out)

    def first(row, kept_row):
        pre = dot(w_in[...], stack[pl.ds(row, 3)].reshape(9 * FIELDS, LON))
        gate = sigmoid(pre)
        hidden_1[row] = (pre * gate * inside(base, row - 4)).astype(BF16)
        if kept_row:
            slope_1[row - 4] = gate * (1.0 + pre * (1.0 - gate))

    loop(0, 4, functools.partial(first, kept_row=False))
    loop(4, 12, functools.partial(first, kept_row=True))
    loop(12, 16, functools.partial(first, kept_row=False))
    keep(hidden_1, hidden_1_out)
    keep(slope_1, slope_1_out)

    def second(row, kept_row):
        part = dot(w_mid[...], hidden_1[pl.ds(row, 3)].reshape(3 * CH, LON))
        pre = turned(part[:CH], 1) + part[CH : 2 * CH] + turned(part[2 * CH :], -1)
        gate = sigmoid(pre)
        hidden_2[row] = (pre * gate * inside(base, row - 3)).astype(BF16)
        if kept_row:
            slope_2[row - 2] = gate * (1.0 + pre * (1.0 - gate))

    loop(0, 2, functools.partial(second, kept_row=False))
    loop(2, 12, functools.partial(second, kept_row=True))
    loop(12, 14, functools.partial(second, kept_row=False))
    keep(hidden_2, hidden_2_out)
    keep(slope_2, slope_2_out)

    send[WIDE:FIXED_AT, :] = jnp.zeros((FIXED_AT - WIDE, LON), F32)
    send[FIXED_AT:, :] = members[:HALF].reshape(HALF * ROWS, LON)
    for row in range(ROWS + 4):
        part = dot(w_out[...], hidden_2[row : row + 3].reshape(3 * CH, LON))
        both = turned(part[:16], 1) + part[16:32] + turned(part[32:], -1)
        log_scale = jnp.tanh(both[:HALF])
        field = wide(row + 3)
        moving = field[INPUTS : INPUTS + HALF]
        moved = moving * jnp.exp(log_scale) + both[8 : 8 + HALF]
        here = slice(row * HALF, (row + 1) * HALF)
        kept[0, here, :] = log_scale
        kept[1, here, :] = moving
        kept[2, here, :] = field[INPUTS + HALF : INPUTS + 2 * HALF]
        kept[3, here, :] = moved
        send[here, :] = moved
        if 2 <= row < 2 + ROWS:
            for var in range(HALF):
                pushed[HALF + var, row - 2 : row - 1, :] = moved[var : var + 1]
    for member in range(MEMBERS):
        keep(send, send_out.at[member])
    keep(kept, kept_out)
    pushed[:HALF] = members[:HALF]
    for copy in copies:
        copy.wait()


def folded(value):
    return sum(value[..., at : at + 128] for at in range(0, LON, 128))


def distance_kernel(
    place, lat, members, observed, fields_in, kept_in, partials_out, fields, kept, partials, sems
):
    copies = [pltpu.make_async_copy(kept_in.at[2:4], kept, sems.at[MEMBERS])]
    for n in range(MEMBERS):
        copies.append(pltpu.make_async_copy(fields_in.at[n], fields.at[n], sems.at[n]))
    for copy in copies:
        copy.start()
    me = place[0]
    spot = lax.broadcasted_iota(jnp.int32, (WIDE, 1), 0)
    wide = jnp.where((spot >= 2 * HALF) & (spot < WIDE - 2 * HALF), lat[:WIDE, :1], 0.0)
    low = jnp.concatenate([lat[FIXED_AT:, :1]] * HALF, 0)
    fixed_mine = members[:HALF].reshape(HALF * ROWS, LON)
    copies[0].wait()
    mine = kept[1]

    def weighed(moved, fixed):
        upper = jnp.sum(folded(wide * (mine - moved) ** 2), 0, keepdims=True)
        lower = jnp.sum(folded(low * (fixed_mine - fixed) ** 2), 0, keepdims=True)
        return upper + lower

    rows = [weighed(kept[0], observed[:HALF].reshape(HALF * ROWS, LON))]
    for n in range(MEMBERS):
        copies[1 + n].wait()
        rows.append(weighed(fields[n, :WIDE], fields[n, FIXED_AT:]))
    all_rows = jnp.concatenate(rows[1:], 0)
    spot = lax.broadcasted_iota(jnp.int32, (MEMBERS, 128), 0)
    all_rows = jnp.where(spot == me, rows[0], all_rows)
    for tile in range(TILES):
        partials[tile] = all_rows
    copy = pltpu.make_async_copy(partials, partials_out, sems.at[0])
    copy.start()
    copy.wait()


def backward_kernel(
    place, lat, totals, fields_in, kept_in, stack_in, hidden_1_in, slope_1_in, hidden_2_in,
    slope_2_in, w_back_2_in, w_back_1_in,
    mine, theirs,
    fields, kept, stack, hidden_1, slope_1, hidden_2, slope_2, w_back_2, w_back_1,
    coupled, turned_2, sum_out, sum_mid, sum_in, packed, sems,
):
    sources = [kept_in, fields_in, w_back_2_in, slope_2_in, hidden_2_in, hidden_1_in]
    sources += [w_back_1_in, slope_1_in, stack_in]
    targets = [kept, fields, w_back_2, slope_2, hidden_2, hidden_1, w_back_1, slope_1, stack]
    copies = []
    for source, target in zip(sources, targets):
        copies.append(pltpu.make_async_copy(source, target, sems.at[len(copies)]))
        copies[-1].start()
    me, base, core = place[0], place[1], place[2]
    total = totals[0]
    for tile in range(1, TILES):
        total = total + totals[tile]
    distances = jnp.sqrt(jnp.sum(total, 1, keepdims=True) / ENTRIES + EPSILON)
    is_me = lax.broadcasted_iota(jnp.int32, (MEMBERS, 1), 0) == me
    shares = jnp.where(is_me, distances / MEMBERS, -distances / (2.0 * MEMBERS * MEMBERS))
    share = jnp.sum(shares, 0, keepdims=True) / TILES
    weights = 1.0 / (jnp.where(is_me, MEMBERS, MEMBERS * MEMBERS) * distances)
    own_weight = jnp.sum(jnp.where(is_me, weights, 0.0), 0, keepdims=True)
    weights = jnp.where(is_me, 0.0, weights)
    sum_out[...] = jnp.zeros_like(sum_out)
    sum_mid[...] = jnp.zeros_like(sum_mid)
    sum_in[...] = jnp.zeros_like(sum_in)
    copies[0].wait()
    log_scale, moving, observed, moved = kept[0], kept[1], kept[2], kept[3]
    inner = (moved - observed) * own_weight
    copies[1].wait()
    for n in range(MEMBERS):
        inner = inner - weights[n : n + 1] * (moved - fields[n, :WIDE])
    upper = lat[:WIDE, :1] * inner / math.sqrt(ENTRIES)
    scaled = upper * moving * jnp.exp(log_scale) * (1.0 - log_scale * log_scale)
    blank = jnp.zeros((8 - HALF, LON), F32)
    for row in range(ROWS + 4):
        here = slice(row * HALF, (row + 1) * HALF)
        field = jnp.concatenate([scaled[here], blank, upper[here], blank], 0)
        for shift in range(3):
            part = turned(field, shift - 1).astype(BF16)
            coupled[row, shift * 16 : (shift + 1) * 16, :] = part
    copies[2].wait()
    copies[3].wait()

    def second(row):
        back = dot(w_back_2[...], coupled[pl.ds(row, 3)].reshape(144, LON))
        grad = back * slope_2[row] * inside(base, row - 1)
        for shift in range(3):
            part = turned(grad, shift - 1).astype(BF16)
            turned_2[row, shift * CH : (shift + 1) * CH, :] = part

    loop(0, ROWS + 2, second)
    for copy in copies[4:]:
        copy.wait()

    def last(row):
        near_2 = hidden_2[pl.ds(row + 2, 3)].reshape(3 * CH, LON)
        sum_out[...] += dot_cells(coupled[row + 2], near_2)
        near_1 = hidden_1[pl.ds(row + 3, 3)].reshape(3 * CH, LON)
        sum_mid[...] += dot_cells(turned_2[row + 1], near_1)
        back = dot(w_back_1[...], turned_2[pl.ds(row, 3)].reshape(9 * CH, LON))
        grad = (back * slope_1[row]).astype(BF16)
        near_0 = stack[pl.ds(row + 4, 3)].reshape(9 * FIELDS, LON)
        sum_in[...] += dot_cells(near_0, grad)

    loop(0, ROWS, last)
    packed[5 * CH :, :] = jnp.zeros((CH, 128), F32)
    packed[4 * CH : 5 * CH, CH:] = jnp.zeros((CH, CH), F32)
    for tap in range(9):
        a, b = tap // 3, tap % 3
        at, side = place_mid(tap)
        packed[at : at + CH, side] = sum_mid[b * CH : (b + 1) * CH, a * CH : (a + 1) * CH]
        at = 5 * CH + tap * VARS
        across = slice(a * CH, (a + 1) * CH)
        packed[at : at + HALF, :CH] = sum_out[b * 16 : b * 16 + HALF, across]
        packed[at + HALF : at + VARS, :CH] = sum_out[b * 16 + 8 : b * 16 + 8 + HALF, across]
        at = 4 * CH + tap * INPUTS
        packed[at : at + INPUTS, CH:] = sum_in[tap * FIELDS : tap * FIELDS + INPUTS]
    packed[6 * CH - 1 :, 127:] = share
    half = MEMBERS * CHUNK
    for copy in range(2):

        @pl.when(core == copy)
        def _():
            mine[...] = packed[copy * half : (copy + 1) * half, :]
            theirs[...] = packed[(1 - copy) * half : (2 - copy) * half, :]


def place_mid(tap):
    return (tap * CH, slice(0, CH)) if tap < 5 else ((tap - 5) * CH, slice(CH, 2 * CH))


def unpack_kernel(place, mine, theirs, grad_in, grad_mid, grad_out, energy, packed):
    half = MEMBERS * CHUNK
    for copy in range(2):

        @pl.when(place[2] == copy)
        def _():
            packed[copy * half : (copy + 1) * half, :] = mine[...]
            packed[(1 - copy) * half : (2 - copy) * half, :] = theirs[...]

    for tap in range(9):
        at, side = place_mid(tap)
        grad_mid[tap] = packed[at : at + CH, side]
        at = 5 * CH + tap * VARS
        grad_out[tap] = packed[at : at + VARS, :CH]
        at = 4 * CH + tap * INPUTS
        grad_in[tap] = packed[at : at + INPUTS, CH:]
    energy[...] = packed[6 * CH - 1 :, 127:]


VMEM_LIMIT = 32 * 2**20
VMEM = pl.BlockSpec(memory_space=pltpu.VMEM)
HBM = pl.BlockSpec(memory_space=pltpu.HBM)


def call(kernel, ins, outs, scratch=(), copies=0, flops=10**6):
    held = [pltpu.VMEM(shape, dtype) for shape, dtype in scratch]
    if copies > 0:
        held.append(pltpu.SemaphoreType.DMA((copies,)))
    return pl.pallas_call(
        kernel,
        out_shape=[jax.ShapeDtypeStruct(shape, dtype) for shape, dtype, spec in outs],
        in_specs=[pl.BlockSpec(memory_space=pltpu.SMEM)] + ins,
        out_specs=[spec for shape, dtype, spec in outs],
        scratch_shapes=held,
        compiler_params=pltpu.CompilerParams(vmem_limit_bytes=VMEM_LIMIT),
        cost_estimate=pl.CostEstimate(flops=flops, bytes_accessed=10**6, transcendentals=0),
    )


def per_device(members, condition, observed, kernel_in, kernel_mid, kernel_out):
    members = members[0]
    core = lax.axis_index("core")
    tile = lax.axis_index(TILE)
    place = jnp.stack([lax.axis_index("member"), tile * ROWS, core]).astype(jnp.int32)
    table = jnp.asarray(lat_table())
    lat = lax.dynamic_slice_in_dim(table, tile, 1, 0)[0]
    lat = jnp.broadcast_to(lat[:, None], (FIXED_AT + ROWS, 128))
    edge = ((HALO, FIELDS, LON), F32, VMEM)
    own, edge_far, edge_near = call(
        pack_kernel, [VMEM] * 3, [((ROWS, FIELDS, LON), F32, VMEM), edge, edge]
    )(place, members, condition, observed)
    across = [(i, i + 1) for i in range(1, TILES - 1, 2)]
    far = lax.ppermute(edge_far, TILE, across + [(j, i) for i, j in across])
    near = lax.ppermute(edge_near, "core", [(0, 1), (1, 0)])
    w_shapes = [(CH, 9 * FIELDS), (3 * CH, 3 * CH), (48, 3 * CH), (CH, 144), (CH, 9 * CH)]
    w_in, w_mid, w_out, w_back_2, w_back_1 = call(
        weights_kernel,
        [VMEM] * 3,
        [(shape, BF16, VMEM) for shape in w_shapes[:3]]
        + [(shape, BF16, HBM) for shape in w_shapes[3:]],
        [(shape, F32) for shape in w_shapes] + [(shape, BF16) for shape in w_shapes[3:]],
        copies=2,
    )(place, kernel_in, kernel_mid, kernel_out)
    saved = [
        ((ROWS + 10, 3 * FIELDS, LON), BF16),
        ((ROWS + 8, CH, LON), BF16),
        ((ROWS, CH, LON), F32),
        ((ROWS + 6, CH, LON), BF16),
        ((ROWS + 2, CH, LON), F32),
    ]
    rows = FIXED_AT + HALF * ROWS
    fields_shape = ((MEMBERS, rows, LON), F32)
    kept_shape = ((4, WIDE, LON), F32)
    send, pushed, kept, stack, hidden_1, slope_1, hidden_2, slope_2 = call(
        forward_kernel,
        [VMEM] * 7,
        [fields_shape + (HBM,), ((VARS, ROWS, LON), F32, VMEM), kept_shape + (HBM,)]
        + [shape + (HBM,) for shape in saved],
        [((rows, LON), F32), kept_shape] + saved + [((2 * HALO, FIELDS, LON), F32)],
        copies=MEMBERS + 6,
        flops=10**9,
    )(place, far, near, own, members, w_in, w_mid, w_out)
    fields = lax.all_to_all(send, "member", 0, 0)
    partials_shape = ((TILES, MEMBERS, 128), F32)
    (partials,) = call(
        distance_kernel,
        [VMEM] * 3 + [HBM] * 2,
        [partials_shape + (HBM,)],
        [fields_shape, ((2, WIDE, LON), F32), partials_shape],
        copies=MEMBERS + 1,
    )(place, lat, members, observed, fields, kept)
    totals = lax.all_to_all(partials, TILE, 0, 0)
    mine, theirs = call(
        backward_kernel,
        [VMEM] * 2 + [HBM] * 9,
        [((MEMBERS * CHUNK, 128), F32, VMEM)] * 2,
        [fields_shape, kept_shape]
        + saved
        + [(shape, BF16) for shape in w_shapes[3:]]
        + [
            ((ROWS + 4, 48, LON), BF16),
            ((ROWS + 2, 3 * CH, LON), BF16),
            ((48, 3 * CH), F32),
            ((3 * CH, 3 * CH), F32),
            ((9 * FIELDS, CH), F32),
            ((6 * CH, 128), F32),
        ],
        copies=9,
        flops=10**9,
    )(
        place, lat, totals, fields, kept, stack, hidden_1, slope_1, hidden_2, slope_2,
        w_back_2, w_back_1,
    )
    swap = [(0, 1), (1, 0)]
    mine = mine + lax.ppermute(theirs, "core", swap)
    chunk = jnp.sum(lax.all_to_all(mine.reshape(MEMBERS, CHUNK, 128), "member", 0, 0), 0)
    chunk = jnp.sum(spread(chunk, "ring", RING), 0)
    half = spread(chunk, "member", MEMBERS).reshape(MEMBERS * CHUNK, 128)
    other = lax.ppermute(half, "core", swap)
    grad_in, grad_mid, grad_out, energy = call(
        unpack_kernel,
        [VMEM] * 2,
        [
            ((9, INPUTS, CH), F32, VMEM),
            ((9, CH, CH), F32, VMEM),
            ((9, VARS, CH), F32, VMEM),
            ((1, 1), F32, VMEM),
        ],
        [((6 * CH, 128), F32)],
    )(place, half, other)
    return (pushed[None], energy[0, 0], grad_in.transpose(0, 2, 1), grad_mid, grad_out)


def solution(mesh):
    fine = Mesh(mesh.devices.reshape(MEMBERS, -1, 2), ("member",) + TILE)
    in_specs = (
        P("member", None, TILE, None),
        P(None, TILE, None),
        P(None, TILE, None),
        P(),
        P(),
        P(),
    )
    out_specs = (P("member", None, TILE, None), P(), P(), P(), P())
    return jax.shard_map(
        per_device, mesh=fine, in_specs=in_specs, out_specs=out_specs, check_vma=False
    )
```

```python
import functools
import math

import jax
import jax.numpy as jnp
import numpy as np
from jax import lax
from jax.experimental import pallas as pl
from jax.experimental.pallas import tpu as pltpu
from jax.sharding import Mesh, PartitionSpec as P

EPSILON = 1e-06
MEMBERS, NLAT, LON, ROWS = 8, 256, 512, 8
VARS, HALF, COND, CH = 6, 3, 6, 64
TILES, RING = 32, 16
ENTRIES = VARS * NLAT * LON
HALO = 5
FIELDS = 16
INPUTS = HALF + COND
WIDE = (ROWS + 4) * HALF
FIXED_AT = 40
CHUNK = 24
TILE = ("ring", "core")
F32, BF16 = jnp.float32, jnp.bfloat16


def spread(value, axes, count):
    copies = jnp.broadcast_to(value[None], (count,) + value.shape)
    return lax.all_to_all(copies, axes, 0, 0)


def lat_table():
    rows = np.arange(NLAT)
    cosine = np.cos((-90.0 + 180.0 * (rows + 0.5) / NLAT) * (np.pi / 180.0))
    lat = (cosine / cosine.mean()).astype(np.float32)
    padded = np.pad(lat, (2, 2))
    table = np.zeros((TILES, FIXED_AT + ROWS), np.float32)
    for tile in range(TILES):
        wide = padded[tile * ROWS : tile * ROWS + ROWS + 4]
        table[tile, :WIDE] = np.repeat(wide, HALF)
        table[tile, FIXED_AT:] = lat[tile * ROWS : (tile + 1) * ROWS]
    return table


def turned(value, step):
    return value if step == 0 else pltpu.roll(value, step % LON, 1)


def dot(left, right):
    return jnp.dot(left, right, preferred_element_type=F32)


def dot_cells(left, right):
    return lax.dot_general(left, right, (((1,), (1,)), ((), ())), preferred_element_type=F32)


def inside(base, row):
    row = base + row
    return jnp.where((row >= 0) & (row < NLAT), 1.0, 0.0).astype(F32)


def sigmoid(value):
    return 0.5 * jnp.tanh(0.5 * value) + 0.5


def loop(start, stop, body):
    lax.fori_loop(start, stop, lambda row, carry: (body(row), carry)[1], 0, unroll=2)


def pack_kernel(place, members, condition, observed, own, edge_far, edge_near):
    for row in range(ROWS):
        own[row, :HALF, :] = members[:HALF, row, :]
        own[row, HALF:INPUTS, :] = condition[:, row, :]
        own[row, INPUTS : INPUTS + HALF, :] = members[HALF:, row, :]
        own[row, INPUTS + HALF : INPUTS + 2 * HALF, :] = observed[HALF:, row, :]
        own[row, FIELDS - 1 :, :] = jnp.zeros((1, LON), F32)
    odd = place[2] == 1
    for row in range(HALO):
        initial, last = own[row], own[ROWS - HALO + row]
        edge_far[row] = jnp.where(odd, last, initial)
        edge_near[row] = jnp.where(odd, initial, last)


def weights_kernel(
    place, kernel_in, kernel_mid, kernel_out, w_in, w_mid, w_out, w_back_2, w_back_1,
    flat_in, square, flat_out, back_2, back_1, held_2, held_1, sems,
):
    flat_out[...] = jnp.zeros_like(flat_out)
    back_2[...] = jnp.zeros_like(back_2)
    for tap in range(9):
        a, b = tap // 3, tap % 3
        back = 3 * (2 - a) + b
        first = kernel_in[tap].astype(F32)
        first = jnp.concatenate([first, jnp.zeros((FIELDS - INPUTS, CH), F32)], 0).T
        flat_in[:, tap * FIELDS : (tap + 1) * FIELDS] = first
        mid = kernel_mid[tap].astype(F32)
        square[b * CH : (b + 1) * CH, a * CH : (a + 1) * CH] = mid
        back_1[:, back * CH : (back + 1) * CH] = mid.T
        out = kernel_out[tap].astype(F32)
        across = slice(a * CH, (a + 1) * CH)
        flat_out[b * 16 : b * 16 + HALF, across] = out[:HALF]
        flat_out[b * 16 + 8 : b * 16 + 8 + HALF, across] = out[HALF:]
        out = jnp.concatenate([out, jnp.zeros((8 - VARS, CH), F32)], 0).T
        back_2[:, back * 16 : back * 16 + HALF] = out[:, :HALF]
        back_2[:, back * 16 + 8 : back * 16 + 8 + HALF] = out[:, HALF:VARS]
    held_2[...] = back_2[...].astype(BF16)
    held_1[...] = back_1[...].astype(BF16)
    copies = [
        pltpu.make_async_copy(held_2, w_back_2, sems.at[0]),
        pltpu.make_async_copy(held_1, w_back_1, sems.at[1]),
    ]
    for copy in copies:
        copy.start()
    w_in[...] = flat_in[...].astype(BF16)
    w_mid[...] = square[...].astype(BF16)
    w_out[...] = flat_out[...].astype(BF16)
    for copy in copies:
        copy.wait()


def forward_kernel(
    place, far, near, own, members, w_in, w_mid, w_out,
    send_out, pushed, kept_out, stack_out, hidden_1_out, slope_1_out, hidden_2_out, slope_2_out,
    send, kept, stack, hidden_1, slope_1, hidden_2, slope_2, edges, sems,
):
    base = place[1]
    odd = place[2] == 1
    copies = []

    def keep(source, target):
        copy = pltpu.make_async_copy(source, target, sems.at[len(copies)])
        copy.start()
        copies.append(copy)

    for row in range(HALO):
        edges[row] = jnp.where(odd, near[row], far[row])
        edges[HALO + row] = jnp.where(odd, far[row], near[row])

    def wide(row):
        if row < HALO:
            return edges[row]
        return own[row - HALO] if row < HALO + ROWS else edges[row - ROWS]

    for row in range(ROWS + 2 * HALO):
        field = wide(row)
        for shift in range(3):
            part = turned(field, 1 - shift).astype(BF16)
            stack[row, shift * FIELDS : (shift + 1) * FIELDS, :] = part
    keep(stack, stack_out)

    def first(row, kept_row):
        pre = dot(w_in[...], stack[pl.ds(row, 3)].reshape(9 * FIELDS, LON))
        gate = sigmoid(pre)
        hidden_1[row] = (pre * gate * inside(base, row - 4)).astype(BF16)
        if kept_row:
            slope_1[row - 4] = gate * (1.0 + pre * (1.0 - gate))

    loop(0, 4, functools.partial(first, kept_row=False))
    loop(4, 12, functools.partial(first, kept_row=True))
    loop(12, 16, functools.partial(first, kept_row=False))
    keep(hidden_1, hidden_1_out)
    keep(slope_1, slope_1_out)

    def second(row, kept_row):
        part = dot(w_mid[...], hidden_1[pl.ds(row, 3)].reshape(3 * CH, LON))
        pre = turned(part[:CH], 1) + part[CH : 2 * CH] + turned(part[2 * CH :], -1)
        gate = sigmoid(pre)
        hidden_2[row] = (pre * gate * inside(base, row - 3)).astype(BF16)
        if kept_row:
            slope_2[row - 2] = gate * (1.0 + pre * (1.0 - gate))

    loop(0, 2, functools.partial(second, kept_row=False))
    loop(2, 12, functools.partial(second, kept_row=True))
    loop(12, 14, functools.partial(second, kept_row=False))
    keep(hidden_2, hidden_2_out)
    keep(slope_2, slope_2_out)

    send[WIDE:FIXED_AT, :] = jnp.zeros((FIXED_AT - WIDE, LON), F32)
    send[FIXED_AT:, :] = members[:HALF].reshape(HALF * ROWS, LON)
    for row in range(ROWS + 4):
        part = dot(w_out[...], hidden_2[row : row + 3].reshape(3 * CH, LON))
        both = turned(part[:16], 1) + part[16:32] + turned(part[32:], -1)
        log_scale = jnp.tanh(both[:HALF])
        field = wide(row + 3)
        moving = field[INPUTS : INPUTS + HALF]
        moved = moving * jnp.exp(log_scale) + both[8 : 8 + HALF]
        here = slice(row * HALF, (row + 1) * HALF)
        kept[0, here, :] = log_scale
        kept[1, here, :] = moving
        kept[2, here, :] = field[INPUTS + HALF : INPUTS + 2 * HALF]
        kept[3, here, :] = moved
        send[here, :] = moved
        if 2 <= row < 2 + ROWS:
            for var in range(HALF):
                pushed[HALF + var, row - 2 : row - 1, :] = moved[var : var + 1]
    for member in range(MEMBERS):
        keep(send, send_out.at[member])
    keep(kept, kept_out)
    pushed[:HALF] = members[:HALF]
    for copy in copies:
        copy.wait()


def folded(value):
    return sum(value[..., at : at + 128] for at in range(0, LON, 128))


def distance_kernel(
    place, lat, members, observed, fields_in, kept_in, partials_out, fields, kept, partials, sems
):
    copies = [pltpu.make_async_copy(kept_in.at[2:4], kept, sems.at[MEMBERS])]
    for n in range(MEMBERS):
        copies.append(pltpu.make_async_copy(fields_in.at[n], fields.at[n], sems.at[n]))
    for copy in copies:
        copy.start()
    me = place[0]
    spot = lax.broadcasted_iota(jnp.int32, (WIDE, 1), 0)
    wide = jnp.where((spot >= 2 * HALF) & (spot < WIDE - 2 * HALF), lat[:WIDE, :1], 0.0)
    low = jnp.concatenate([lat[FIXED_AT:, :1]] * HALF, 0)
    fixed_mine = members[:HALF].reshape(HALF * ROWS, LON)
    copies[0].wait()
    mine = kept[1]

    def weighed(moved, fixed):
        upper = jnp.sum(folded(wide * (mine - moved) ** 2), 0, keepdims=True)
        lower = jnp.sum(folded(low * (fixed_mine - fixed) ** 2), 0, keepdims=True)
        return upper + lower

    rows = [weighed(kept[0], observed[:HALF].reshape(HALF * ROWS, LON))]
    for n in range(MEMBERS):
        copies[1 + n].wait()
        rows.append(weighed(fields[n, :WIDE], fields[n, FIXED_AT:]))
    all_rows = jnp.concatenate(rows[1:], 0)
    spot = lax.broadcasted_iota(jnp.int32, (MEMBERS, 128), 0)
    all_rows = jnp.where(spot == me, rows[0], all_rows)
    for tile in range(TILES):
        partials[tile] = all_rows
    copy = pltpu.make_async_copy(partials, partials_out, sems.at[0])
    copy.start()
    copy.wait()


def backward_kernel(
    place, lat, totals, fields_in, kept_in, stack_in, hidden_1_in, slope_1_in, hidden_2_in,
    slope_2_in, w_back_2_in, w_back_1_in,
    mine, theirs,
    fields, kept, stack, hidden_1, slope_1, hidden_2, slope_2, w_back_2, w_back_1,
    coupled, turned_2, sum_out, sum_mid, sum_in, packed, sems,
):
    sources = [kept_in, fields_in, w_back_2_in, slope_2_in, hidden_2_in, hidden_1_in]
    sources += [w_back_1_in, slope_1_in, stack_in]
    targets = [kept, fields, w_back_2, slope_2, hidden_2, hidden_1, w_back_1, slope_1, stack]
    copies = []
    for source, target in zip(sources, targets):
        copies.append(pltpu.make_async_copy(source, target, sems.at[len(copies)]))
        copies[-1].start()
    me, base, core = place[0], place[1], place[2]
    total = totals[0]
    for tile in range(1, TILES):
        total = total + totals[tile]
    distances = jnp.sqrt(jnp.sum(total, 1, keepdims=True) / ENTRIES + EPSILON)
    is_me = lax.broadcasted_iota(jnp.int32, (MEMBERS, 1), 0) == me
    shares = jnp.where(is_me, distances / MEMBERS, -distances / (2.0 * MEMBERS * MEMBERS))
    share = jnp.sum(shares, 0, keepdims=True) / TILES
    weights = 1.0 / (jnp.where(is_me, MEMBERS, MEMBERS * MEMBERS) * distances)
    own_weight = jnp.sum(jnp.where(is_me, weights, 0.0), 0, keepdims=True)
    weights = jnp.where(is_me, 0.0, weights)
    sum_out[...] = jnp.zeros_like(sum_out)
    sum_mid[...] = jnp.zeros_like(sum_mid)
    sum_in[...] = jnp.zeros_like(sum_in)
    copies[0].wait()
    log_scale, moving, observed, moved = kept[0], kept[1], kept[2], kept[3]
    inner = (moved - observed) * own_weight
    copies[1].wait()
    for n in range(MEMBERS):
        inner = inner - weights[n : n + 1] * (moved - fields[n, :WIDE])
    upper = lat[:WIDE, :1] * inner / math.sqrt(ENTRIES)
    scaled = upper * moving * jnp.exp(log_scale) * (1.0 - log_scale * log_scale)
    blank = jnp.zeros((8 - HALF, LON), F32)
    for row in range(ROWS + 4):
        here = slice(row * HALF, (row + 1) * HALF)
        field = jnp.concatenate([scaled[here], blank, upper[here], blank], 0)
        for shift in range(3):
            part = turned(field, shift - 1).astype(BF16)
            coupled[row, shift * 16 : (shift + 1) * 16, :] = part
    copies[2].wait()
    copies[3].wait()

    def second(row):
        back = dot(w_back_2[...], coupled[pl.ds(row, 3)].reshape(144, LON))
        grad = back * slope_2[row] * inside(base, row - 1)
        for shift in range(3):
            part = turned(grad, shift - 1).astype(BF16)
            turned_2[row, shift * CH : (shift + 1) * CH, :] = part

    loop(0, ROWS + 2, second)
    for copy in copies[4:]:
        copy.wait()

    def last(row):
        near_2 = hidden_2[pl.ds(row + 2, 3)].reshape(3 * CH, LON)
        sum_out[...] += dot_cells(coupled[row + 2], near_2)
        near_1 = hidden_1[pl.ds(row + 3, 3)].reshape(3 * CH, LON)
        sum_mid[...] += dot_cells(turned_2[row + 1], near_1)
        back = dot(w_back_1[...], turned_2[pl.ds(row, 3)].reshape(9 * CH, LON))
        grad = (back * slope_1[row]).astype(BF16)
        near_0 = stack[pl.ds(row + 4, 3)].reshape(9 * FIELDS, LON)
        sum_in[...] += dot_cells(near_0, grad)

    loop(0, ROWS, last)
    packed[5 * CH :, :] = jnp.zeros((CH, 128), F32)
    packed[4 * CH : 5 * CH, CH:] = jnp.zeros((CH, CH), F32)
    for tap in range(9):
        a, b = tap // 3, tap % 3
        at, side = place_mid(tap)
        packed[at : at + CH, side] = sum_mid[b * CH : (b + 1) * CH, a * CH : (a + 1) * CH]
        at = 5 * CH + tap * VARS
        across = slice(a * CH, (a + 1) * CH)
        packed[at : at + HALF, :CH] = sum_out[b * 16 : b * 16 + HALF, across]
        packed[at + HALF : at + VARS, :CH] = sum_out[b * 16 + 8 : b * 16 + 8 + HALF, across]
        at = 4 * CH + tap * INPUTS
        packed[at : at + INPUTS, CH:] = sum_in[tap * FIELDS : tap * FIELDS + INPUTS]
    packed[6 * CH - 1 :, 127:] = share
    half = MEMBERS * CHUNK
    for copy in range(2):

        @pl.when(core == copy)
        def _():
            mine[...] = packed[copy * half : (copy + 1) * half, :]
            theirs[...] = packed[(1 - copy) * half : (2 - copy) * half, :]


def place_mid(tap):
    return (tap * CH, slice(0, CH)) if tap < 5 else ((tap - 5) * CH, slice(CH, 2 * CH))


def unpack_kernel(place, mine, theirs, grad_in, grad_mid, grad_out, energy, packed):
    half = MEMBERS * CHUNK
    for copy in range(2):

        @pl.when(place[2] == copy)
        def _():
            packed[copy * half : (copy + 1) * half, :] = mine[...]
            packed[(1 - copy) * half : (2 - copy) * half, :] = theirs[...]

    for tap in range(9):
        at, side = place_mid(tap)
        grad_mid[tap] = packed[at : at + CH, side]
        at = 5 * CH + tap * VARS
        grad_out[tap] = packed[at : at + VARS, :CH]
        at = 4 * CH + tap * INPUTS
        grad_in[tap] = packed[at : at + INPUTS, CH:]
    energy[...] = packed[6 * CH - 1 :, 127:]


VMEM_LIMIT = 60 * 10**6
VMEM = pl.BlockSpec(memory_space=pltpu.VMEM)
HBM = pl.BlockSpec(memory_space=pltpu.HBM)


def call(kernel, ins, outs, scratch=(), copies=0, flops=10**6, vmem=VMEM_LIMIT):
    held = [pltpu.VMEM(shape, dtype) for shape, dtype in scratch]
    if copies > 0:
        held.append(pltpu.SemaphoreType.DMA((copies,)))
    return pl.pallas_call(
        kernel,
        out_shape=[jax.ShapeDtypeStruct(shape, dtype) for shape, dtype, spec in outs],
        in_specs=[pl.BlockSpec(memory_space=pltpu.SMEM)] + ins,
        out_specs=[spec for shape, dtype, spec in outs],
        scratch_shapes=held,
        compiler_params=pltpu.CompilerParams(vmem_limit_bytes=vmem),
        cost_estimate=pl.CostEstimate(flops=flops, bytes_accessed=10**6, transcendentals=0),
    )


def per_device(members, condition, observed, kernel_in, kernel_mid, kernel_out):
    members = members[0]
    core = lax.axis_index("core")
    tile = lax.axis_index(TILE)
    place = jnp.stack([lax.axis_index("member"), tile * ROWS, core]).astype(jnp.int32)
    table = jnp.asarray(lat_table())
    lat = lax.dynamic_slice_in_dim(table, tile, 1, 0)[0]
    lat = jnp.broadcast_to(lat[:, None], (FIXED_AT + ROWS, 128))
    edge = ((HALO, FIELDS, LON), F32, VMEM)
    own, edge_far, edge_near = call(
        pack_kernel, [VMEM] * 3, [((ROWS, FIELDS, LON), F32, VMEM), edge, edge]
    )(place, members, condition, observed)
    across = [(i, i + 1) for i in range(1, TILES - 1, 2)]
    far = lax.ppermute(edge_far, TILE, across + [(j, i) for i, j in across])
    near = lax.ppermute(edge_near, "core", [(0, 1), (1, 0)])
    w_shapes = [(CH, 9 * FIELDS), (3 * CH, 3 * CH), (48, 3 * CH), (CH, 144), (CH, 9 * CH)]
    w_in, w_mid, w_out, w_back_2, w_back_1 = call(
        weights_kernel,
        [VMEM] * 3,
        [(shape, BF16, VMEM) for shape in w_shapes[:3]]
        + [(shape, BF16, HBM) for shape in w_shapes[3:]],
        [(shape, F32) for shape in w_shapes] + [(shape, BF16) for shape in w_shapes[3:]],
        copies=2,
    )(place, kernel_in.transpose(0, 2, 1), kernel_mid, kernel_out)
    saved = [
        ((ROWS + 10, 3 * FIELDS, LON), BF16),
        ((ROWS + 8, CH, LON), BF16),
        ((ROWS, CH, LON), F32),
        ((ROWS + 6, CH, LON), BF16),
        ((ROWS + 2, CH, LON), F32),
    ]
    rows = FIXED_AT + HALF * ROWS
    fields_shape = ((MEMBERS, rows, LON), F32)
    kept_shape = ((4, WIDE, LON), F32)
    send, pushed, kept, stack, hidden_1, slope_1, hidden_2, slope_2 = call(
        forward_kernel,
        [VMEM] * 7,
        [fields_shape + (HBM,), ((VARS, ROWS, LON), F32, VMEM), kept_shape + (HBM,)]
        + [shape + (HBM,) for shape in saved],
        [((rows, LON), F32), kept_shape] + saved + [((2 * HALO, FIELDS, LON), F32)],
        copies=MEMBERS + 6,
        flops=10**9,
    )(place, far, near, own, members, w_in, w_mid, w_out)
    fields = lax.all_to_all(send, "member", 0, 0)
    partials_shape = ((TILES, MEMBERS, 128), F32)
    (partials,) = call(
        distance_kernel,
        [VMEM] * 3 + [HBM] * 2,
        [partials_shape + (HBM,)],
        [fields_shape, ((2, WIDE, LON), F32), partials_shape],
        copies=MEMBERS + 1,
    )(place, lat, members, observed, fields, kept)
    totals = lax.all_to_all(partials, TILE, 0, 0)
    mine, theirs = call(
        backward_kernel,
        [VMEM] * 2 + [HBM] * 9,
        [((MEMBERS * CHUNK, 128), F32, VMEM)] * 2,
        [fields_shape, kept_shape]
        + saved
        + [(shape, BF16) for shape in w_shapes[3:]]
        + [
            ((ROWS + 4, 48, LON), BF16),
            ((ROWS + 2, 3 * CH, LON), BF16),
            ((48, 3 * CH), F32),
            ((3 * CH, 3 * CH), F32),
            ((9 * FIELDS, CH), F32),
            ((6 * CH, 128), F32),
        ],
        copies=9,
        flops=10**9,
    )(
        place, lat, totals, fields, kept, stack, hidden_1, slope_1, hidden_2, slope_2,
        w_back_2, w_back_1,
    )
    swap = [(0, 1), (1, 0)]
    mine = mine + lax.ppermute(theirs, "core", swap)
    chunk = jnp.sum(lax.all_to_all(mine.reshape(MEMBERS, CHUNK, 128), "member", 0, 0), 0)
    chunk = jnp.sum(spread(chunk, "ring", RING), 0)
    half = spread(chunk, "member", MEMBERS).reshape(MEMBERS * CHUNK, 128)
    other = lax.ppermute(half, "core", swap)
    grad_in, grad_mid, grad_out, energy = call(
        unpack_kernel,
        [VMEM] * 2,
        [
            ((9, INPUTS, CH), F32, VMEM),
            ((9, CH, CH), F32, VMEM),
            ((9, VARS, CH), F32, VMEM),
            ((1, 1), F32, VMEM),
        ],
        [((6 * CH, 128), F32)],
        vmem=16 * 10**6,
    )(place, half, other)
    return (pushed[None], energy[0, 0], grad_in.transpose(0, 2, 1), grad_mid, grad_out)


def solution(mesh):
    fine = Mesh(mesh.devices.reshape(MEMBERS, -1, 2), ("member",) + TILE)
    in_specs = (
        P("member", None, TILE, None),
        P(None, TILE, None),
        P(None, TILE, None),
        P(),
        P(),
        P(),
    )
    out_specs = (P("member", None, TILE, None), P(), P(), P(), P())
    return jax.shard_map(
        per_device, mesh=fine, in_specs=in_specs, out_specs=out_specs, check_vma=False
    )
```

```python
import functools
import math

import jax
import jax.numpy as jnp
import numpy as np
from jax import lax
from jax.experimental import pallas as pl
from jax.experimental.pallas import tpu as pltpu
from jax.sharding import Mesh, PartitionSpec as P

EPSILON = 1e-06
MEMBERS, NLAT, LON, ROWS = 8, 256, 512, 8
VARS, HALF, COND, CH = 6, 3, 6, 64
TILES, RING = 32, 16
ENTRIES = VARS * NLAT * LON
HALO = 5
FIELDS = 16
INPUTS = HALF + COND
WIDE = (ROWS + 4) * HALF
FIXED_AT = 40
CHUNK = 24
TILE = ("ring", "core")
F32, BF16 = jnp.float32, jnp.bfloat16


def spread(value, axes, count):
    copies = jnp.broadcast_to(value[None], (count,) + value.shape)
    return lax.all_to_all(copies, axes, 0, 0)


def lat_table():
    rows = np.arange(NLAT)
    cosine = np.cos((-90.0 + 180.0 * (rows + 0.5) / NLAT) * (np.pi / 180.0))
    lat = (cosine / cosine.mean()).astype(np.float32)
    padded = np.pad(lat, (2, 2))
    table = np.zeros((TILES, FIXED_AT + ROWS), np.float32)
    for tile in range(TILES):
        wide = padded[tile * ROWS : tile * ROWS + ROWS + 4]
        table[tile, :WIDE] = np.repeat(wide, HALF)
        table[tile, FIXED_AT:] = lat[tile * ROWS : (tile + 1) * ROWS]
    return table


def turned(value, step):
    return value if step == 0 else pltpu.roll(value, step % LON, 1)


def dot(left, right):
    return jnp.dot(left, right, preferred_element_type=F32)


def dot_cells(left, right):
    return lax.dot_general(left, right, (((1,), (1,)), ((), ())), preferred_element_type=F32)


def inside(base, row):
    row = base + row
    return jnp.where((row >= 0) & (row < NLAT), 1.0, 0.0).astype(F32)


def sigmoid(value):
    return 0.5 * jnp.tanh(0.5 * value) + 0.5


def loop(start, stop, body):
    lax.fori_loop(start, stop, lambda row, carry: (body(row), carry)[1], 0, unroll=True)


def pack_kernel(members, condition, observed, own, edge_far, edge_near):
    for row in range(ROWS):
        own[row, :HALF, :] = members[:HALF, row, :]
        own[row, HALF:INPUTS, :] = condition[:, row, :]
        own[row, INPUTS : INPUTS + HALF, :] = members[HALF:, row, :]
        own[row, INPUTS + HALF : INPUTS + 2 * HALF, :] = observed[HALF:, row, :]
        own[row, FIELDS - 1 :, :] = jnp.zeros((1, LON), F32)
    odd = lax.axis_index("core") == 1
    for row in range(HALO):
        initial, last = own[row], own[ROWS - HALO + row]
        edge_far[row] = jnp.where(odd, last, initial)
        edge_near[row] = jnp.where(odd, initial, last)


def weights_kernel(
    kernel_in, kernel_mid, kernel_out, w_in, w_mid, w_out, w_back_2, w_back_1,
    flat_in, square, flat_out, back_2, back_1, held_2, held_1, sems,
):
    flat_out[...] = jnp.zeros_like(flat_out)
    back_2[...] = jnp.zeros_like(back_2)
    for tap in range(9):
        a, b = tap // 3, tap % 3
        back = 3 * (2 - a) + b
        first = kernel_in[tap].astype(F32)
        first = jnp.concatenate([first, jnp.zeros((FIELDS - INPUTS, CH), F32)], 0).T
        flat_in[:, tap * FIELDS : (tap + 1) * FIELDS] = first
        mid = kernel_mid[tap].astype(F32)
        square[b * CH : (b + 1) * CH, a * CH : (a + 1) * CH] = mid
        back_1[a * CH : (a + 1) * CH, b * CH : (b + 1) * CH] = mid.T
        out = kernel_out[tap].astype(F32)
        across = slice(a * CH, (a + 1) * CH)
        flat_out[b * 16 : b * 16 + HALF, across] = out[:HALF]
        flat_out[b * 16 + 8 : b * 16 + 8 + HALF, across] = out[HALF:]
        out = jnp.concatenate([out, jnp.zeros((8 - VARS, CH), F32)], 0).T
        back_2[:, back * 16 : back * 16 + HALF] = out[:, :HALF]
        back_2[:, back * 16 + 8 : back * 16 + 8 + HALF] = out[:, HALF:VARS]
    held_2[...] = back_2[...].astype(BF16)
    held_1[...] = back_1[...].astype(BF16)
    copies = [
        pltpu.make_async_copy(held_2, w_back_2, sems.at[0]),
        pltpu.make_async_copy(held_1, w_back_1, sems.at[1]),
    ]
    for copy in copies:
        copy.start()
    w_in[...] = flat_in[...].astype(BF16)
    w_mid[...] = square[...].astype(BF16)
    w_out[...] = flat_out[...].astype(BF16)
    for copy in copies:
        copy.wait()


def forward_kernel(
    place, far, near, own, members, w_in, w_mid, w_out,
    send_out, pushed, kept_out, stack_out, hidden_1_out, slope_1_out, hidden_2_out, slope_2_out,
    send, kept, stack, hidden_1, slope_1, hidden_2, slope_2, edges, sems,
):
    base = place[1]
    odd = place[2] == 1
    copies = []

    def keep(source, target):
        copy = pltpu.make_async_copy(source, target, sems.at[len(copies)])
        copy.start()
        copies.append(copy)

    for row in range(HALO):
        edges[row] = jnp.where(odd, near[row], far[row])
        edges[HALO + row] = jnp.where(odd, far[row], near[row])

    def wide(row):
        if row < HALO:
            return edges[row]
        return own[row - HALO] if row < HALO + ROWS else edges[row - ROWS]

    for row in range(ROWS + 2 * HALO):
        field = wide(row)
        for shift in range(3):
            part = turned(field, 1 - shift).astype(BF16)
            stack[row, shift * FIELDS : (shift + 1) * FIELDS, :] = part
    keep(stack.at[4:14], stack_out)

    def first(row, kept_row):
        pre = dot(w_in[...], stack[pl.ds(row, 3)].reshape(9 * FIELDS, LON))
        gate = sigmoid(pre)
        hidden_1[row] = (pre * gate * inside(base, row - 4)).astype(BF16)
        if kept_row:
            slope_1[row - 4] = gate * (1.0 + pre * (1.0 - gate))

    loop(0, 4, functools.partial(first, kept_row=False))
    loop(4, 12, functools.partial(first, kept_row=True))
    loop(12, 16, functools.partial(first, kept_row=False))
    keep(hidden_1.at[3:13], hidden_1_out)
    keep(slope_1, slope_1_out)

    def second(row, kept_row):
        part = dot(w_mid[...], hidden_1[pl.ds(row, 3)].reshape(3 * CH, LON))
        pre = turned(part[:CH], 1) + part[CH : 2 * CH] + turned(part[2 * CH :], -1)
        gate = sigmoid(pre)
        hidden_2[row] = (pre * gate * inside(base, row - 3)).astype(BF16)
        if kept_row:
            slope_2[row - 2] = gate * (1.0 + pre * (1.0 - gate))

    loop(0, 2, functools.partial(second, kept_row=False))
    loop(2, 12, functools.partial(second, kept_row=True))
    loop(12, 14, functools.partial(second, kept_row=False))
    keep(hidden_2.at[2:12], hidden_2_out)
    keep(slope_2, slope_2_out)

    send[WIDE:FIXED_AT, :] = jnp.zeros((FIXED_AT - WIDE, LON), F32)
    send[FIXED_AT:, :] = members[:HALF].reshape(HALF * ROWS, LON)
    for row in range(ROWS + 4):
        part = dot(w_out[...], hidden_2[row : row + 3].reshape(3 * CH, LON))
        both = turned(part[:16], 1) + part[16:32] + turned(part[32:], -1)
        log_scale = jnp.tanh(both[:HALF])
        field = wide(row + 3)
        moving = field[INPUTS : INPUTS + HALF]
        moved = moving * jnp.exp(log_scale) + both[8 : 8 + HALF]
        here = slice(row * HALF, (row + 1) * HALF)
        kept[0, here, :] = log_scale
        kept[1, here, :] = moving
        kept[2, here, :] = field[INPUTS + HALF : INPUTS + 2 * HALF]
        kept[3, here, :] = moved
        send[here, :] = moved
        if 2 <= row < 2 + ROWS:
            for var in range(HALF):
                pushed[HALF + var, row - 2 : row - 1, :] = moved[var : var + 1]
    for member in range(MEMBERS):
        keep(send, send_out.at[member])
    keep(kept, kept_out)
    pushed[:HALF] = members[:HALF]
    for copy in copies:
        copy.wait()


def folded(value):
    return sum(value[..., at : at + 128] for at in range(0, LON, 128))


def distance_kernel(place, lat, members, observed, fields, kept, partials):
    me = place[0]
    spot = lax.broadcasted_iota(jnp.int32, (WIDE, 1), 0)
    wide = jnp.where((spot >= 2 * HALF) & (spot < WIDE - 2 * HALF), lat[:WIDE, :1], 0.0)
    low = jnp.concatenate([lat[FIXED_AT:, :1]] * HALF, 0)
    fixed_mine = members[:HALF].reshape(HALF * ROWS, LON)
    mine = kept[3]

    def weighed(moved, fixed):
        upper = jnp.sum(folded(wide * (mine - moved) ** 2), 0, keepdims=True)
        lower = jnp.sum(folded(low * (fixed_mine - fixed) ** 2), 0, keepdims=True)
        return upper + lower

    to_observed = weighed(kept[2], observed[:HALF].reshape(HALF * ROWS, LON))
    rows = [weighed(fields[n, :WIDE], fields[n, FIXED_AT:]) for n in range(MEMBERS)]
    all_rows = jnp.concatenate(rows, 0)
    spot = lax.broadcasted_iota(jnp.int32, (MEMBERS, 128), 0)
    partials[...] = jnp.where(spot == me, to_observed, all_rows)


def started(pairs, sems):
    copies = [
        pltpu.make_async_copy(source, target, sems.at[at])
        for at, (source, target) in enumerate(pairs)
    ]
    for copy in copies:
        copy.start()
    return copies


def backward_kernel(
    place, lat_in, totals_in, fields_in, kept_in, stack_in, hidden_1_in, slope_1_in, hidden_2_in,
    slope_2_in, w_back_2_in, w_back_1_in,
    mine, theirs,
    lat, totals, fields, kept, stack, hidden_1, slope_1, hidden_2, slope_2, w_back_2, w_back_1,
    coupled, turned_2, by_row, sum_out, sum_mid, sum_in, packed, sems,
):
    sources = [totals_in, lat_in, kept_in, fields_in.at[:, :FIXED_AT], w_back_2_in, slope_2_in]
    sources += [w_back_1_in, hidden_1_in, hidden_2_in, slope_1_in, stack_in]
    targets = [totals, lat, kept, fields, w_back_2, slope_2]
    targets += [w_back_1, hidden_1, hidden_2, slope_1, stack]
    copies = started(list(zip(sources, targets)), sems)
    me, base, core = place[0], place[1], place[2]
    sum_out[...] = jnp.zeros_like(sum_out)
    sum_mid[...] = jnp.zeros_like(sum_mid)
    sum_in[...] = jnp.zeros_like(sum_in)
    copies[0].wait()
    total = totals[0]
    for tile in range(1, RING):
        total = total + totals[tile]
    distances = jnp.sqrt(jnp.sum(total, 1, keepdims=True) / ENTRIES + EPSILON)
    is_me = lax.broadcasted_iota(jnp.int32, (MEMBERS, 1), 0) == me
    shares = jnp.where(is_me, distances / MEMBERS, -distances / (2.0 * MEMBERS * MEMBERS))
    share = jnp.sum(shares, 0, keepdims=True) / TILES
    weights = 1.0 / (jnp.where(is_me, MEMBERS, MEMBERS * MEMBERS) * distances)
    own_weight = jnp.sum(jnp.where(is_me, weights, 0.0), 0, keepdims=True)
    weights = jnp.where(is_me, 0.0, weights)
    copies[1].wait()
    copies[2].wait()
    log_scale, moving, observed, moved = kept[0], kept[1], kept[2], kept[3]
    inner = (moved - observed) * own_weight
    copies[3].wait()
    for n in range(MEMBERS):
        inner = inner - weights[n : n + 1] * (moved - fields[n, :WIDE])
    upper = lat[:WIDE, :1] * inner / math.sqrt(ENTRIES)
    scaled = upper * moving * jnp.exp(log_scale) * (1.0 - log_scale * log_scale)
    blank = jnp.zeros((8 - HALF, LON), F32)
    for row in range(ROWS + 4):
        here = slice(row * HALF, (row + 1) * HALF)
        field = jnp.concatenate([scaled[here], blank, upper[here], blank], 0)
        for shift in range(3):
            part = turned(field, shift - 1).astype(BF16)
            coupled[row, shift * 16 : (shift + 1) * 16, :] = part
    copies[4].wait()
    copies[5].wait()

    def second(row):
        back = dot(w_back_2[...], coupled[pl.ds(row, 3)].reshape(144, LON))
        grad = back * slope_2[row] * inside(base, row - 1)
        for shift in range(3):
            part = turned(grad, shift - 1).astype(BF16)
            turned_2[row, shift * CH : (shift + 1) * CH, :] = part

    loop(0, ROWS + 2, second)
    copies[6].wait()

    def across_rows(row):
        by_row[row] = dot(w_back_1[...], turned_2[row])

    loop(0, ROWS + 2, across_rows)
    copies[7].wait()

    def middle(row):
        near = hidden_1[pl.ds(row, 3)].reshape(3 * CH, LON)
        sum_mid[...] += dot_cells(turned_2[row + 1], near)

    loop(0, ROWS, middle)
    copies[8].wait()

    def outer(row):
        near = hidden_2[pl.ds(row, 3)].reshape(3 * CH, LON)
        sum_out[...] += dot_cells(coupled[row + 2], near)

    loop(0, ROWS, outer)
    copies[9].wait()
    copies[10].wait()

    def last(row):
        back = by_row[row + 2, :CH] + by_row[row + 1, CH : 2 * CH] + by_row[row, 2 * CH :]
        grad = (back * slope_1[row]).astype(BF16)
        near = stack[pl.ds(row, 3)].reshape(9 * FIELDS, LON)
        sum_in[...] += dot_cells(near, grad)

    loop(0, ROWS, last)
    packed[5 * CH :, :] = jnp.zeros((CH, 128), F32)
    packed[4 * CH : 5 * CH, CH:] = jnp.zeros((CH, CH), F32)
    for tap in range(9):
        a, b = tap // 3, tap % 3
        at, side = place_mid(tap)
        packed[at : at + CH, side] = sum_mid[b * CH : (b + 1) * CH, a * CH : (a + 1) * CH]
        at = 5 * CH + tap * VARS
        across = slice(a * CH, (a + 1) * CH)
        packed[at : at + HALF, :CH] = sum_out[b * 16 : b * 16 + HALF, across]
        packed[at + HALF : at + VARS, :CH] = sum_out[b * 16 + 8 : b * 16 + 8 + HALF, across]
        at = 4 * CH + tap * INPUTS
        packed[at : at + INPUTS, CH:] = sum_in[tap * FIELDS : tap * FIELDS + INPUTS]
    packed[6 * CH - 1 :, 127:] = share
    half = MEMBERS * CHUNK
    for copy in range(2):

        @pl.when(core == copy)
        def _():
            mine[...] = packed[copy * half : (copy + 1) * half, :]
            theirs[...] = packed[(1 - copy) * half : (2 - copy) * half, :]


def place_mid(tap):
    return (tap * CH, slice(0, CH)) if tap < 5 else ((tap - 5) * CH, slice(CH, 2 * CH))


def unpack_kernel(place, chunks, grad_in, grad_mid, grad_out, energy, packed):
    core = place[2]
    for member in range(MEMBERS):
        first, second = chunks[member, 0], chunks[member, 1]
        at = member * CHUNK
        packed[at : at + CHUNK, :] = jnp.where(core == 0, first, second)
        at += MEMBERS * CHUNK
        packed[at : at + CHUNK, :] = jnp.where(core == 0, second, first)
    for tap in range(9):
        at, side = place_mid(tap)
        grad_mid[tap] = packed[at : at + CH, side]
        at = 5 * CH + tap * VARS
        grad_out[tap] = packed[at : at + VARS, :CH]
        at = 4 * CH + tap * INPUTS
        grad_in[tap] = packed[at : at + INPUTS, CH:]
    energy[...] = packed[6 * CH - 1 :, 127:]


VMEM_LIMIT = 60 * 10**6
VMEM = pl.BlockSpec(memory_space=pltpu.VMEM)
HBM = pl.BlockSpec(memory_space=pltpu.HBM)
SMEM = pl.BlockSpec(memory_space=pltpu.SMEM)


def call(kernel, ins, outs, scratch=(), copies=0, flops=10**6, vmem=VMEM_LIMIT):
    held = [pltpu.VMEM(shape, dtype) for shape, dtype in scratch]
    if copies > 0:
        held.append(pltpu.SemaphoreType.DMA((copies,)))
    return pl.pallas_call(
        kernel,
        out_shape=[jax.ShapeDtypeStruct(shape, dtype) for shape, dtype, spec in outs],
        in_specs=ins,
        out_specs=[spec for shape, dtype, spec in outs],
        scratch_shapes=held,
        compiler_params=pltpu.CompilerParams(vmem_limit_bytes=vmem),
        cost_estimate=pl.CostEstimate(flops=flops, bytes_accessed=10**6, transcendentals=0),
    )


def per_device(members, condition, observed, kernel_in, kernel_mid, kernel_out):
    members = members[0]
    core = lax.axis_index("core")
    tile = lax.axis_index(TILE)
    place = jnp.stack([lax.axis_index("member"), tile * ROWS, core]).astype(jnp.int32)
    table = jnp.asarray(lat_table())
    lat = lax.dynamic_slice_in_dim(table, tile, 1, 0)[0]
    lat = jnp.broadcast_to(lat[:, None], (FIXED_AT + ROWS, 128))
    edge = ((HALO, FIELDS, LON), F32, VMEM)
    own, edge_far, edge_near = call(
        pack_kernel, [VMEM] * 3, [((ROWS, FIELDS, LON), F32, VMEM), edge, edge]
    )(members, condition, observed)
    across = [(i, i + 1) for i in range(1, TILES - 1, 2)]
    far = lax.ppermute(edge_far, TILE, across + [(j, i) for i, j in across])
    near = lax.ppermute(edge_near, "core", [(0, 1), (1, 0)])
    near, place, lat = lax.optimization_barrier((near, place, lat))
    w_shapes = [(CH, 9 * FIELDS), (3 * CH, 3 * CH), (48, 3 * CH), (CH, 144), (3 * CH, 3 * CH)]
    w_in, w_mid, w_out, w_back_2, w_back_1 = call(
        weights_kernel,
        [VMEM] * 3,
        [(shape, BF16, VMEM) for shape in w_shapes[:3]]
        + [(shape, BF16, HBM) for shape in w_shapes[3:]],
        [(shape, F32) for shape in w_shapes] + [(shape, BF16) for shape in w_shapes[3:]],
        copies=2,
    )(kernel_in.transpose(0, 2, 1), kernel_mid, kernel_out)
    saved = [
        ((ROWS + 2, 3 * FIELDS, LON), BF16),
        ((ROWS + 2, CH, LON), BF16),
        ((ROWS, CH, LON), F32),
        ((ROWS + 2, CH, LON), BF16),
        ((ROWS + 2, CH, LON), F32),
    ]
    worked = [
        ((ROWS + 10, 3 * FIELDS, LON), BF16),
        ((ROWS + 8, CH, LON), BF16),
        ((ROWS, CH, LON), F32),
        ((ROWS + 6, CH, LON), BF16),
        ((ROWS + 2, CH, LON), F32),
    ]
    rows = FIXED_AT + HALF * ROWS
    fields_shape = ((MEMBERS, rows, LON), F32)
    kept_shape = ((4, WIDE, LON), F32)
    send, pushed, kept, stack, hidden_1, slope_1, hidden_2, slope_2 = call(
        forward_kernel,
        [SMEM] + [VMEM] * 7,
        [fields_shape + (HBM,), ((VARS, ROWS, LON), F32, VMEM), kept_shape + (HBM,)]
        + [shape + (HBM,) for shape in saved],
        [((rows, LON), F32), kept_shape] + worked + [((2 * HALO, FIELDS, LON), F32)],
        copies=MEMBERS + 6,
        flops=10**9,
    )(place, far, near, own, members, w_in, w_mid, w_out)
    fields = lax.all_to_all(send, "member", 0, 0)
    near_fields = ((MEMBERS, FIXED_AT, LON), F32)
    lat_shape = ((FIXED_AT + ROWS, 128), F32)
    (partials,) = call(
        distance_kernel,
        [SMEM] + [VMEM] * 5,
        [((MEMBERS, 128), F32, VMEM)],
        vmem=8 * 10**6,
    )(place, lat, members, observed, fields, kept)
    swap = [(0, 1), (1, 0)]
    partials = partials + lax.ppermute(partials, "core", swap)
    totals = spread(partials, "ring", RING)
    mine, theirs = call(
        backward_kernel,
        [SMEM] + [HBM] * 11,
        [((MEMBERS * CHUNK, 128), F32, VMEM)] * 2,
        [lat_shape, ((RING, MEMBERS, 128), F32), near_fields, kept_shape]
        + saved
        + [(shape, BF16) for shape in w_shapes[3:]]
        + [
            ((ROWS + 4, 48, LON), BF16),
            ((ROWS + 2, 3 * CH, LON), BF16),
            ((ROWS + 2, 3 * CH, LON), F32),
            ((48, 3 * CH), F32),
            ((3 * CH, 3 * CH), F32),
            ((9 * FIELDS, CH), F32),
            ((6 * CH, 128), F32),
        ],
        copies=11,
        flops=10**9,
    )(
        place, lat, totals, fields, kept, stack, hidden_1, slope_1, hidden_2, slope_2,
        w_back_2, w_back_1,
    )
    mine = mine + lax.ppermute(theirs, "core", swap)
    chunk = jnp.sum(lax.all_to_all(mine.reshape(MEMBERS, CHUNK, 128), "member", 0, 0), 0)
    chunk = jnp.sum(spread(chunk, "ring", RING), 0)
    other = lax.ppermute(chunk, "core", swap)
    chunks = spread(jnp.stack([chunk, other]), "member", MEMBERS)
    grad_in, grad_mid, grad_out, energy = call(
        unpack_kernel,
        [SMEM, VMEM],
        [
            ((9, INPUTS, CH), F32, VMEM),
            ((9, CH, CH), F32, VMEM),
            ((9, VARS, CH), F32, VMEM),
            ((1, 1), F32, VMEM),
        ],
        [((6 * CH, 128), F32)],
        vmem=16 * 10**6,
    )(place, chunks)
    return (pushed[None], energy[0, 0], grad_in.transpose(0, 2, 1), grad_mid, grad_out)


def solution(mesh):
    fine = Mesh(mesh.devices.reshape(MEMBERS, -1, 2), ("member",) + TILE)
    in_specs = (
        P("member", None, TILE, None),
        P(None, TILE, None),
        P(None, TILE, None),
        P(),
        P(),
        P(),
    )
    out_specs = (P("member", None, TILE, None), P(), P(), P(), P())
    return jax.shard_map(
        per_device, mesh=fine, in_specs=in_specs, out_specs=out_specs, check_vma=False
    )
```

```python
import functools
import math

import jax
import jax.numpy as jnp
import numpy as np
from jax import lax
from jax.experimental import pallas as pl
from jax.experimental.pallas import tpu as pltpu
from jax.sharding import Mesh, PartitionSpec as P

EPSILON = 1e-06
MEMBERS, NLAT, LON, ROWS = 8, 256, 512, 8
VARS, HALF, COND, CH = 6, 3, 6, 64
TILES, RING = 32, 16
ENTRIES = VARS * NLAT * LON
HALO = 5
FIELDS = 16
INPUTS = HALF + COND
WIDE = (ROWS + 4) * HALF
FIXED_AT = 40
CHUNK = 24
TILE = ("ring", "core")
F32, BF16 = jnp.float32, jnp.bfloat16


def spread(value, axes, count):
    copies = jnp.broadcast_to(value[None], (count,) + value.shape)
    return lax.all_to_all(copies, axes, 0, 0)


def lat_table():
    rows = np.arange(NLAT)
    cosine = np.cos((-90.0 + 180.0 * (rows + 0.5) / NLAT) * (np.pi / 180.0))
    lat = (cosine / cosine.mean()).astype(np.float32)
    padded = np.pad(lat, (2, 2))
    table = np.zeros((TILES, FIXED_AT + ROWS), np.float32)
    for tile in range(TILES):
        wide = padded[tile * ROWS : tile * ROWS + ROWS + 4]
        table[tile, :WIDE] = np.repeat(wide, HALF)
        table[tile, FIXED_AT:] = lat[tile * ROWS : (tile + 1) * ROWS]
    return table


def turned(value, step):
    return value if step == 0 else pltpu.roll(value, step % LON, 1)


def dot(left, right):
    return jnp.dot(left, right, preferred_element_type=F32)


def dot_cells(left, right):
    return lax.dot_general(left, right, (((1,), (1,)), ((), ())), preferred_element_type=F32)


def inside(base, row):
    row = base + row
    return jnp.where((row >= 0) & (row < NLAT), 1.0, 0.0).astype(F32)


def sigmoid(value):
    return 0.5 * jnp.tanh(0.5 * value) + 0.5


def loop(start, stop, body):
    lax.fori_loop(start, stop, lambda row, carry: (body(row), carry)[1], 0, unroll=True)


def pack_kernel(
    members_in, condition_in, observed_in, own, edge_far, edge_near,
    members, condition, observed, sems,
):
    pairs = [(members_in, members), (condition_in, condition)]
    pairs.append((observed_in.at[HALF:], observed))
    for copy in started(pairs, sems):
        copy.wait()
    for row in range(ROWS):
        own[row, :HALF, :] = members[:HALF, row, :]
        own[row, HALF:INPUTS, :] = condition[:, row, :]
        own[row, INPUTS : INPUTS + HALF, :] = members[HALF:, row, :]
        own[row, INPUTS + HALF : INPUTS + 2 * HALF, :] = observed[:, row, :]
        own[row, FIELDS - 1 :, :] = jnp.zeros((1, LON), F32)
    odd = lax.axis_index("core") == 1
    for row in range(HALO):
        initial, last = own[row], own[ROWS - HALO + row]
        edge_far[row] = jnp.where(odd, last, initial)
        edge_near[row] = jnp.where(odd, initial, last)


def weights_kernel(
    kernel_in_in, kernel_mid_in, kernel_out_in, w_in, w_mid, w_out, w_back_2, w_back_1,
    kernel_in, kernel_mid, kernel_out, flat_in, square, flat_out, back_2, back_1, held_2, held_1, sems,
):
    pairs = [(kernel_in_in, kernel_in), (kernel_mid_in, kernel_mid), (kernel_out_in, kernel_out)]
    copies = [
        pltpu.make_async_copy(source, target, sems.at[2 + at])
        for at, (source, target) in enumerate(pairs)
    ]
    for copy in copies:
        copy.start()
    flat_out[...] = jnp.zeros_like(flat_out)
    back_2[...] = jnp.zeros_like(back_2)
    for copy in copies:
        copy.wait()
    for tap in range(9):
        a, b = tap // 3, tap % 3
        back = 3 * (2 - a) + b
        first = kernel_in[tap].astype(F32)
        first = jnp.concatenate([first, jnp.zeros((FIELDS - INPUTS, CH), F32)], 0).T
        flat_in[:, tap * FIELDS : (tap + 1) * FIELDS] = first
        mid = kernel_mid[tap].astype(F32)
        square[b * CH : (b + 1) * CH, a * CH : (a + 1) * CH] = mid
        back_1[a * CH : (a + 1) * CH, b * CH : (b + 1) * CH] = mid.T
        out = kernel_out[tap].astype(F32)
        across = slice(a * CH, (a + 1) * CH)
        flat_out[b * 16 : b * 16 + HALF, across] = out[:HALF]
        flat_out[b * 16 + 8 : b * 16 + 8 + HALF, across] = out[HALF:]
        out = jnp.concatenate([out, jnp.zeros((8 - VARS, CH), F32)], 0).T
        back_2[:, back * 16 : back * 16 + HALF] = out[:, :HALF]
        back_2[:, back * 16 + 8 : back * 16 + 8 + HALF] = out[:, HALF:VARS]
    held_2[...] = back_2[...].astype(BF16)
    held_1[...] = back_1[...].astype(BF16)
    copies = [
        pltpu.make_async_copy(held_2, w_back_2, sems.at[0]),
        pltpu.make_async_copy(held_1, w_back_1, sems.at[1]),
    ]
    for copy in copies:
        copy.start()
    w_in[...] = flat_in[...].astype(BF16)
    w_mid[...] = square[...].astype(BF16)
    w_out[...] = flat_out[...].astype(BF16)
    for copy in copies:
        copy.wait()


def forward_kernel(
    place, far, near, own, members_in, w_in, w_mid, w_out,
    send_out, pushed, kept_out, stack_out, hidden_1_out, slope_1_out, hidden_2_out, slope_2_out,
    send, kept, stack, hidden_1, slope_1, hidden_2, slope_2, edges, members, sems,
):
    brought = pltpu.make_async_copy(members_in.at[:HALF], members, sems.at[MEMBERS + 6])
    brought.start()
    base = place[1]
    odd = place[2] == 1
    copies = []

    def keep(source, target):
        copy = pltpu.make_async_copy(source, target, sems.at[len(copies)])
        copy.start()
        copies.append(copy)

    for row in range(HALO):
        edges[row] = jnp.where(odd, near[row], far[row])
        edges[HALO + row] = jnp.where(odd, far[row], near[row])

    def wide(row):
        if row < HALO:
            return edges[row]
        return own[row - HALO] if row < HALO + ROWS else edges[row - ROWS]

    for row in range(ROWS + 2 * HALO):
        field = wide(row)
        for shift in range(3):
            part = turned(field, 1 - shift).astype(BF16)
            stack[row, shift * FIELDS : (shift + 1) * FIELDS, :] = part
    keep(stack.at[4:14], stack_out)

    def first(row, kept_row):
        pre = dot(w_in[...], stack[pl.ds(row, 3)].reshape(9 * FIELDS, LON))
        gate = sigmoid(pre)
        hidden_1[row] = (pre * gate * inside(base, row - 4)).astype(BF16)
        if kept_row:
            slope_1[row - 4] = gate * (1.0 + pre * (1.0 - gate))

    loop(0, 4, functools.partial(first, kept_row=False))
    loop(4, 12, functools.partial(first, kept_row=True))
    loop(12, 16, functools.partial(first, kept_row=False))
    keep(hidden_1.at[3:13], hidden_1_out)
    keep(slope_1, slope_1_out)

    def second(row, kept_row):
        part = dot(w_mid[...], hidden_1[pl.ds(row, 3)].reshape(3 * CH, LON))
        pre = turned(part[:CH], 1) + part[CH : 2 * CH] + turned(part[2 * CH :], -1)
        gate = sigmoid(pre)
        hidden_2[row] = (pre * gate * inside(base, row - 3)).astype(BF16)
        if kept_row:
            slope_2[row - 2] = gate * (1.0 + pre * (1.0 - gate))

    loop(0, 2, functools.partial(second, kept_row=False))
    loop(2, 12, functools.partial(second, kept_row=True))
    loop(12, 14, functools.partial(second, kept_row=False))
    keep(hidden_2.at[2:12], hidden_2_out)
    keep(slope_2, slope_2_out)

    brought.wait()
    send[WIDE:FIXED_AT, :] = jnp.zeros((FIXED_AT - WIDE, LON), F32)
    send[FIXED_AT:, :] = members[...].reshape(HALF * ROWS, LON)
    for row in range(ROWS + 4):
        part = dot(w_out[...], hidden_2[row : row + 3].reshape(3 * CH, LON))
        both = turned(part[:16], 1) + part[16:32] + turned(part[32:], -1)
        log_scale = jnp.tanh(both[:HALF])
        field = wide(row + 3)
        moving = field[INPUTS : INPUTS + HALF]
        moved = moving * jnp.exp(log_scale) + both[8 : 8 + HALF]
        here = slice(row * HALF, (row + 1) * HALF)
        kept[0, here, :] = log_scale
        kept[1, here, :] = moving
        kept[2, here, :] = field[INPUTS + HALF : INPUTS + 2 * HALF]
        kept[3, here, :] = moved
        send[here, :] = moved
        if 2 <= row < 2 + ROWS:
            for var in range(HALF):
                pushed[HALF + var, row - 2 : row - 1, :] = moved[var : var + 1]
    for member in range(MEMBERS):
        keep(send, send_out.at[member])
    keep(kept, kept_out)
    pushed[:HALF] = members[...]
    for copy in copies:
        copy.wait()


def folded(value):
    return sum(value[..., at : at + 128] for at in range(0, LON, 128))


def distance_kernel(place, lat, members, observed, fields, kept, partials):
    me = place[0]
    spot = lax.broadcasted_iota(jnp.int32, (WIDE, 1), 0)
    wide = jnp.where((spot >= 2 * HALF) & (spot < WIDE - 2 * HALF), lat[:WIDE, :1], 0.0)
    low = jnp.concatenate([lat[FIXED_AT:, :1]] * HALF, 0)
    fixed_mine = members[:HALF].reshape(HALF * ROWS, LON)
    mine = kept[3]

    def weighed(moved, fixed):
        upper = jnp.sum(folded(wide * (mine - moved) ** 2), 0, keepdims=True)
        lower = jnp.sum(folded(low * (fixed_mine - fixed) ** 2), 0, keepdims=True)
        return upper + lower

    to_observed = weighed(kept[2], observed[:HALF].reshape(HALF * ROWS, LON))
    rows = [weighed(fields[n, :WIDE], fields[n, FIXED_AT:]) for n in range(MEMBERS)]
    all_rows = jnp.concatenate(rows, 0)
    spot = lax.broadcasted_iota(jnp.int32, (MEMBERS, 128), 0)
    partials[...] = jnp.where(spot == me, to_observed, all_rows)


def started(pairs, sems):
    copies = [
        pltpu.make_async_copy(source, target, sems.at[at])
        for at, (source, target) in enumerate(pairs)
    ]
    for copy in copies:
        copy.start()
    return copies


def backward_kernel(
    place, lat, totals, fields_in, kept_in, stack_in, hidden_1_in, slope_1_in, hidden_2_in,
    slope_2_in, w_back_2_in, w_back_1_in,
    mine, theirs,
    fields, kept, stack, hidden_1, slope_1, hidden_2, slope_2, w_back_2, w_back_1,
    coupled, turned_2, by_row, sum_out, sum_mid, sum_in, packed, sems,
):
    sources = [kept_in, fields_in.at[:, :FIXED_AT], w_back_2_in, slope_2_in]
    sources += [w_back_1_in, hidden_1_in, hidden_2_in, slope_1_in, stack_in]
    targets = [kept, fields, w_back_2, slope_2]
    targets += [w_back_1, hidden_1, hidden_2, slope_1, stack]
    copies = started(list(zip(sources, targets)), sems)
    me, base, core = place[0], place[1], place[2]
    sum_out[...] = jnp.zeros_like(sum_out)
    sum_mid[...] = jnp.zeros_like(sum_mid)
    sum_in[...] = jnp.zeros_like(sum_in)
    total = totals[0]
    for tile in range(1, RING):
        total = total + totals[tile]
    distances = jnp.sqrt(jnp.sum(total, 1, keepdims=True) / ENTRIES + EPSILON)
    is_me = lax.broadcasted_iota(jnp.int32, (MEMBERS, 1), 0) == me
    shares = jnp.where(is_me, distances / MEMBERS, -distances / (2.0 * MEMBERS * MEMBERS))
    share = jnp.sum(shares, 0, keepdims=True) / TILES
    weights = 1.0 / (jnp.where(is_me, MEMBERS, MEMBERS * MEMBERS) * distances)
    own_weight = jnp.sum(jnp.where(is_me, weights, 0.0), 0, keepdims=True)
    weights = jnp.where(is_me, 0.0, weights)
    copies[0].wait()
    log_scale, moving, observed, moved = kept[0], kept[1], kept[2], kept[3]
    inner = (moved - observed) * own_weight
    copies[1].wait()
    for n in range(MEMBERS):
        inner = inner - weights[n : n + 1] * (moved - fields[n, :WIDE])
    upper = lat[:WIDE, :1] * inner / math.sqrt(ENTRIES)
    scaled = upper * moving * jnp.exp(log_scale) * (1.0 - log_scale * log_scale)
    blank = jnp.zeros((8 - HALF, LON), F32)
    for row in range(ROWS + 4):
        here = slice(row * HALF, (row + 1) * HALF)
        field = jnp.concatenate([scaled[here], blank, upper[here], blank], 0)
        for shift in range(3):
            part = turned(field, shift - 1).astype(BF16)
            coupled[row, shift * 16 : (shift + 1) * 16, :] = part
    copies[2].wait()
    copies[3].wait()

    def second(row):
        back = dot(w_back_2[...], coupled[pl.ds(row, 3)].reshape(144, LON))
        grad = back * slope_2[row] * inside(base, row - 1)
        for shift in range(3):
            part = turned(grad, shift - 1).astype(BF16)
            turned_2[row, shift * CH : (shift + 1) * CH, :] = part

    loop(0, ROWS + 2, second)
    copies[4].wait()

    def across_rows(row):
        by_row[row] = dot(w_back_1[...], turned_2[row])

    loop(0, ROWS + 2, across_rows)
    copies[5].wait()

    def middle(row):
        near = hidden_1[pl.ds(row, 3)].reshape(3 * CH, LON)
        sum_mid[...] += dot_cells(turned_2[row + 1], near)

    loop(0, ROWS, middle)
    copies[6].wait()

    def outer(row):
        near = hidden_2[pl.ds(row, 3)].reshape(3 * CH, LON)
        sum_out[...] += dot_cells(coupled[row + 2], near)

    loop(0, ROWS, outer)
    copies[7].wait()
    copies[8].wait()

    def last(row):
        back = by_row[row + 2, :CH] + by_row[row + 1, CH : 2 * CH] + by_row[row, 2 * CH :]
        grad = (back * slope_1[row]).astype(BF16)
        near = stack[pl.ds(row, 3)].reshape(9 * FIELDS, LON)
        sum_in[...] += dot_cells(near, grad)

    loop(0, ROWS, last)
    packed[5 * CH :, :] = jnp.zeros((CH, 128), F32)
    packed[4 * CH : 5 * CH, CH:] = jnp.zeros((CH, CH), F32)
    for tap in range(9):
        a, b = tap // 3, tap % 3
        at, side = place_mid(tap)
        packed[at : at + CH, side] = sum_mid[b * CH : (b + 1) * CH, a * CH : (a + 1) * CH]
        at = 5 * CH + tap * VARS
        across = slice(a * CH, (a + 1) * CH)
        packed[at : at + HALF, :CH] = sum_out[b * 16 : b * 16 + HALF, across]
        packed[at + HALF : at + VARS, :CH] = sum_out[b * 16 + 8 : b * 16 + 8 + HALF, across]
        at = 4 * CH + tap * INPUTS
        packed[at : at + INPUTS, CH:] = sum_in[tap * FIELDS : tap * FIELDS + INPUTS]
    packed[6 * CH - 1 :, 127:] = share
    half = MEMBERS * CHUNK
    for copy in range(2):

        @pl.when(core == copy)
        def _():
            mine[...] = packed[copy * half : (copy + 1) * half, :]
            theirs[...] = packed[(1 - copy) * half : (2 - copy) * half, :]


def place_mid(tap):
    return (tap * CH, slice(0, CH)) if tap < 5 else ((tap - 5) * CH, slice(CH, 2 * CH))


def unpack_kernel(place, chunks, grad_in, grad_mid, grad_out, energy, packed):
    core = place[2]
    for member in range(MEMBERS):
        first, second = chunks[member, 0], chunks[member, 1]
        at = member * CHUNK
        packed[at : at + CHUNK, :] = jnp.where(core == 0, first, second)
        at += MEMBERS * CHUNK
        packed[at : at + CHUNK, :] = jnp.where(core == 0, second, first)
    for tap in range(9):
        at, side = place_mid(tap)
        grad_mid[tap] = packed[at : at + CH, side]
        at = 5 * CH + tap * VARS
        grad_out[tap] = packed[at : at + VARS, :CH]
        at = 4 * CH + tap * INPUTS
        grad_in[tap] = packed[at : at + INPUTS, CH:]
    energy[...] = packed[6 * CH - 1 :, 127:]


VMEM_LIMIT = 28 * 10**6
VMEM = pl.BlockSpec(memory_space=pltpu.VMEM)
HBM = pl.BlockSpec(memory_space=pltpu.HBM)
SMEM = pl.BlockSpec(memory_space=pltpu.SMEM)


def call(kernel, ins, outs, scratch=(), copies=0, flops=10**6, vmem=VMEM_LIMIT):
    held = [pltpu.VMEM(shape, dtype) for shape, dtype in scratch]
    if copies > 0:
        held.append(pltpu.SemaphoreType.DMA((copies,)))
    shapes = [
        pltpu.HBM(shape, dtype) if spec is HBM else jax.ShapeDtypeStruct(shape, dtype)
        for shape, dtype, spec in outs
    ]
    run = pl.pallas_call(
        kernel,
        out_shape=shapes,
        in_specs=ins,
        out_specs=[spec for shape, dtype, spec in outs],
        scratch_shapes=held,
        compiler_params=pltpu.CompilerParams(vmem_limit_bytes=vmem),
        cost_estimate=pl.CostEstimate(flops=flops, bytes_accessed=10**6, transcendentals=0),
    )

    def placed(*arrays):
        return run(
            *[
                pltpu.with_memory_space_constraint(array, pltpu.HBM) if spec is HBM else array
                for array, spec in zip(arrays, ins)
            ]
        )

    return placed


def per_device(members, condition, observed, kernel_in, kernel_mid, kernel_out):
    members = members[0]
    core = lax.axis_index("core")
    tile = lax.axis_index(TILE)
    place = jnp.stack([lax.axis_index("member"), tile * ROWS, core]).astype(jnp.int32)
    table = jnp.asarray(lat_table())
    lat = lax.dynamic_slice_in_dim(table, tile, 1, 0)[0]
    lat = jnp.broadcast_to(lat[:, None], (FIXED_AT + ROWS, 128))
    edge = ((HALO, FIELDS, LON), F32, VMEM)
    own, edge_far, edge_near = call(
        pack_kernel,
        [HBM] * 3,
        [((ROWS, FIELDS, LON), F32, VMEM), edge, edge],
        [((VARS, ROWS, LON), F32), ((COND, ROWS, LON), F32), ((HALF, ROWS, LON), F32)],
        copies=3,
    )(members, condition, observed)
    across = [(i, i + 1) for i in range(1, TILES - 1, 2)]
    far = lax.ppermute(edge_far, TILE, across + [(j, i) for i, j in across])
    near = lax.ppermute(edge_near, "core", [(0, 1), (1, 0)])
    near, place, lat = lax.optimization_barrier((near, place, lat))
    w_shapes = [(CH, 9 * FIELDS), (3 * CH, 3 * CH), (48, 3 * CH), (CH, 144), (3 * CH, 3 * CH)]
    w_in, w_mid, w_out, w_back_2, w_back_1 = call(
        weights_kernel,
        [HBM] * 3,
        [(shape, BF16, VMEM) for shape in w_shapes[:3]]
        + [(shape, BF16, HBM) for shape in w_shapes[3:]],
        [((9, INPUTS, CH), BF16), ((9, CH, CH), BF16), ((9, VARS, CH), BF16)]
        + [(shape, F32) for shape in w_shapes]
        + [(shape, BF16) for shape in w_shapes[3:]],
        copies=5,
    )(kernel_in.transpose(0, 2, 1), kernel_mid, kernel_out)
    saved = [
        ((ROWS + 2, 3 * FIELDS, LON), BF16),
        ((ROWS + 2, CH, LON), BF16),
        ((ROWS, CH, LON), F32),
        ((ROWS + 2, CH, LON), BF16),
        ((ROWS + 2, CH, LON), F32),
    ]
    worked = [
        ((ROWS + 10, 3 * FIELDS, LON), BF16),
        ((ROWS + 8, CH, LON), BF16),
        ((ROWS, CH, LON), F32),
        ((ROWS + 6, CH, LON), BF16),
        ((ROWS + 2, CH, LON), F32),
    ]
    rows = FIXED_AT + HALF * ROWS
    fields_shape = ((MEMBERS, rows, LON), F32)
    kept_shape = ((4, WIDE, LON), F32)
    send, pushed, kept, stack, hidden_1, slope_1, hidden_2, slope_2 = call(
        forward_kernel,
        [SMEM] + [VMEM] * 3 + [HBM] + [VMEM] * 3,
        [fields_shape + (HBM,), ((VARS, ROWS, LON), F32, VMEM), kept_shape + (HBM,)]
        + [shape + (HBM,) for shape in saved],
        [((rows, LON), F32), kept_shape] + worked
        + [((2 * HALO, FIELDS, LON), F32), ((HALF, ROWS, LON), F32)],
        copies=MEMBERS + 7,
        flops=10**9,
    )(place, far, near, own, members, w_in, w_mid, w_out)
    fields = lax.all_to_all(send, "member", 0, 0)
    near_fields = ((MEMBERS, FIXED_AT, LON), F32)
    (partials,) = call(
        distance_kernel,
        [SMEM] + [VMEM] * 5,
        [((MEMBERS, 128), F32, VMEM)],
        vmem=8 * 10**6,
    )(place, lat, members, observed, fields, kept)
    swap = [(0, 1), (1, 0)]
    partials = partials + lax.ppermute(partials, "core", swap)
    totals = spread(partials, "ring", RING)
    mine, theirs = call(
        backward_kernel,
        [SMEM] + [VMEM] * 2 + [HBM] * 9,
        [((MEMBERS * CHUNK, 128), F32, VMEM)] * 2,
        [near_fields, kept_shape]
        + saved
        + [(shape, BF16) for shape in w_shapes[3:]]
        + [
            ((ROWS + 4, 48, LON), BF16),
            ((ROWS + 2, 3 * CH, LON), BF16),
            ((ROWS + 2, 3 * CH, LON), F32),
            ((48, 3 * CH), F32),
            ((3 * CH, 3 * CH), F32),
            ((9 * FIELDS, CH), F32),
            ((6 * CH, 128), F32),
        ],
        copies=9,
        flops=10**9,
    )(
        place, lat, totals, fields, kept, stack, hidden_1, slope_1, hidden_2, slope_2,
        w_back_2, w_back_1,
    )
    mine = mine + lax.ppermute(theirs, "core", swap)
    chunk = jnp.sum(lax.all_to_all(mine.reshape(MEMBERS, CHUNK, 128), "member", 0, 0), 0)
    chunk = jnp.sum(spread(chunk, "ring", RING), 0)
    other = lax.ppermute(chunk, "core", swap)
    chunks = spread(jnp.stack([chunk, other]), "member", MEMBERS)
    grad_in, grad_mid, grad_out, energy = call(
        unpack_kernel,
        [SMEM, VMEM],
        [
            ((9, INPUTS, CH), F32, VMEM),
            ((9, CH, CH), F32, VMEM),
            ((9, VARS, CH), F32, VMEM),
            ((1, 1), F32, VMEM),
        ],
        [((6 * CH, 128), F32)],
        vmem=16 * 10**6,
    )(place, chunks)
    return (pushed[None], energy[0, 0], grad_in.transpose(0, 2, 1), grad_mid, grad_out)


def solution(mesh):
    fine = Mesh(mesh.devices.reshape(MEMBERS, -1, 2), ("member",) + TILE)
    in_specs = (
        P("member", None, TILE, None),
        P(None, TILE, None),
        P(None, TILE, None),
        P(),
        P(),
        P(),
    )
    out_specs = (P("member", None, TILE, None), P(), P(), P(), P())
    return jax.shard_map(
        per_device, mesh=fine, in_specs=in_specs, out_specs=out_specs, check_vma=False
    )
```

```python
import functools
import math

import jax
import jax.numpy as jnp
import numpy as np
from jax import lax
from jax.experimental import pallas as pl
from jax.experimental.pallas import tpu as pltpu
from jax.sharding import Mesh, PartitionSpec as P

EPSILON = 1e-06
MEMBERS, NLAT, LON, ROWS = 8, 256, 512, 8
VARS, HALF, COND, CH = 6, 3, 6, 64
TILES, RING = 32, 16
ENTRIES = VARS * NLAT * LON
HALO = 5
FIELDS = 16
INPUTS = HALF + COND
WIDE = (ROWS + 4) * HALF
FIXED_AT = 40
CHUNK = 24
TILE = ("ring", "core")
F32, BF16 = jnp.float32, jnp.bfloat16


def spread(value, axes, count):
    copies = jnp.broadcast_to(value[None], (count,) + value.shape)
    return lax.all_to_all(copies, axes, 0, 0)


def lat_table():
    rows = np.arange(NLAT)
    cosine = np.cos((-90.0 + 180.0 * (rows + 0.5) / NLAT) * (np.pi / 180.0))
    lat = (cosine / cosine.mean()).astype(np.float32)
    padded = np.pad(lat, (2, 2))
    table = np.zeros((TILES, FIXED_AT + ROWS), np.float32)
    for tile in range(TILES):
        wide = padded[tile * ROWS : tile * ROWS + ROWS + 4]
        table[tile, :WIDE] = np.repeat(wide, HALF)
        table[tile, FIXED_AT:] = lat[tile * ROWS : (tile + 1) * ROWS]
    return table


def turned(value, step):
    return value if step == 0 else pltpu.roll(value, step % LON, 1)


def dot(left, right):
    return jnp.dot(left, right, preferred_element_type=F32)


def dot_cells(left, right):
    return lax.dot_general(left, right, (((1,), (1,)), ((), ())), preferred_element_type=F32)


def inside(base, row):
    row = base + row
    return jnp.where((row >= 0) & (row < NLAT), 1.0, 0.0).astype(F32)


def sigmoid(value):
    return 0.5 * jnp.tanh(0.5 * value) + 0.5


def loop(start, stop, body):
    lax.fori_loop(start, stop, lambda row, carry: (body(row), carry)[1], 0, unroll=True)


def pack_kernel(
    members_in, condition_in, observed_in, own, edge_far, edge_near,
    members, condition, observed, sems,
):
    pairs = [(members_in, members), (condition_in, condition)]
    pairs.append((observed_in.at[HALF:], observed))
    for copy in started(pairs, sems):
        copy.wait()
    for row in range(ROWS):
        own[row, :HALF, :] = members[:HALF, row, :]
        own[row, HALF:INPUTS, :] = condition[:, row, :]
        own[row, INPUTS : INPUTS + HALF, :] = members[HALF:, row, :]
        own[row, INPUTS + HALF : INPUTS + 2 * HALF, :] = observed[:, row, :]
        own[row, FIELDS - 1 :, :] = jnp.zeros((1, LON), F32)
    odd = lax.axis_index("core") == 1
    for row in range(HALO):
        initial, last = own[row], own[ROWS - HALO + row]
        edge_far[row] = jnp.where(odd, last, initial)
        edge_near[row] = jnp.where(odd, initial, last)


def weights_kernel(
    kernel_in_in, kernel_mid_in, kernel_out_in, w_in, w_mid, w_out, w_back_2, w_back_1,
    kernel_in, kernel_mid, kernel_out, flat_in, square, flat_out, back_2, back_1, held_2, held_1, sems,
):
    pairs = [(kernel_in_in, kernel_in), (kernel_mid_in, kernel_mid), (kernel_out_in, kernel_out)]
    copies = [
        pltpu.make_async_copy(source, target, sems.at[2 + at])
        for at, (source, target) in enumerate(pairs)
    ]
    for copy in copies:
        copy.start()
    flat_out[...] = jnp.zeros_like(flat_out)
    back_2[...] = jnp.zeros_like(back_2)
    for copy in copies:
        copy.wait()
    for tap in range(9):
        a, b = tap // 3, tap % 3
        back = 3 * (2 - a) + b
        first = kernel_in[tap].astype(F32)
        first = jnp.concatenate([first, jnp.zeros((FIELDS - INPUTS, CH), F32)], 0).T
        flat_in[:, tap * FIELDS : (tap + 1) * FIELDS] = first
        mid = kernel_mid[tap].astype(F32)
        square[b * CH : (b + 1) * CH, a * CH : (a + 1) * CH] = mid
        back_1[a * CH : (a + 1) * CH, b * CH : (b + 1) * CH] = mid.T
        out = kernel_out[tap].astype(F32)
        across = slice(a * CH, (a + 1) * CH)
        flat_out[b * 16 : b * 16 + HALF, across] = out[:HALF]
        flat_out[b * 16 + 8 : b * 16 + 8 + HALF, across] = out[HALF:]
        out = jnp.concatenate([out, jnp.zeros((8 - VARS, CH), F32)], 0).T
        back_2[:, back * 16 : back * 16 + HALF] = out[:, :HALF]
        back_2[:, back * 16 + 8 : back * 16 + 8 + HALF] = out[:, HALF:VARS]
    held_2[...] = back_2[...].astype(BF16)
    held_1[...] = back_1[...].astype(BF16)
    copies = [
        pltpu.make_async_copy(held_2, w_back_2, sems.at[0]),
        pltpu.make_async_copy(held_1, w_back_1, sems.at[1]),
    ]
    for copy in copies:
        copy.start()
    w_in[...] = flat_in[...].astype(BF16)
    w_mid[...] = square[...].astype(BF16)
    w_out[...] = flat_out[...].astype(BF16)
    for copy in copies:
        copy.wait()


def forward_kernel(
    place, far, near, own, members_in, w_in, w_mid, w_out,
    send, pushed, kept_out, stack_out, hidden_1_out, slope_1_out, hidden_2_out, slope_2_out,
    kept, stack, hidden_1, slope_1, hidden_2, slope_2, edges, members, sems,
):
    brought = pltpu.make_async_copy(members_in.at[:HALF], members, sems.at[6])
    brought.start()
    base = place[1]
    odd = place[2] == 1
    copies = []

    def keep(source, target):
        copy = pltpu.make_async_copy(source, target, sems.at[len(copies)])
        copy.start()
        copies.append(copy)

    for row in range(HALO):
        edges[row] = jnp.where(odd, near[row], far[row])
        edges[HALO + row] = jnp.where(odd, far[row], near[row])

    def wide(row):
        if row < HALO:
            return edges[row]
        return own[row - HALO] if row < HALO + ROWS else edges[row - ROWS]

    for row in range(ROWS + 2 * HALO):
        field = wide(row)
        for shift in range(3):
            part = turned(field, 1 - shift).astype(BF16)
            stack[row, shift * FIELDS : (shift + 1) * FIELDS, :] = part
    keep(stack.at[4:14], stack_out)

    def first(row, kept_row):
        pre = dot(w_in[...], stack[pl.ds(row, 3)].reshape(9 * FIELDS, LON))
        gate = sigmoid(pre)
        hidden_1[row] = (pre * gate * inside(base, row - 4)).astype(BF16)
        if kept_row:
            slope_1[row - 4] = gate * (1.0 + pre * (1.0 - gate))

    loop(0, 4, functools.partial(first, kept_row=False))
    loop(4, 12, functools.partial(first, kept_row=True))
    loop(12, 16, functools.partial(first, kept_row=False))
    keep(hidden_1.at[3:13], hidden_1_out)
    keep(slope_1, slope_1_out)

    def second(row, kept_row):
        part = dot(w_mid[...], hidden_1[pl.ds(row, 3)].reshape(3 * CH, LON))
        pre = turned(part[:CH], 1) + part[CH : 2 * CH] + turned(part[2 * CH :], -1)
        gate = sigmoid(pre)
        hidden_2[row] = (pre * gate * inside(base, row - 3)).astype(BF16)
        if kept_row:
            slope_2[row - 2] = gate * (1.0 + pre * (1.0 - gate))

    loop(0, 2, functools.partial(second, kept_row=False))
    loop(2, 12, functools.partial(second, kept_row=True))
    loop(12, 14, functools.partial(second, kept_row=False))
    keep(hidden_2.at[2:12], hidden_2_out)
    keep(slope_2, slope_2_out)

    brought.wait()
    send[WIDE:FIXED_AT, :] = jnp.zeros((FIXED_AT - WIDE, LON), F32)
    send[FIXED_AT:, :] = members[...].reshape(HALF * ROWS, LON)
    for row in range(ROWS + 4):
        part = dot(w_out[...], hidden_2[row : row + 3].reshape(3 * CH, LON))
        both = turned(part[:16], 1) + part[16:32] + turned(part[32:], -1)
        log_scale = jnp.tanh(both[:HALF])
        field = wide(row + 3)
        moving = field[INPUTS : INPUTS + HALF]
        moved = moving * jnp.exp(log_scale) + both[8 : 8 + HALF]
        here = slice(row * HALF, (row + 1) * HALF)
        kept[0, here, :] = log_scale
        kept[1, here, :] = moving
        kept[2, here, :] = field[INPUTS + HALF : INPUTS + 2 * HALF]
        kept[3, here, :] = moved
        send[here, :] = moved
        if 2 <= row < 2 + ROWS:
            for var in range(HALF):
                pushed[HALF + var, row - 2 : row - 1, :] = moved[var : var + 1]
    keep(kept, kept_out)
    pushed[:HALF] = members[...]
    for copy in copies:
        copy.wait()


def folded(value):
    return sum(value[..., at : at + 128] for at in range(0, LON, 128))


def distance_kernel(place, lat, members, observed, fields, kept, partials):
    me = place[0]
    spot = lax.broadcasted_iota(jnp.int32, (WIDE, 1), 0)
    wide = jnp.where((spot >= 2 * HALF) & (spot < WIDE - 2 * HALF), lat[:WIDE, :1], 0.0)
    low = jnp.concatenate([lat[FIXED_AT:, :1]] * HALF, 0)
    fixed_mine = members[:HALF].reshape(HALF * ROWS, LON)
    mine = kept[3]

    def weighed(moved, fixed):
        upper = jnp.sum(folded(wide * (mine - moved) ** 2), 0, keepdims=True)
        lower = jnp.sum(folded(low * (fixed_mine - fixed) ** 2), 0, keepdims=True)
        return upper + lower

    to_observed = weighed(kept[2], observed[:HALF].reshape(HALF * ROWS, LON))
    rows = [weighed(fields[n, :WIDE], fields[n, FIXED_AT:]) for n in range(MEMBERS)]
    all_rows = jnp.concatenate(rows, 0)
    spot = lax.broadcasted_iota(jnp.int32, (MEMBERS, 128), 0)
    partials[...] = jnp.where(spot == me, to_observed, all_rows)


def started(pairs, sems):
    copies = [
        pltpu.make_async_copy(source, target, sems.at[at])
        for at, (source, target) in enumerate(pairs)
    ]
    for copy in copies:
        copy.start()
    return copies


def backward_kernel(
    place, lat, totals, fields_in, kept_in, stack_in, hidden_1_in, slope_1_in, hidden_2_in,
    slope_2_in, w_back_2_in, w_back_1_in,
    mine, theirs,
    fields, kept, stack, hidden_1, slope_1, hidden_2, slope_2, w_back_2, w_back_1,
    coupled, turned_2, by_row, sum_out, sum_mid, sum_in, packed, sems,
):
    sources = [kept_in, fields_in.at[:, :FIXED_AT], w_back_2_in, slope_2_in]
    sources += [w_back_1_in, hidden_1_in, hidden_2_in, slope_1_in, stack_in]
    targets = [kept, fields, w_back_2, slope_2]
    targets += [w_back_1, hidden_1, hidden_2, slope_1, stack]
    copies = started(list(zip(sources, targets)), sems)
    me, base, core = place[0], place[1], place[2]
    sum_out[...] = jnp.zeros_like(sum_out)
    sum_mid[...] = jnp.zeros_like(sum_mid)
    sum_in[...] = jnp.zeros_like(sum_in)
    total = totals[0]
    for tile in range(1, RING):
        total = total + totals[tile]
    distances = jnp.sqrt(jnp.sum(total, 1, keepdims=True) / ENTRIES + EPSILON)
    is_me = lax.broadcasted_iota(jnp.int32, (MEMBERS, 1), 0) == me
    shares = jnp.where(is_me, distances / MEMBERS, -distances / (2.0 * MEMBERS * MEMBERS))
    share = jnp.sum(shares, 0, keepdims=True) / TILES
    weights = 1.0 / (jnp.where(is_me, MEMBERS, MEMBERS * MEMBERS) * distances)
    own_weight = jnp.sum(jnp.where(is_me, weights, 0.0), 0, keepdims=True)
    weights = jnp.where(is_me, 0.0, weights)
    copies[0].wait()
    log_scale, moving, observed, moved = kept[0], kept[1], kept[2], kept[3]
    inner = (moved - observed) * own_weight
    copies[1].wait()
    for n in range(MEMBERS):
        inner = inner - weights[n : n + 1] * (moved - fields[n, :WIDE])
    upper = lat[:WIDE, :1] * inner / math.sqrt(ENTRIES)
    scaled = upper * moving * jnp.exp(log_scale) * (1.0 - log_scale * log_scale)
    blank = jnp.zeros((8 - HALF, LON), F32)
    for row in range(ROWS + 4):
        here = slice(row * HALF, (row + 1) * HALF)
        field = jnp.concatenate([scaled[here], blank, upper[here], blank], 0)
        for shift in range(3):
            part = turned(field, shift - 1).astype(BF16)
            coupled[row, shift * 16 : (shift + 1) * 16, :] = part
    copies[2].wait()
    copies[3].wait()

    def second(row):
        back = dot(w_back_2[...], coupled[pl.ds(row, 3)].reshape(144, LON))
        grad = back * slope_2[row] * inside(base, row - 1)
        for shift in range(3):
            part = turned(grad, shift - 1).astype(BF16)
            turned_2[row, shift * CH : (shift + 1) * CH, :] = part

    loop(0, ROWS + 2, second)
    copies[4].wait()

    def across_rows(row):
        by_row[row] = dot(w_back_1[...], turned_2[row])

    loop(0, ROWS + 2, across_rows)
    copies[5].wait()

    def middle(row):
        near = hidden_1[pl.ds(row, 3)].reshape(3 * CH, LON)
        sum_mid[...] += dot_cells(turned_2[row + 1], near)

    loop(0, ROWS, middle)
    copies[6].wait()

    def outer(row):
        near = hidden_2[pl.ds(row, 3)].reshape(3 * CH, LON)
        sum_out[...] += dot_cells(coupled[row + 2], near)

    loop(0, ROWS, outer)
    copies[7].wait()
    copies[8].wait()

    def last(row):
        back = by_row[row + 2, :CH] + by_row[row + 1, CH : 2 * CH] + by_row[row, 2 * CH :]
        grad = (back * slope_1[row]).astype(BF16)
        near = stack[pl.ds(row, 3)].reshape(9 * FIELDS, LON)
        sum_in[...] += dot_cells(near, grad)

    loop(0, ROWS, last)
    packed[5 * CH :, :] = jnp.zeros((CH, 128), F32)
    packed[4 * CH : 5 * CH, CH:] = jnp.zeros((CH, CH), F32)
    for tap in range(9):
        a, b = tap // 3, tap % 3
        at, side = place_mid(tap)
        packed[at : at + CH, side] = sum_mid[b * CH : (b + 1) * CH, a * CH : (a + 1) * CH]
        at = 5 * CH + tap * VARS
        across = slice(a * CH, (a + 1) * CH)
        packed[at : at + HALF, :CH] = sum_out[b * 16 : b * 16 + HALF, across]
        packed[at + HALF : at + VARS, :CH] = sum_out[b * 16 + 8 : b * 16 + 8 + HALF, across]
        at = 4 * CH + tap * INPUTS
        packed[at : at + INPUTS, CH:] = sum_in[tap * FIELDS : tap * FIELDS + INPUTS]
    packed[6 * CH - 1 :, 127:] = share
    half = MEMBERS * CHUNK
    for copy in range(2):

        @pl.when(core == copy)
        def _():
            mine[...] = packed[copy * half : (copy + 1) * half, :]
            theirs[...] = packed[(1 - copy) * half : (2 - copy) * half, :]


def place_mid(tap):
    return (tap * CH, slice(0, CH)) if tap < 5 else ((tap - 5) * CH, slice(CH, 2 * CH))


def unpack_kernel(place, chunks, grad_in, grad_mid, grad_out, energy, packed):
    core = place[2]
    for member in range(MEMBERS):
        first, second = chunks[member, 0], chunks[member, 1]
        at = member * CHUNK
        packed[at : at + CHUNK, :] = jnp.where(core == 0, first, second)
        at += MEMBERS * CHUNK
        packed[at : at + CHUNK, :] = jnp.where(core == 0, second, first)
    for tap in range(9):
        at, side = place_mid(tap)
        grad_mid[tap] = packed[at : at + CH, side]
        at = 5 * CH + tap * VARS
        grad_out[tap] = packed[at : at + VARS, :CH]
        at = 4 * CH + tap * INPUTS
        grad_in[tap] = packed[at : at + INPUTS, CH:]
    energy[...] = packed[6 * CH - 1 :, 127:]


VMEM_LIMIT = 28 * 10**6
VMEM = pl.BlockSpec(memory_space=pltpu.VMEM)
HBM = pl.BlockSpec(memory_space=pltpu.HBM)
SMEM = pl.BlockSpec(memory_space=pltpu.SMEM)


def call(kernel, ins, outs, scratch=(), copies=0, flops=10**6, vmem=VMEM_LIMIT):
    held = [pltpu.VMEM(shape, dtype) for shape, dtype in scratch]
    if copies > 0:
        held.append(pltpu.SemaphoreType.DMA((copies,)))
    shapes = [
        pltpu.HBM(shape, dtype) if spec is HBM else jax.ShapeDtypeStruct(shape, dtype)
        for shape, dtype, spec in outs
    ]
    run = pl.pallas_call(
        kernel,
        out_shape=shapes,
        in_specs=ins,
        out_specs=[spec for shape, dtype, spec in outs],
        scratch_shapes=held,
        compiler_params=pltpu.CompilerParams(vmem_limit_bytes=vmem),
        cost_estimate=pl.CostEstimate(flops=flops, bytes_accessed=10**6, transcendentals=0),
    )

    def placed(*arrays):
        return run(
            *[
                pltpu.with_memory_space_constraint(array, pltpu.HBM) if spec is HBM else array
                for array, spec in zip(arrays, ins)
            ]
        )

    return placed


def per_device(members, condition, observed, kernel_in, kernel_mid, kernel_out):
    members = members[0]
    core = lax.axis_index("core")
    tile = lax.axis_index(TILE)
    place = jnp.stack([lax.axis_index("member"), tile * ROWS, core]).astype(jnp.int32)
    table = jnp.asarray(lat_table())
    lat = lax.dynamic_slice_in_dim(table, tile, 1, 0)[0]
    lat = jnp.broadcast_to(lat[:, None], (FIXED_AT + ROWS, 128))
    edge = ((HALO, FIELDS, LON), F32, VMEM)
    own, edge_far, edge_near = call(
        pack_kernel,
        [HBM] * 3,
        [((ROWS, FIELDS, LON), F32, VMEM), edge, edge],
        [((VARS, ROWS, LON), F32), ((COND, ROWS, LON), F32), ((HALF, ROWS, LON), F32)],
        copies=3,
    )(members, condition, observed)
    across = [(i, i + 1) for i in range(1, TILES - 1, 2)]
    far = lax.ppermute(edge_far, TILE, across + [(j, i) for i, j in across])
    near = lax.ppermute(edge_near, "core", [(0, 1), (1, 0)])
    near, place, lat = lax.optimization_barrier((near, place, lat))
    w_shapes = [(CH, 9 * FIELDS), (3 * CH, 3 * CH), (48, 3 * CH), (CH, 144), (3 * CH, 3 * CH)]
    w_in, w_mid, w_out, w_back_2, w_back_1 = call(
        weights_kernel,
        [HBM] * 3,
        [(shape, BF16, VMEM) for shape in w_shapes[:3]]
        + [(shape, BF16, HBM) for shape in w_shapes[3:]],
        [((9, INPUTS, CH), BF16), ((9, CH, CH), BF16), ((9, VARS, CH), BF16)]
        + [(shape, F32) for shape in w_shapes]
        + [(shape, BF16) for shape in w_shapes[3:]],
        copies=5,
    )(kernel_in.transpose(0, 2, 1), kernel_mid, kernel_out)
    saved = [
        ((ROWS + 2, 3 * FIELDS, LON), BF16),
        ((ROWS + 2, CH, LON), BF16),
        ((ROWS, CH, LON), F32),
        ((ROWS + 2, CH, LON), BF16),
        ((ROWS + 2, CH, LON), F32),
    ]
    worked = [
        ((ROWS + 10, 3 * FIELDS, LON), BF16),
        ((ROWS + 8, CH, LON), BF16),
        ((ROWS, CH, LON), F32),
        ((ROWS + 6, CH, LON), BF16),
        ((ROWS + 2, CH, LON), F32),
    ]
    rows = FIXED_AT + HALF * ROWS
    kept_shape = ((4, WIDE, LON), F32)
    send, pushed, kept, stack, hidden_1, slope_1, hidden_2, slope_2 = call(
        forward_kernel,
        [SMEM] + [VMEM] * 3 + [HBM] + [VMEM] * 3,
        [((rows, LON), F32, VMEM), ((VARS, ROWS, LON), F32, VMEM), kept_shape + (HBM,)]
        + [shape + (HBM,) for shape in saved],
        [kept_shape] + worked
        + [((2 * HALO, FIELDS, LON), F32), ((HALF, ROWS, LON), F32)],
        copies=7,
        flops=10**9,
    )(place, far, near, own, members, w_in, w_mid, w_out)
    fields = spread(send, "member", MEMBERS)
    near_fields = ((MEMBERS, FIXED_AT, LON), F32)
    (partials,) = call(
        distance_kernel,
        [SMEM] + [VMEM] * 5,
        [((MEMBERS, 128), F32, VMEM)],
        vmem=8 * 10**6,
    )(place, lat, members, observed, fields, kept)
    swap = [(0, 1), (1, 0)]
    partials = partials + lax.ppermute(partials, "core", swap)
    totals = spread(partials, "ring", RING)
    mine, theirs = call(
        backward_kernel,
        [SMEM] + [VMEM] * 2 + [HBM] * 9,
        [((MEMBERS * CHUNK, 128), F32, VMEM)] * 2,
        [near_fields, kept_shape]
        + saved
        + [(shape, BF16) for shape in w_shapes[3:]]
        + [
            ((ROWS + 4, 48, LON), BF16),
            ((ROWS + 2, 3 * CH, LON), BF16),
            ((ROWS + 2, 3 * CH, LON), F32),
            ((48, 3 * CH), F32),
            ((3 * CH, 3 * CH), F32),
            ((9 * FIELDS, CH), F32),
            ((6 * CH, 128), F32),
        ],
        copies=9,
        flops=10**9,
    )(
        place, lat, totals, fields, kept, stack, hidden_1, slope_1, hidden_2, slope_2,
        w_back_2, w_back_1,
    )
    mine = mine + lax.ppermute(theirs, "core", swap)
    chunk = jnp.sum(lax.all_to_all(mine.reshape(MEMBERS, CHUNK, 128), "member", 0, 0), 0)
    chunk = jnp.sum(spread(chunk, "ring", RING), 0)
    other = lax.ppermute(chunk, "core", swap)
    chunks = spread(jnp.stack([chunk, other]), "member", MEMBERS)
    grad_in, grad_mid, grad_out, energy = call(
        unpack_kernel,
        [SMEM, VMEM],
        [
            ((9, INPUTS, CH), F32, VMEM),
            ((9, CH, CH), F32, VMEM),
            ((9, VARS, CH), F32, VMEM),
            ((1, 1), F32, VMEM),
        ],
        [((6 * CH, 128), F32)],
        vmem=16 * 10**6,
    )(place, chunks)
    return (pushed[None], energy[0, 0], grad_in.transpose(0, 2, 1), grad_mid, grad_out)


def solution(mesh):
    fine = Mesh(mesh.devices.reshape(MEMBERS, -1, 2), ("member",) + TILE)
    in_specs = (
        P("member", None, TILE, None),
        P(None, TILE, None),
        P(None, TILE, None),
        P(),
        P(),
        P(),
    )
    out_specs = (P("member", None, TILE, None), P(), P(), P(), P())
    return jax.shard_map(
        per_device, mesh=fine, in_specs=in_specs, out_specs=out_specs, check_vma=False
    )
```

```python
import functools
import math

import jax
import jax.numpy as jnp
import numpy as np
from jax import lax
from jax.experimental import pallas as pl
from jax.experimental.pallas import tpu as pltpu
from jax.sharding import Mesh, PartitionSpec as P

EPSILON = 1e-06
MEMBERS, NLAT, LON, ROWS = 8, 256, 512, 8
VARS, HALF, COND, CH = 6, 3, 6, 64
TILES, RING = 32, 16
ENTRIES = VARS * NLAT * LON
HALO = 5
FIELDS = 16
INPUTS = HALF + COND
WIDE = (ROWS + 4) * HALF
LAT_AT = 40
OWN = ROWS * HALF
FAR_AT = 2 * OWN
NEAR = 2 * HALF
SENT = 56
CHUNK = 24
TILE = ("ring", "core")
F32, BF16 = jnp.float32, jnp.bfloat16


def spread(value, axes, count):
    copies = jnp.broadcast_to(value[None], (count,) + value.shape)
    return lax.all_to_all(copies, axes, 0, 0)


def lat_table():
    rows = np.arange(NLAT)
    cosine = np.cos((-90.0 + 180.0 * (rows + 0.5) / NLAT) * (np.pi / 180.0))
    lat = (cosine / cosine.mean()).astype(np.float32)
    padded = np.pad(lat, (2, 2))
    table = np.zeros((TILES, LAT_AT + ROWS), np.float32)
    for tile in range(TILES):
        wide = padded[tile * ROWS : tile * ROWS + ROWS + 4]
        table[tile, :WIDE] = np.repeat(wide, HALF)
        table[tile, LAT_AT:] = lat[tile * ROWS : (tile + 1) * ROWS]
    return table


def turned(value, step):
    return value if step == 0 else pltpu.roll(value, step % LON, 1)


def dot(left, right):
    return jnp.dot(left, right, preferred_element_type=F32)


def dot_cells(left, right):
    return lax.dot_general(left, right, (((1,), (1,)), ((), ())), preferred_element_type=F32)


def inside(base, row):
    row = base + row
    return jnp.where((row >= 0) & (row < NLAT), 1.0, 0.0).astype(F32)


def sigmoid(value):
    return 0.5 * jnp.tanh(0.5 * value) + 0.5


def loop(start, stop, body):
    lax.fori_loop(start, stop, lambda row, carry: (body(row), carry)[1], 0, unroll=True)


def pack_kernel(
    members_in, condition_in, observed_in, own, edge_far, edge_near,
    members, condition, observed, sems,
):
    pairs = [(members_in, members), (condition_in, condition)]
    pairs.append((observed_in.at[HALF:], observed))
    for copy in started(pairs, sems):
        copy.wait()
    for row in range(ROWS):
        own[row, :HALF, :] = members[:HALF, row, :]
        own[row, HALF:INPUTS, :] = condition[:, row, :]
        own[row, INPUTS : INPUTS + HALF, :] = members[HALF:, row, :]
        own[row, INPUTS + HALF : INPUTS + 2 * HALF, :] = observed[:, row, :]
        own[row, FIELDS - 1 :, :] = jnp.zeros((1, LON), F32)
    odd = lax.axis_index("core") == 1
    is_input = lax.broadcasted_iota(jnp.int32, (FIELDS, 1), 0) < INPUTS
    initial = in_parts(own[0], own[1])
    last = in_parts(own[ROWS - 2], own[ROWS - 1])
    for row in range(HALO + 1):
        at = min(row, HALO - 1)
        first = jnp.where(is_input, own[at], initial[row])
        final = jnp.where(is_input, own[ROWS - HALO + at], last[row])
        edge_far[row] = jnp.where(odd, final, first).astype(BF16)
        edge_near[row] = jnp.where(odd, first, final).astype(BF16)


def in_parts(row_a, row_b):
    parts = []
    for value in (row_a, row_b):
        high = value.astype(BF16).astype(F32)
        middle = (value - high).astype(BF16).astype(F32)
        parts.append((high, middle, value - high - middle))
    (high_a, middle_a, low_a), (high_b, middle_b, low_b) = parts
    return [high_a, high_b, middle_a, middle_b, low_a, low_b]


def weights_kernel(
    kernel_in_in, kernel_mid_in, kernel_out_in, w_in, w_mid, w_out, w_back_2, w_back_1,
    kernel_in, kernel_mid, kernel_out, flat_in, square, flat_out, back_2, back_1, held_2, held_1, sems,
):
    pairs = [(kernel_in_in, kernel_in), (kernel_mid_in, kernel_mid), (kernel_out_in, kernel_out)]
    copies = [
        pltpu.make_async_copy(source, target, sems.at[2 + at])
        for at, (source, target) in enumerate(pairs)
    ]
    for copy in copies:
        copy.start()
    flat_out[...] = jnp.zeros_like(flat_out)
    back_2[...] = jnp.zeros_like(back_2)
    for copy in copies:
        copy.wait()
    for tap in range(9):
        a, b = tap // 3, tap % 3
        back = 3 * (2 - a) + b
        first = kernel_in[tap].astype(F32)
        first = jnp.concatenate([first, jnp.zeros((FIELDS - INPUTS, CH), F32)], 0).T
        flat_in[:, tap * FIELDS : (tap + 1) * FIELDS] = first
        mid = kernel_mid[tap].astype(F32)
        square[b * CH : (b + 1) * CH, a * CH : (a + 1) * CH] = mid
        back_1[a * CH : (a + 1) * CH, b * CH : (b + 1) * CH] = mid.T
        out = kernel_out[tap].astype(F32)
        across = slice(a * CH, (a + 1) * CH)
        flat_out[b * 16 : b * 16 + HALF, across] = out[:HALF]
        flat_out[b * 16 + 8 : b * 16 + 8 + HALF, across] = out[HALF:]
        out = jnp.concatenate([out, jnp.zeros((8 - VARS, CH), F32)], 0).T
        back_2[:, back * 16 : back * 16 + HALF] = out[:, :HALF]
        back_2[:, back * 16 + 8 : back * 16 + 8 + HALF] = out[:, HALF:VARS]
    held_2[...] = back_2[...].astype(BF16)
    held_1[...] = back_1[...].astype(BF16)
    copies = [
        pltpu.make_async_copy(held_2, w_back_2, sems.at[0]),
        pltpu.make_async_copy(held_1, w_back_1, sems.at[1]),
    ]
    for copy in copies:
        copy.start()
    w_in[...] = flat_in[...].astype(BF16)
    w_mid[...] = square[...].astype(BF16)
    w_out[...] = flat_out[...].astype(BF16)
    for copy in copies:
        copy.wait()


def forward_kernel(
    place, far, near, own, members_in, w_in, w_mid, w_out,
    send, pushed, kept_out, stack_out, hidden_1_out, slope_1_out, hidden_2_out, slope_2_out,
    kept, stack, hidden_1, slope_1, hidden_2, slope_2, edges, members, sems,
):
    brought = pltpu.make_async_copy(members_in.at[:HALF], members, sems.at[6])
    brought.start()
    base = place[1]
    odd = place[2] == 1
    copies = []

    def keep(source, target):
        copy = pltpu.make_async_copy(source, target, sems.at[len(copies)])
        copy.start()
        copies.append(copy)

    is_input = lax.broadcasted_iota(jnp.int32, (FIELDS, 1), 0) < INPUTS
    for side in range(2):
        got = []
        for row in range(HALO + 1):
            one, other = far[row].astype(F32), near[row].astype(F32)
            got.append(jnp.where(odd == (side == 0), other, one))
        whole = [got[0] + got[2] + got[4], got[1] + got[3] + got[5]]
        for row in range(HALO):
            field = got[row]
            exact = row - (HALO - 2) if side == 0 else row
            if 0 <= exact < 2:
                field = jnp.where(is_input, field, whole[exact])
            edges[side * HALO + row] = field

    def wide(row):
        if row < HALO:
            return edges[row]
        return own[row - HALO] if row < HALO + ROWS else edges[row - ROWS]

    for row in range(ROWS + 2 * HALO):
        field = wide(row)
        for shift in range(3):
            part = turned(field, 1 - shift).astype(BF16)
            stack[row, shift * FIELDS : (shift + 1) * FIELDS, :] = part
    keep(stack.at[4:14], stack_out)

    def first(row, kept_row):
        pre = dot(w_in[...], stack[pl.ds(row, 3)].reshape(9 * FIELDS, LON))
        gate = sigmoid(pre)
        hidden_1[row] = (pre * gate * inside(base, row - 4)).astype(BF16)
        if kept_row:
            slope_1[row - 4] = gate * (1.0 + pre * (1.0 - gate))

    loop(0, 4, functools.partial(first, kept_row=False))
    loop(4, 12, functools.partial(first, kept_row=True))
    loop(12, 16, functools.partial(first, kept_row=False))
    keep(hidden_1.at[3:13], hidden_1_out)
    keep(slope_1, slope_1_out)

    def second(row, kept_row):
        part = dot(w_mid[...], hidden_1[pl.ds(row, 3)].reshape(3 * CH, LON))
        pre = turned(part[:CH], 1) + part[CH : 2 * CH] + turned(part[2 * CH :], -1)
        gate = sigmoid(pre)
        hidden_2[row] = (pre * gate * inside(base, row - 3)).astype(BF16)
        if kept_row:
            slope_2[row - 2] = gate * (1.0 + pre * (1.0 - gate))

    loop(0, 2, functools.partial(second, kept_row=False))
    loop(2, 12, functools.partial(second, kept_row=True))
    loop(12, 14, functools.partial(second, kept_row=False))
    keep(hidden_2.at[2:12], hidden_2_out)
    keep(slope_2, slope_2_out)

    brought.wait()
    send[OWN:FAR_AT, :] = members[...].reshape(OWN, LON)
    for row in range(ROWS + 4):
        part = dot(w_out[...], hidden_2[row : row + 3].reshape(3 * CH, LON))
        both = turned(part[:16], 1) + part[16:32] + turned(part[32:], -1)
        log_scale = jnp.tanh(both[:HALF])
        field = wide(row + 3)
        moving = field[INPUTS : INPUTS + HALF]
        moved = moving * jnp.exp(log_scale) + both[8 : 8 + HALF]
        here = slice(row * HALF, (row + 1) * HALF)
        kept[0, here, :] = log_scale
        kept[1, here, :] = moving
        kept[2, here, :] = field[INPUTS + HALF : INPUTS + 2 * HALF]
        kept[3, here, :] = moved
        if 2 <= row < 2 + ROWS:
            send[(row - 2) * HALF : (row - 1) * HALF, :] = moved
            for var in range(HALF):
                pushed[HALF + var, row - 2 : row - 1, :] = moved[var : var + 1]
    keep(kept, kept_out)
    far_rows = jnp.where(odd, kept[3, WIDE - NEAR :, :], kept[3, :NEAR, :])
    send[FAR_AT:, :] = jnp.concatenate([far_rows, jnp.zeros((SENT - FAR_AT - NEAR, LON), F32)], 0)
    pushed[:HALF] = members[...]
    for copy in copies:
        copy.wait()


def folded(value):
    return sum(value[..., at : at + 128] for at in range(0, LON, 128))


def distance_kernel(place, lat, members, observed, fields, kept, partials, swapped):
    me = place[0]
    odd = place[2] == 1
    upper_lat = lat[NEAR : NEAR + OWN, :1]
    lower_lat = jnp.concatenate([lat[LAT_AT:, :1]] * HALF, 0)
    fixed_mine = members[:HALF].reshape(OWN, LON)
    mine = kept[3, NEAR : NEAR + OWN, :]

    def weighed(moved, fixed):
        upper = jnp.sum(folded(upper_lat * (mine - moved) ** 2), 0, keepdims=True)
        lower = jnp.sum(folded(lower_lat * (fixed_mine - fixed) ** 2), 0, keepdims=True)
        return upper + lower

    seen = kept[2, NEAR : NEAR + OWN, :]
    to_observed = weighed(seen, observed[:HALF].reshape(OWN, LON))
    rows = []
    for n in range(MEMBERS):
        first, last = fields[n, :NEAR], fields[n, OWN - NEAR : OWN]
        swapped[n * NEAR : (n + 1) * NEAR, :] = jnp.where(odd, first, last)
        rows.append(weighed(fields[n, :OWN], fields[n, OWN:FAR_AT]))
    all_rows = jnp.concatenate(rows, 0)
    spot = lax.broadcasted_iota(jnp.int32, (MEMBERS, 128), 0)
    partials[...] = jnp.where(spot == me, to_observed, all_rows)


def started(pairs, sems):
    copies = [
        pltpu.make_async_copy(source, target, sems.at[at])
        for at, (source, target) in enumerate(pairs)
    ]
    for copy in copies:
        copy.start()
    return copies


def backward_kernel(
    place, lat, totals, near, fields_in, kept_in, stack_in, hidden_1_in, slope_1_in, hidden_2_in,
    slope_2_in, w_back_2_in, w_back_1_in,
    mine, theirs,
    fields, kept, stack, hidden_1, slope_1, hidden_2, slope_2, w_back_2, w_back_1,
    coupled, turned_2, by_row, sum_out, sum_mid, sum_in, packed, sems,
):
    sources = [kept_in, fields_in, w_back_2_in, slope_2_in]
    sources += [w_back_1_in, hidden_1_in, hidden_2_in, slope_1_in, stack_in]
    targets = [kept, fields, w_back_2, slope_2]
    targets += [w_back_1, hidden_1, hidden_2, slope_1, stack]
    copies = started(list(zip(sources, targets)), sems)
    me, base, core = place[0], place[1], place[2]
    sum_out[...] = jnp.zeros_like(sum_out)
    sum_mid[...] = jnp.zeros_like(sum_mid)
    sum_in[...] = jnp.zeros_like(sum_in)
    total = totals[0]
    for tile in range(1, RING):
        total = total + totals[tile]
    distances = jnp.sqrt(jnp.sum(total, 1, keepdims=True) / ENTRIES + EPSILON)
    is_me = lax.broadcasted_iota(jnp.int32, (MEMBERS, 1), 0) == me
    shares = jnp.where(is_me, distances / MEMBERS, -distances / (2.0 * MEMBERS * MEMBERS))
    share = jnp.sum(shares, 0, keepdims=True) / TILES
    weights = 1.0 / (jnp.where(is_me, MEMBERS, MEMBERS * MEMBERS) * distances)
    own_weight = jnp.sum(jnp.where(is_me, weights, 0.0), 0, keepdims=True)
    weights = jnp.where(is_me, 0.0, weights)
    copies[0].wait()
    log_scale, moving, observed, moved = kept[0], kept[1], kept[2], kept[3]
    inner = (moved - observed) * own_weight
    copies[1].wait()
    odd = core == 1
    first, last = moved[:NEAR], moved[WIDE - NEAR :]
    near_mine, far_mine = jnp.where(odd, first, last), jnp.where(odd, last, first)
    own_sum = jnp.zeros((OWN, LON), F32)
    near_sum = jnp.zeros((NEAR, LON), F32)
    far_sum = near_sum
    for n in range(MEMBERS):
        weight = weights[n : n + 1]
        own_sum += weight * (moved[NEAR : NEAR + OWN] - fields[n, :OWN])
        near_sum += weight * (near_mine - near[n * NEAR : (n + 1) * NEAR])
        far_sum += weight * (far_mine - fields[n, FAR_AT : FAR_AT + NEAR])
    first, last = jnp.where(odd, near_sum, far_sum), jnp.where(odd, far_sum, near_sum)
    inner = inner - jnp.concatenate([first, own_sum, last], 0)
    upper = lat[:WIDE, :1] * inner / math.sqrt(ENTRIES)
    scaled = upper * moving * jnp.exp(log_scale) * (1.0 - log_scale * log_scale)
    blank = jnp.zeros((8 - HALF, LON), F32)
    for row in range(ROWS + 4):
        here = slice(row * HALF, (row + 1) * HALF)
        field = jnp.concatenate([scaled[here], blank, upper[here], blank], 0)
        for shift in range(3):
            part = turned(field, shift - 1).astype(BF16)
            coupled[row, shift * 16 : (shift + 1) * 16, :] = part
    copies[2].wait()
    copies[3].wait()

    def second(row):
        back = dot(w_back_2[...], coupled[pl.ds(row, 3)].reshape(144, LON))
        grad = back * slope_2[row] * inside(base, row - 1)
        for shift in range(3):
            part = turned(grad, shift - 1).astype(BF16)
            turned_2[row, shift * CH : (shift + 1) * CH, :] = part

    loop(0, ROWS + 2, second)
    copies[4].wait()

    def across_rows(row):
        by_row[row] = dot(w_back_1[...], turned_2[row])

    loop(0, ROWS + 2, across_rows)
    copies[5].wait()

    def middle(row):
        near = hidden_1[pl.ds(row, 3)].reshape(3 * CH, LON)
        sum_mid[...] += dot_cells(turned_2[row + 1], near)

    loop(0, ROWS, middle)
    copies[6].wait()

    def outer(row):
        near = hidden_2[pl.ds(row, 3)].reshape(3 * CH, LON)
        sum_out[...] += dot_cells(coupled[row + 2], near)

    loop(0, ROWS, outer)
    copies[7].wait()
    copies[8].wait()

    def last(row):
        back = by_row[row + 2, :CH] + by_row[row + 1, CH : 2 * CH] + by_row[row, 2 * CH :]
        grad = (back * slope_1[row]).astype(BF16)
        near = stack[pl.ds(row, 3)].reshape(9 * FIELDS, LON)
        sum_in[...] += dot_cells(near, grad)

    loop(0, ROWS, last)
    packed[5 * CH :, :] = jnp.zeros((CH, 128), F32)
    packed[4 * CH : 5 * CH, CH:] = jnp.zeros((CH, CH), F32)
    for tap in range(9):
        a, b = tap // 3, tap % 3
        at, side = place_mid(tap)
        packed[at : at + CH, side] = sum_mid[b * CH : (b + 1) * CH, a * CH : (a + 1) * CH]
        at = 5 * CH + tap * VARS
        across = slice(a * CH, (a + 1) * CH)
        packed[at : at + HALF, :CH] = sum_out[b * 16 : b * 16 + HALF, across]
        packed[at + HALF : at + VARS, :CH] = sum_out[b * 16 + 8 : b * 16 + 8 + HALF, across]
        at = 4 * CH + tap * INPUTS
        packed[at : at + INPUTS, CH:] = sum_in[tap * FIELDS : tap * FIELDS + INPUTS]
    packed[6 * CH - 1 :, 127:] = share
    half = MEMBERS * CHUNK
    for copy in range(2):

        @pl.when(core == copy)
        def _():
            mine[...] = packed[copy * half : (copy + 1) * half, :]
            theirs[...] = packed[(1 - copy) * half : (2 - copy) * half, :]


def place_mid(tap):
    return (tap * CH, slice(0, CH)) if tap < 5 else ((tap - 5) * CH, slice(CH, 2 * CH))


def unpack_kernel(place, chunks, grad_in, grad_mid, grad_out, energy, packed):
    core = place[2]
    for member in range(MEMBERS):
        first, second = chunks[member, 0], chunks[member, 1]
        at = member * CHUNK
        packed[at : at + CHUNK, :] = jnp.where(core == 0, first, second)
        at += MEMBERS * CHUNK
        packed[at : at + CHUNK, :] = jnp.where(core == 0, second, first)
    for tap in range(9):
        at, side = place_mid(tap)
        grad_mid[tap] = packed[at : at + CH, side]
        at = 5 * CH + tap * VARS
        grad_out[tap] = packed[at : at + VARS, :CH]
        at = 4 * CH + tap * INPUTS
        grad_in[tap] = packed[at : at + INPUTS, CH:]
    energy[...] = packed[6 * CH - 1 :, 127:]


VMEM_LIMIT = 28 * 10**6
VMEM = pl.BlockSpec(memory_space=pltpu.VMEM)
HBM = pl.BlockSpec(memory_space=pltpu.HBM)
SMEM = pl.BlockSpec(memory_space=pltpu.SMEM)


def call(kernel, ins, outs, scratch=(), copies=0, flops=10**6, vmem=VMEM_LIMIT):
    held = [pltpu.VMEM(shape, dtype) for shape, dtype in scratch]
    if copies > 0:
        held.append(pltpu.SemaphoreType.DMA((copies,)))
    shapes = [
        pltpu.HBM(shape, dtype) if spec is HBM else jax.ShapeDtypeStruct(shape, dtype)
        for shape, dtype, spec in outs
    ]
    run = pl.pallas_call(
        kernel,
        out_shape=shapes,
        in_specs=ins,
        out_specs=[spec for shape, dtype, spec in outs],
        scratch_shapes=held,
        compiler_params=pltpu.CompilerParams(vmem_limit_bytes=vmem),
        cost_estimate=pl.CostEstimate(flops=flops, bytes_accessed=10**6, transcendentals=0),
    )

    def placed(*arrays):
        return run(
            *[
                pltpu.with_memory_space_constraint(array, pltpu.HBM) if spec is HBM else array
                for array, spec in zip(arrays, ins)
            ]
        )

    return placed


def per_device(members, condition, observed, kernel_in, kernel_mid, kernel_out):
    members = members[0]
    core = lax.axis_index("core")
    tile = lax.axis_index(TILE)
    place = jnp.stack([lax.axis_index("member"), tile * ROWS, core]).astype(jnp.int32)
    table = jnp.asarray(lat_table())
    lat = lax.dynamic_slice_in_dim(table, tile, 1, 0)[0]
    lat = jnp.broadcast_to(lat[:, None], (LAT_AT + ROWS, 128))
    edge = ((HALO + 1, FIELDS, LON), BF16, VMEM)
    own, edge_far, edge_near = call(
        pack_kernel,
        [HBM] * 3,
        [((ROWS, FIELDS, LON), F32, VMEM), edge, edge],
        [((VARS, ROWS, LON), F32), ((COND, ROWS, LON), F32), ((HALF, ROWS, LON), F32)],
        copies=3,
    )(members, condition, observed)
    across = [(i, i + 1) for i in range(1, TILES - 1, 2)]
    far = lax.ppermute(edge_far, TILE, across + [(j, i) for i, j in across])
    near = lax.ppermute(edge_near, "core", [(0, 1), (1, 0)])
    near, place, lat = lax.optimization_barrier((near, place, lat))
    w_shapes = [(CH, 9 * FIELDS), (3 * CH, 3 * CH), (48, 3 * CH), (CH, 144), (3 * CH, 3 * CH)]
    w_in, w_mid, w_out, w_back_2, w_back_1 = call(
        weights_kernel,
        [HBM] * 3,
        [(shape, BF16, VMEM) for shape in w_shapes[:3]]
        + [(shape, BF16, HBM) for shape in w_shapes[3:]],
        [((9, INPUTS, CH), BF16), ((9, CH, CH), BF16), ((9, VARS, CH), BF16)]
        + [(shape, F32) for shape in w_shapes]
        + [(shape, BF16) for shape in w_shapes[3:]],
        copies=5,
    )(kernel_in.transpose(0, 2, 1), kernel_mid, kernel_out)
    saved = [
        ((ROWS + 2, 3 * FIELDS, LON), BF16),
        ((ROWS + 2, CH, LON), BF16),
        ((ROWS, CH, LON), F32),
        ((ROWS + 2, CH, LON), BF16),
        ((ROWS + 2, CH, LON), F32),
    ]
    worked = [
        ((ROWS + 10, 3 * FIELDS, LON), BF16),
        ((ROWS + 8, CH, LON), BF16),
        ((ROWS, CH, LON), F32),
        ((ROWS + 6, CH, LON), BF16),
        ((ROWS + 2, CH, LON), F32),
    ]
    kept_shape = ((4, WIDE, LON), F32)
    send, pushed, kept, stack, hidden_1, slope_1, hidden_2, slope_2 = call(
        forward_kernel,
        [SMEM] + [VMEM] * 3 + [HBM] + [VMEM] * 3,
        [((SENT, LON), F32, VMEM), ((VARS, ROWS, LON), F32, VMEM), kept_shape + (HBM,)]
        + [shape + (HBM,) for shape in saved],
        [kept_shape] + worked
        + [((2 * HALO, FIELDS, LON), F32), ((HALF, ROWS, LON), F32)],
        copies=7,
        flops=10**9,
    )(place, far, near, own, members, w_in, w_mid, w_out)
    fields = spread(send, "member", MEMBERS)
    fields_shape = ((MEMBERS, SENT, LON), F32)
    partials, swapped = call(
        distance_kernel,
        [SMEM] + [VMEM] * 5,
        [((MEMBERS, 128), F32, VMEM), ((MEMBERS * NEAR, LON), F32, VMEM)],
        vmem=8 * 10**6,
    )(place, lat, members, observed, fields, kept)
    swap = [(0, 1), (1, 0)]
    beside = lax.ppermute(swapped, "core", swap)
    partials = partials + lax.ppermute(partials, "core", swap)
    totals = spread(partials, "ring", RING)
    mine, theirs = call(
        backward_kernel,
        [SMEM] + [VMEM] * 3 + [HBM] * 9,
        [((MEMBERS * CHUNK, 128), F32, VMEM)] * 2,
        [fields_shape, kept_shape]
        + saved
        + [(shape, BF16) for shape in w_shapes[3:]]
        + [
            ((ROWS + 4, 48, LON), BF16),
            ((ROWS + 2, 3 * CH, LON), BF16),
            ((ROWS + 2, 3 * CH, LON), F32),
            ((48, 3 * CH), F32),
            ((3 * CH, 3 * CH), F32),
            ((9 * FIELDS, CH), F32),
            ((6 * CH, 128), F32),
        ],
        copies=9,
        flops=10**9,
    )(
        place, lat, totals, beside, fields, kept, stack, hidden_1, slope_1, hidden_2, slope_2,
        w_back_2, w_back_1,
    )
    mine = mine + lax.ppermute(theirs, "core", swap)
    chunk = jnp.sum(lax.all_to_all(mine.reshape(MEMBERS, CHUNK, 128), "member", 0, 0), 0)
    chunk = jnp.sum(spread(chunk, "ring", RING), 0)
    other = lax.ppermute(chunk, "core", swap)
    chunks = spread(jnp.stack([chunk, other]), "member", MEMBERS)
    grad_in, grad_mid, grad_out, energy = call(
        unpack_kernel,
        [SMEM, VMEM],
        [
            ((9, INPUTS, CH), F32, VMEM),
            ((9, CH, CH), F32, VMEM),
            ((9, VARS, CH), F32, VMEM),
            ((1, 1), F32, VMEM),
        ],
        [((6 * CH, 128), F32)],
        vmem=16 * 10**6,
    )(place, chunks)
    return (pushed[None], energy[0, 0], grad_in.transpose(0, 2, 1), grad_mid, grad_out)


def solution(mesh):
    fine = Mesh(mesh.devices.reshape(MEMBERS, -1, 2), ("member",) + TILE)
    in_specs = (
        P("member", None, TILE, None),
        P(None, TILE, None),
        P(None, TILE, None),
        P(),
        P(),
        P(),
    )
    out_specs = (P("member", None, TILE, None), P(), P(), P(), P())
    return jax.shard_map(
        per_device, mesh=fine, in_specs=in_specs, out_specs=out_specs, check_vma=False
    )
```

```python
import functools
import math

import jax
import jax.numpy as jnp
import numpy as np
from jax import lax
from jax.experimental import pallas as pl
from jax.experimental.pallas import tpu as pltpu
from jax.sharding import Mesh, PartitionSpec as P

EPSILON = 1e-06
MEMBERS, NLAT, LON, ROWS = 8, 256, 512, 8
VARS, HALF, COND, CH = 6, 3, 6, 64
TILES, RING = 32, 16
ENTRIES = VARS * NLAT * LON
HALO = 5
FIELDS = 16
INPUTS = HALF + COND
WIDE = (ROWS + 4) * HALF
LAT_AT = 40
OWN = ROWS * HALF
FAR_AT = 2 * OWN
NEAR = 2 * HALF
SENT = 56
CHUNK = 24
TILE = ("ring", "core")
F32, BF16 = jnp.float32, jnp.bfloat16


def spread(value, axes, count):
    copies = jnp.broadcast_to(value[None], (count,) + value.shape)
    return lax.all_to_all(copies, axes, 0, 0)


def lat_table():
    rows = np.arange(NLAT)
    cosine = np.cos((-90.0 + 180.0 * (rows + 0.5) / NLAT) * (np.pi / 180.0))
    lat = (cosine / cosine.mean()).astype(np.float32)
    padded = np.pad(lat, (2, 2))
    table = np.zeros((TILES, LAT_AT + ROWS), np.float32)
    for tile in range(TILES):
        wide = padded[tile * ROWS : tile * ROWS + ROWS + 4]
        table[tile, :WIDE] = np.repeat(wide, HALF)
        table[tile, LAT_AT:] = lat[tile * ROWS : (tile + 1) * ROWS]
    return table


def turned(value, step):
    return value if step == 0 else pltpu.roll(value, step % LON, 1)


def dot(left, right):
    return jnp.dot(left, right, preferred_element_type=F32)


def dot_cells(left, right):
    return lax.dot_general(left, right, (((1,), (1,)), ((), ())), preferred_element_type=F32)


def first_row():
    return lax.axis_index(TILE) * ROWS


def inside(base, row):
    row = base + row
    return jnp.where((row >= 0) & (row < NLAT), 1.0, 0.0).astype(F32)


def sigmoid(value):
    return 0.5 * jnp.tanh(0.5 * value) + 0.5


def loop(start, stop, body):
    lax.fori_loop(start, stop, lambda row, carry: (body(row), carry)[1], 0, unroll=True)


def pack_kernel(
    members_in, condition_in, observed_in, own, edge_far, edge_near,
    members, condition, observed, sems,
):
    pairs = [(members_in, members), (condition_in, condition)]
    pairs.append((observed_in.at[HALF:], observed))
    for copy in started(pairs, sems):
        copy.wait()
    for row in range(ROWS):
        own[row, :HALF, :] = members[:HALF, row, :]
        own[row, HALF:INPUTS, :] = condition[:, row, :]
        own[row, INPUTS : INPUTS + HALF, :] = members[HALF:, row, :]
        own[row, INPUTS + HALF : INPUTS + 2 * HALF, :] = observed[:, row, :]
        own[row, FIELDS - 1 :, :] = jnp.zeros((1, LON), F32)
    odd = lax.axis_index("core") == 1
    is_input = lax.broadcasted_iota(jnp.int32, (FIELDS, 1), 0) < INPUTS
    initial = in_parts(own[0], own[1])
    last = in_parts(own[ROWS - 2], own[ROWS - 1])
    for row in range(HALO + 1):
        at = min(row, HALO - 1)
        first = jnp.where(is_input, own[at], initial[row])
        final = jnp.where(is_input, own[ROWS - HALO + at], last[row])
        edge_far[row] = jnp.where(odd, final, first).astype(BF16)
        edge_near[row] = jnp.where(odd, first, final).astype(BF16)


def in_parts(row_a, row_b):
    parts = []
    for value in (row_a, row_b):
        high = value.astype(BF16).astype(F32)
        middle = (value - high).astype(BF16).astype(F32)
        parts.append((high, middle, value - high - middle))
    (high_a, middle_a, low_a), (high_b, middle_b, low_b) = parts
    return [high_a, high_b, middle_a, middle_b, low_a, low_b]


def weights_kernel(
    kernel_in_in, kernel_mid_in, kernel_out_in, w_in, w_mid, w_out, w_back_2, w_back_1,
    kernel_in, kernel_mid, kernel_out, flat_in, square, flat_out, back_2, back_1, held_2, held_1, sems,
):
    pairs = [(kernel_in_in, kernel_in), (kernel_mid_in, kernel_mid), (kernel_out_in, kernel_out)]
    copies = [
        pltpu.make_async_copy(source, target, sems.at[2 + at])
        for at, (source, target) in enumerate(pairs)
    ]
    for copy in copies:
        copy.start()
    flat_out[...] = jnp.zeros_like(flat_out)
    back_2[...] = jnp.zeros_like(back_2)
    for copy in copies:
        copy.wait()
    for tap in range(9):
        a, b = tap // 3, tap % 3
        back = 3 * (2 - a) + b
        first = kernel_in[tap].astype(F32)
        first = jnp.concatenate([first, jnp.zeros((FIELDS - INPUTS, CH), F32)], 0).T
        flat_in[:, tap * FIELDS : (tap + 1) * FIELDS] = first
        mid = kernel_mid[tap].astype(F32)
        square[b * CH : (b + 1) * CH, a * CH : (a + 1) * CH] = mid
        back_1[a * CH : (a + 1) * CH, b * CH : (b + 1) * CH] = mid.T
        out = kernel_out[tap].astype(F32)
        across = slice(a * CH, (a + 1) * CH)
        flat_out[b * 16 : b * 16 + HALF, across] = out[:HALF]
        flat_out[b * 16 + 8 : b * 16 + 8 + HALF, across] = out[HALF:]
        out = jnp.concatenate([out, jnp.zeros((8 - VARS, CH), F32)], 0).T
        back_2[:, back * 16 : back * 16 + HALF] = out[:, :HALF]
        back_2[:, back * 16 + 8 : back * 16 + 8 + HALF] = out[:, HALF:VARS]
    held_2[...] = back_2[...].astype(BF16)
    held_1[...] = back_1[...].astype(BF16)
    copies = [
        pltpu.make_async_copy(held_2, w_back_2, sems.at[0]),
        pltpu.make_async_copy(held_1, w_back_1, sems.at[1]),
    ]
    for copy in copies:
        copy.start()
    w_in[...] = flat_in[...].astype(BF16)
    w_mid[...] = square[...].astype(BF16)
    w_out[...] = flat_out[...].astype(BF16)
    for copy in copies:
        copy.wait()


def forward_kernel(
    far, near, own, members_in, w_in, w_mid, w_out,
    send, pushed, kept_out, stack_out, hidden_1_out, slope_1_out, hidden_2_out, slope_2_out,
    kept, stack, hidden_1, slope_1, hidden_2, slope_2, edges, members, sems,
):
    brought = pltpu.make_async_copy(members_in.at[:HALF], members, sems.at[6])
    brought.start()
    base, odd = first_row(), lax.axis_index("core") == 1
    copies = []

    def keep(source, target):
        copy = pltpu.make_async_copy(source, target, sems.at[len(copies)])
        copy.start()
        copies.append(copy)

    is_input = lax.broadcasted_iota(jnp.int32, (FIELDS, 1), 0) < INPUTS
    for side in range(2):
        got = []
        for row in range(HALO + 1):
            one, other = far[row].astype(F32), near[row].astype(F32)
            got.append(jnp.where(odd == (side == 0), other, one))
        whole = [got[0] + got[2] + got[4], got[1] + got[3] + got[5]]
        for row in range(HALO):
            field = got[row]
            exact = row - (HALO - 2) if side == 0 else row
            if 0 <= exact < 2:
                field = jnp.where(is_input, field, whole[exact])
            edges[side * HALO + row] = field

    def wide(row):
        if row < HALO:
            return edges[row]
        return own[row - HALO] if row < HALO + ROWS else edges[row - ROWS]

    for row in range(ROWS + 2 * HALO):
        field = wide(row)
        for shift in range(3):
            part = turned(field, 1 - shift).astype(BF16)
            stack[row, shift * FIELDS : (shift + 1) * FIELDS, :] = part
    keep(stack.at[4:14], stack_out)

    def first(row, kept_row):
        pre = dot(w_in[...], stack[pl.ds(row, 3)].reshape(9 * FIELDS, LON))
        gate = sigmoid(pre)
        hidden_1[row] = (pre * gate * inside(base, row - 4)).astype(BF16)
        if kept_row:
            slope_1[row - 4] = gate * (1.0 + pre * (1.0 - gate))

    loop(0, 4, functools.partial(first, kept_row=False))
    loop(4, 12, functools.partial(first, kept_row=True))
    loop(12, 16, functools.partial(first, kept_row=False))
    keep(hidden_1.at[3:13], hidden_1_out)
    keep(slope_1, slope_1_out)

    def second(row, kept_row):
        part = dot(w_mid[...], hidden_1[pl.ds(row, 3)].reshape(3 * CH, LON))
        pre = turned(part[:CH], 1) + part[CH : 2 * CH] + turned(part[2 * CH :], -1)
        gate = sigmoid(pre)
        hidden_2[row] = (pre * gate * inside(base, row - 3)).astype(BF16)
        if kept_row:
            slope_2[row - 2] = gate * (1.0 + pre * (1.0 - gate))

    loop(0, 2, functools.partial(second, kept_row=False))
    loop(2, 12, functools.partial(second, kept_row=True))
    loop(12, 14, functools.partial(second, kept_row=False))
    keep(hidden_2.at[2:12], hidden_2_out)
    keep(slope_2, slope_2_out)

    brought.wait()
    send[OWN:FAR_AT, :] = members[...].reshape(OWN, LON)
    for row in range(ROWS + 4):
        part = dot(w_out[...], hidden_2[row : row + 3].reshape(3 * CH, LON))
        both = turned(part[:16], 1) + part[16:32] + turned(part[32:], -1)
        log_scale = jnp.tanh(both[:HALF])
        field = wide(row + 3)
        moving = field[INPUTS : INPUTS + HALF]
        moved = moving * jnp.exp(log_scale) + both[8 : 8 + HALF]
        here = slice(row * HALF, (row + 1) * HALF)
        kept[0, here, :] = log_scale
        kept[1, here, :] = moving
        kept[2, here, :] = field[INPUTS + HALF : INPUTS + 2 * HALF]
        kept[3, here, :] = moved
        if 2 <= row < 2 + ROWS:
            send[(row - 2) * HALF : (row - 1) * HALF, :] = moved
            for var in range(HALF):
                pushed[HALF + var, row - 2 : row - 1, :] = moved[var : var + 1]
    keep(kept, kept_out)
    far_rows = jnp.where(odd, kept[3, WIDE - NEAR :, :], kept[3, :NEAR, :])
    send[FAR_AT:, :] = jnp.concatenate([far_rows, jnp.zeros((SENT - FAR_AT - NEAR, LON), F32)], 0)
    pushed[:HALF] = members[...]
    for copy in copies:
        copy.wait()


def folded(value):
    return sum(value[..., at : at + 128] for at in range(0, LON, 128))


def distance_kernel(lat, members, observed, fields, kept, swapped):
    me, odd = lax.axis_index("member"), lax.axis_index("core") == 1
    upper_lat = lat[NEAR : NEAR + OWN, :1]
    lower_lat = jnp.concatenate([lat[LAT_AT:, :1]] * HALF, 0)
    fixed_mine = members[:HALF].reshape(OWN, LON)
    mine = kept[3, NEAR : NEAR + OWN, :]

    def weighed(moved, fixed):
        upper = jnp.sum(folded(upper_lat * (mine - moved) ** 2), 0, keepdims=True)
        lower = jnp.sum(folded(lower_lat * (fixed_mine - fixed) ** 2), 0, keepdims=True)
        return upper + lower

    seen = kept[2, NEAR : NEAR + OWN, :]
    to_observed = weighed(seen, observed[:HALF].reshape(OWN, LON))
    rows = []
    for n in range(MEMBERS):
        first, last = fields[n, :NEAR], fields[n, OWN - NEAR : OWN]
        swapped[n * NEAR : (n + 1) * NEAR, :] = jnp.where(odd, first, last)
        rows.append(weighed(fields[n, :OWN], fields[n, OWN:FAR_AT]))
    all_rows = jnp.concatenate(rows, 0)
    spot = lax.broadcasted_iota(jnp.int32, (MEMBERS, 128), 0)
    swapped[MEMBERS * NEAR :, :128] = jnp.where(spot == me, to_observed, all_rows)
    swapped[MEMBERS * NEAR :, 128:] = jnp.zeros((MEMBERS, LON - 128), F32)


def started(pairs, sems):
    copies = [
        pltpu.make_async_copy(source, target, sems.at[at])
        for at, (source, target) in enumerate(pairs)
    ]
    for copy in copies:
        copy.start()
    return copies


def backward_kernel(
    lat, totals, near, fields_in, kept_in, stack_in, hidden_1_in, slope_1_in, hidden_2_in,
    slope_2_in, w_back_2_in, w_back_1_in,
    mine, theirs,
    fields, kept, stack, hidden_1, slope_1, hidden_2, slope_2, w_back_2, w_back_1,
    coupled, turned_2, by_row, sum_out, sum_mid, sum_in, packed, sems,
):
    sources = [kept_in, fields_in, w_back_2_in, slope_2_in]
    sources += [w_back_1_in, hidden_1_in, hidden_2_in, slope_1_in, stack_in]
    targets = [kept, fields, w_back_2, slope_2]
    targets += [w_back_1, hidden_1, hidden_2, slope_1, stack]
    copies = started(list(zip(sources, targets)), sems)
    me, base, core = lax.axis_index("member"), first_row(), lax.axis_index("core")
    sum_out[...] = jnp.zeros_like(sum_out)
    sum_mid[...] = jnp.zeros_like(sum_mid)
    sum_in[...] = jnp.zeros_like(sum_in)
    total = totals[0]
    for tile in range(1, RING):
        total = total + totals[tile]
    distances = jnp.sqrt(jnp.sum(total, 1, keepdims=True) / ENTRIES + EPSILON)
    is_me = lax.broadcasted_iota(jnp.int32, (MEMBERS, 1), 0) == me
    shares = jnp.where(is_me, distances / MEMBERS, -distances / (2.0 * MEMBERS * MEMBERS))
    share = jnp.sum(shares, 0, keepdims=True) / TILES
    weights = 1.0 / (jnp.where(is_me, MEMBERS, MEMBERS * MEMBERS) * distances)
    own_weight = jnp.sum(jnp.where(is_me, weights, 0.0), 0, keepdims=True)
    weights = jnp.where(is_me, 0.0, weights)
    copies[0].wait()
    log_scale, moving, observed, moved = kept[0], kept[1], kept[2], kept[3]
    inner = (moved - observed) * own_weight
    copies[1].wait()
    odd = core == 1
    first, last = moved[:NEAR], moved[WIDE - NEAR :]
    near_mine, far_mine = jnp.where(odd, first, last), jnp.where(odd, last, first)
    own_sum = jnp.zeros((OWN, LON), F32)
    near_sum = jnp.zeros((NEAR, LON), F32)
    far_sum = near_sum
    for n in range(MEMBERS):
        weight = weights[n : n + 1]
        own_sum += weight * (moved[NEAR : NEAR + OWN] - fields[n, :OWN])
        near_sum += weight * (near_mine - near[n * NEAR : (n + 1) * NEAR])
        far_sum += weight * (far_mine - fields[n, FAR_AT : FAR_AT + NEAR])
    first, last = jnp.where(odd, near_sum, far_sum), jnp.where(odd, far_sum, near_sum)
    inner = inner - jnp.concatenate([first, own_sum, last], 0)
    upper = lat[:WIDE, :1] * inner / math.sqrt(ENTRIES)
    scaled = upper * moving * jnp.exp(log_scale) * (1.0 - log_scale * log_scale)
    blank = jnp.zeros((8 - HALF, LON), F32)
    for row in range(ROWS + 4):
        here = slice(row * HALF, (row + 1) * HALF)
        field = jnp.concatenate([scaled[here], blank, upper[here], blank], 0)
        for shift in range(3):
            part = turned(field, shift - 1).astype(BF16)
            coupled[row, shift * 16 : (shift + 1) * 16, :] = part
    copies[2].wait()
    copies[3].wait()

    def second(row):
        back = dot(w_back_2[...], coupled[pl.ds(row, 3)].reshape(144, LON))
        grad = back * slope_2[row] * inside(base, row - 1)
        for shift in range(3):
            part = turned(grad, shift - 1).astype(BF16)
            turned_2[row, shift * CH : (shift + 1) * CH, :] = part

    loop(0, ROWS + 2, second)
    copies[4].wait()

    def across_rows(row):
        by_row[row] = dot(w_back_1[...], turned_2[row])

    loop(0, ROWS + 2, across_rows)
    copies[5].wait()

    def middle(row):
        near = hidden_1[pl.ds(row, 3)].reshape(3 * CH, LON)
        sum_mid[...] += dot_cells(turned_2[row + 1], near)

    loop(0, ROWS, middle)
    copies[6].wait()

    def outer(row):
        near = hidden_2[pl.ds(row, 3)].reshape(3 * CH, LON)
        sum_out[...] += dot_cells(coupled[row + 2], near)

    loop(0, ROWS, outer)
    copies[7].wait()
    copies[8].wait()

    def last(row):
        back = by_row[row + 2, :CH] + by_row[row + 1, CH : 2 * CH] + by_row[row, 2 * CH :]
        grad = (back * slope_1[row]).astype(BF16)
        near = stack[pl.ds(row, 3)].reshape(9 * FIELDS, LON)
        sum_in[...] += dot_cells(near, grad)

    loop(0, ROWS, last)
    packed[5 * CH :, :] = jnp.zeros((CH, 128), F32)
    packed[4 * CH : 5 * CH, CH:] = jnp.zeros((CH, CH), F32)
    for tap in range(9):
        a, b = tap // 3, tap % 3
        at, side = place_mid(tap)
        packed[at : at + CH, side] = sum_mid[b * CH : (b + 1) * CH, a * CH : (a + 1) * CH]
        at = 5 * CH + tap * VARS
        across = slice(a * CH, (a + 1) * CH)
        packed[at : at + HALF, :CH] = sum_out[b * 16 : b * 16 + HALF, across]
        packed[at + HALF : at + VARS, :CH] = sum_out[b * 16 + 8 : b * 16 + 8 + HALF, across]
        at = 4 * CH + tap * INPUTS
        packed[at : at + INPUTS, CH:] = sum_in[tap * FIELDS : tap * FIELDS + INPUTS]
    packed[6 * CH - 1 :, 127:] = share
    half = MEMBERS * CHUNK
    for copy in range(2):

        @pl.when(core == copy)
        def _():
            mine[...] = packed[copy * half : (copy + 1) * half, :]
            theirs[...] = packed[(1 - copy) * half : (2 - copy) * half, :]


def place_mid(tap):
    return (tap * CH, slice(0, CH)) if tap < 5 else ((tap - 5) * CH, slice(CH, 2 * CH))


def unpack_kernel(chunks, grad_in, grad_mid, grad_out, energy, packed):
    core = lax.axis_index("core")
    for member in range(MEMBERS):
        first, second = chunks[member, 0], chunks[member, 1]
        at = member * CHUNK
        packed[at : at + CHUNK, :] = jnp.where(core == 0, first, second)
        at += MEMBERS * CHUNK
        packed[at : at + CHUNK, :] = jnp.where(core == 0, second, first)
    for tap in range(9):
        at, side = place_mid(tap)
        grad_mid[tap] = packed[at : at + CH, side]
        at = 5 * CH + tap * VARS
        grad_out[tap] = packed[at : at + VARS, :CH]
        at = 4 * CH + tap * INPUTS
        grad_in[tap] = packed[at : at + INPUTS, CH:]
    energy[...] = packed[6 * CH - 1 :, 127:]


VMEM_LIMIT = 28 * 10**6
VMEM = pl.BlockSpec(memory_space=pltpu.VMEM)
HBM = pl.BlockSpec(memory_space=pltpu.HBM)


def call(kernel, ins, outs, scratch=(), copies=0, flops=10**6, vmem=VMEM_LIMIT):
    held = [pltpu.VMEM(shape, dtype) for shape, dtype in scratch]
    if copies > 0:
        held.append(pltpu.SemaphoreType.DMA((copies,)))
    shapes = [
        pltpu.HBM(shape, dtype) if spec is HBM else jax.ShapeDtypeStruct(shape, dtype)
        for shape, dtype, spec in outs
    ]
    run = pl.pallas_call(
        kernel,
        out_shape=shapes,
        in_specs=ins,
        out_specs=[spec for shape, dtype, spec in outs],
        scratch_shapes=held,
        compiler_params=pltpu.CompilerParams(vmem_limit_bytes=vmem),
        cost_estimate=pl.CostEstimate(flops=flops, bytes_accessed=10**6, transcendentals=0),
    )

    def placed(*arrays):
        return run(
            *[
                pltpu.with_memory_space_constraint(array, pltpu.HBM) if spec is HBM else array
                for array, spec in zip(arrays, ins)
            ]
        )

    return placed


def per_device(members, condition, observed, kernel_in, kernel_mid, kernel_out):
    members = members[0]
    tile = lax.axis_index(TILE)
    table = jnp.asarray(lat_table())
    lat = lax.dynamic_slice_in_dim(table, tile, 1, 0)[0]
    lat = jnp.broadcast_to(lat[:, None], (LAT_AT + ROWS, 128))
    edge = ((HALO + 1, FIELDS, LON), BF16, VMEM)
    own, edge_far, edge_near = call(
        pack_kernel,
        [HBM] * 3,
        [((ROWS, FIELDS, LON), F32, VMEM), edge, edge],
        [((VARS, ROWS, LON), F32), ((COND, ROWS, LON), F32), ((HALF, ROWS, LON), F32)],
        copies=3,
    )(members, condition, observed)
    across = [(i, i + 1) for i in range(1, TILES - 1, 2)]
    far = lax.ppermute(edge_far, TILE, across + [(j, i) for i, j in across])
    near = lax.ppermute(edge_near, "core", [(0, 1), (1, 0)])
    near, lat = lax.optimization_barrier((near, lat))
    w_shapes = [(CH, 9 * FIELDS), (3 * CH, 3 * CH), (48, 3 * CH), (CH, 144), (3 * CH, 3 * CH)]
    w_in, w_mid, w_out, w_back_2, w_back_1 = call(
        weights_kernel,
        [HBM] * 3,
        [(shape, BF16, VMEM) for shape in w_shapes[:3]]
        + [(shape, BF16, HBM) for shape in w_shapes[3:]],
        [((9, INPUTS, CH), BF16), ((9, CH, CH), BF16), ((9, VARS, CH), BF16)]
        + [(shape, F32) for shape in w_shapes]
        + [(shape, BF16) for shape in w_shapes[3:]],
        copies=5,
    )(kernel_in.transpose(0, 2, 1), kernel_mid, kernel_out)
    saved = [
        ((ROWS + 2, 3 * FIELDS, LON), BF16),
        ((ROWS + 2, CH, LON), BF16),
        ((ROWS, CH, LON), F32),
        ((ROWS + 2, CH, LON), BF16),
        ((ROWS + 2, CH, LON), F32),
    ]
    worked = [
        ((ROWS + 10, 3 * FIELDS, LON), BF16),
        ((ROWS + 8, CH, LON), BF16),
        ((ROWS, CH, LON), F32),
        ((ROWS + 6, CH, LON), BF16),
        ((ROWS + 2, CH, LON), F32),
    ]
    kept_shape = ((4, WIDE, LON), F32)
    send, pushed, kept, stack, hidden_1, slope_1, hidden_2, slope_2 = call(
        forward_kernel,
        [VMEM] * 3 + [HBM] + [VMEM] * 3,
        [((SENT, LON), F32, VMEM), ((VARS, ROWS, LON), F32, VMEM), kept_shape + (HBM,)]
        + [shape + (HBM,) for shape in saved],
        [kept_shape] + worked
        + [((2 * HALO, FIELDS, LON), F32), ((HALF, ROWS, LON), F32)],
        copies=7,
        flops=10**9,
    )(far, near, own, members, w_in, w_mid, w_out)
    fields = spread(send, "member", MEMBERS)
    fields_shape = ((MEMBERS, SENT, LON), F32)
    (swapped,) = call(
        distance_kernel,
        [VMEM] * 5,
        [((MEMBERS * (NEAR + 1), LON), F32, VMEM)],
        vmem=8 * 10**6,
    )(lat, members, observed, fields, kept)
    swap = [(0, 1), (1, 0)]
    beside = lax.ppermute(swapped, "core", swap)
    partials = swapped[MEMBERS * NEAR :, :128] + beside[MEMBERS * NEAR :, :128]
    totals = spread(partials, "ring", RING)
    mine, theirs = call(
        backward_kernel,
        [VMEM] * 3 + [HBM] * 9,
        [((MEMBERS * CHUNK, 128), F32, VMEM)] * 2,
        [fields_shape, kept_shape]
        + saved
        + [(shape, BF16) for shape in w_shapes[3:]]
        + [
            ((ROWS + 4, 48, LON), BF16),
            ((ROWS + 2, 3 * CH, LON), BF16),
            ((ROWS + 2, 3 * CH, LON), F32),
            ((48, 3 * CH), F32),
            ((3 * CH, 3 * CH), F32),
            ((9 * FIELDS, CH), F32),
            ((6 * CH, 128), F32),
        ],
        copies=9,
        flops=10**9,
    )(
        lat, totals, beside, fields, kept, stack, hidden_1, slope_1, hidden_2, slope_2,
        w_back_2, w_back_1,
    )
    mine = mine + lax.ppermute(theirs, "core", swap)
    chunk = jnp.sum(lax.all_to_all(mine.reshape(MEMBERS, CHUNK, 128), "member", 0, 0), 0)
    chunk = jnp.sum(spread(chunk, "ring", RING), 0)
    other = lax.ppermute(chunk, "core", swap)
    chunks = spread(jnp.stack([chunk, other]), "member", MEMBERS)
    grad_in, grad_mid, grad_out, energy = call(
        unpack_kernel,
        [VMEM],
        [
            ((9, INPUTS, CH), F32, VMEM),
            ((9, CH, CH), F32, VMEM),
            ((9, VARS, CH), F32, VMEM),
            ((1, 1), F32, VMEM),
        ],
        [((6 * CH, 128), F32)],
        vmem=16 * 10**6,
    )(chunks)
    return (pushed[None], energy[0, 0], grad_in.transpose(0, 2, 1), grad_mid, grad_out)


def solution(mesh):
    fine = Mesh(mesh.devices.reshape(MEMBERS, -1, 2), ("member",) + TILE)
    in_specs = (
        P("member", None, TILE, None),
        P(None, TILE, None),
        P(None, TILE, None),
        P(),
        P(),
        P(),
    )
    out_specs = (P("member", None, TILE, None), P(), P(), P(), P())
    return jax.shard_map(
        per_device, mesh=fine, in_specs=in_specs, out_specs=out_specs, check_vma=False
    )
```

```python
import functools
import math

import jax
import jax.numpy as jnp
import numpy as np
from jax import lax
from jax.experimental import pallas as pl
from jax.experimental.pallas import tpu as pltpu
from jax.sharding import Mesh, PartitionSpec as P

EPSILON = 1e-06
MEMBERS, NLAT, LON, ROWS = 8, 256, 512, 8
VARS, HALF, COND, CH = 6, 3, 6, 64
TILES, RING = 32, 16
ENTRIES = VARS * NLAT * LON
HALO = 5
FIELDS = 16
INPUTS = HALF + COND
WIDE = (ROWS + 4) * HALF
LAT_AT = 40
OWN = ROWS * HALF
FAR_AT = 2 * OWN
NEAR = 2 * HALF
SENT = 56
CHUNK = 24
TILE = ("ring", "core")
F32, BF16 = jnp.float32, jnp.bfloat16


def spread(value, axes, count):
    copies = jnp.broadcast_to(value[None], (count,) + value.shape)
    return lax.all_to_all(copies, axes, 0, 0)


def lat_table():
    rows = np.arange(NLAT)
    cosine = np.cos((-90.0 + 180.0 * (rows + 0.5) / NLAT) * (np.pi / 180.0))
    lat = (cosine / cosine.mean()).astype(np.float32)
    padded = np.pad(lat, (2, 2))
    table = np.zeros((TILES, LAT_AT + ROWS), np.float32)
    for tile in range(TILES):
        wide = padded[tile * ROWS : tile * ROWS + ROWS + 4]
        table[tile, :WIDE] = np.repeat(wide, HALF)
        table[tile, LAT_AT:] = lat[tile * ROWS : (tile + 1) * ROWS]
    return table


def turned(value, step):
    return value if step == 0 else pltpu.roll(value, step % LON, 1)


def dot(left, right):
    return jnp.dot(left, right, preferred_element_type=F32)


def dot_cells(left, right):
    return lax.dot_general(left, right, (((1,), (1,)), ((), ())), preferred_element_type=F32)


def first_row():
    return lax.axis_index(TILE) * ROWS


def inside(base, row):
    row = base + row
    return jnp.where((row >= 0) & (row < NLAT), 1.0, 0.0).astype(F32)


def sigmoid(value):
    return 0.5 * jnp.tanh(0.5 * value) + 0.5


def loop(start, stop, body):
    lax.fori_loop(start, stop, lambda row, carry: (body(row), carry)[1], 0, unroll=True)


def pack_kernel(
    members_in, condition_in, observed_in, own, edge_far, edge_near,
    members, condition, observed, sems,
):
    pairs = [(members_in, members), (condition_in, condition)]
    pairs.append((observed_in.at[HALF:], observed))
    for copy in started(pairs, sems):
        copy.wait()
    for row in range(ROWS):
        own[row, :HALF, :] = members[:HALF, row, :]
        own[row, HALF:INPUTS, :] = condition[:, row, :]
        own[row, INPUTS : INPUTS + HALF, :] = members[HALF:, row, :]
        own[row, INPUTS + HALF : INPUTS + 2 * HALF, :] = observed[:, row, :]
        own[row, FIELDS - 1 :, :] = jnp.zeros((1, LON), F32)
    odd = lax.axis_index("core") == 1
    is_input = lax.broadcasted_iota(jnp.int32, (FIELDS, 1), 0) < INPUTS
    initial = in_parts(own[0], own[1])
    last = in_parts(own[ROWS - 2], own[ROWS - 1])
    for row in range(HALO + 1):
        at = min(row, HALO - 1)
        first = jnp.where(is_input, own[at], initial[row])
        final = jnp.where(is_input, own[ROWS - HALO + at], last[row])
        edge_far[row] = jnp.where(odd, final, first).astype(BF16)
        edge_near[row] = jnp.where(odd, first, final).astype(BF16)


def in_parts(row_a, row_b):
    parts = []
    for value in (row_a, row_b):
        high = value.astype(BF16).astype(F32)
        middle = (value - high).astype(BF16).astype(F32)
        parts.append((high, middle, value - high - middle))
    (high_a, middle_a, low_a), (high_b, middle_b, low_b) = parts
    return [high_a, high_b, middle_a, middle_b, low_a, low_b]


def weights_kernel(
    kernel_in_in, kernel_mid_in, kernel_out_in, w_in, w_mid, w_out, w_back_2, w_back_1,
    kernel_in, kernel_mid, kernel_out, flat_in, square, flat_out, back_2, back_1, held_2, held_1, sems,
):
    pairs = [(kernel_in_in, kernel_in), (kernel_mid_in, kernel_mid), (kernel_out_in, kernel_out)]
    copies = [
        pltpu.make_async_copy(source, target, sems.at[2 + at])
        for at, (source, target) in enumerate(pairs)
    ]
    for copy in copies:
        copy.start()
    flat_out[...] = jnp.zeros_like(flat_out)
    back_2[...] = jnp.zeros_like(back_2)
    for copy in copies:
        copy.wait()
    for tap in range(9):
        a, b = tap // 3, tap % 3
        back = 3 * (2 - a) + b
        first = kernel_in[tap].astype(F32)
        first = jnp.concatenate([first, jnp.zeros((FIELDS - INPUTS, CH), F32)], 0).T
        flat_in[:, tap * FIELDS : (tap + 1) * FIELDS] = first
        mid = kernel_mid[tap].astype(F32)
        square[b * CH : (b + 1) * CH, a * CH : (a + 1) * CH] = mid
        back_1[a * CH : (a + 1) * CH, b * CH : (b + 1) * CH] = mid.T
        out = kernel_out[tap].astype(F32)
        across = slice(a * CH, (a + 1) * CH)
        flat_out[b * 16 : b * 16 + HALF, across] = out[:HALF]
        flat_out[b * 16 + 8 : b * 16 + 8 + HALF, across] = out[HALF:]
        out = jnp.concatenate([out, jnp.zeros((8 - VARS, CH), F32)], 0).T
        back_2[:, back * 16 : back * 16 + HALF] = out[:, :HALF]
        back_2[:, back * 16 + 8 : back * 16 + 8 + HALF] = out[:, HALF:VARS]
    held_2[...] = back_2[...].astype(BF16)
    held_1[...] = back_1[...].astype(BF16)
    copies = [
        pltpu.make_async_copy(held_2, w_back_2, sems.at[0]),
        pltpu.make_async_copy(held_1, w_back_1, sems.at[1]),
    ]
    for copy in copies:
        copy.start()
    w_in[...] = flat_in[...].astype(BF16)
    w_mid[...] = square[...].astype(BF16)
    w_out[...] = flat_out[...].astype(BF16)
    for copy in copies:
        copy.wait()


def forward_kernel(
    far, near, own, members_in, w_in, w_mid, w_out,
    send, pushed, kept_out, stack_out, hidden_1_out, slope_1_out, hidden_2_out, slope_2_out,
    kept, stack, hidden_1, slope_1, hidden_2, slope_2, edges, members, sems,
):
    brought = pltpu.make_async_copy(members_in.at[:HALF], members, sems.at[6])
    brought.start()
    base, odd = first_row(), lax.axis_index("core") == 1
    copies = []

    def keep(source, target):
        copy = pltpu.make_async_copy(source, target, sems.at[len(copies)])
        copy.start()
        copies.append(copy)

    is_input = lax.broadcasted_iota(jnp.int32, (FIELDS, 1), 0) < INPUTS
    for side in range(2):
        got = []
        for row in range(HALO + 1):
            one, other = far[row].astype(F32), near[row].astype(F32)
            got.append(jnp.where(odd == (side == 0), other, one))
        whole = [got[0] + got[2] + got[4], got[1] + got[3] + got[5]]
        for row in range(HALO):
            field = got[row]
            exact = row - (HALO - 2) if side == 0 else row
            if 0 <= exact < 2:
                field = jnp.where(is_input, field, whole[exact])
            edges[side * HALO + row] = field

    def wide(row):
        if row < HALO:
            return edges[row]
        return own[row - HALO] if row < HALO + ROWS else edges[row - ROWS]

    for row in range(ROWS + 2 * HALO):
        field = wide(row)
        for shift in range(3):
            part = turned(field, 1 - shift).astype(BF16)
            stack[row, shift * FIELDS : (shift + 1) * FIELDS, :] = part
    keep(stack.at[4:14], stack_out)

    def first(row, kept_row):
        pre = dot(w_in[...], stack[pl.ds(row, 3)].reshape(9 * FIELDS, LON))
        gate = sigmoid(pre)
        hidden_1[row] = (pre * gate * inside(base, row - 4)).astype(BF16)
        if kept_row:
            slope_1[row - 4] = gate * (1.0 + pre * (1.0 - gate))

    loop(0, 4, functools.partial(first, kept_row=False))
    loop(4, 12, functools.partial(first, kept_row=True))
    loop(12, 16, functools.partial(first, kept_row=False))
    keep(hidden_1.at[3:13], hidden_1_out)
    keep(slope_1, slope_1_out)

    def second(row, kept_row):
        part = dot(w_mid[...], hidden_1[pl.ds(row, 3)].reshape(3 * CH, LON))
        pre = turned(part[:CH], 1) + part[CH : 2 * CH] + turned(part[2 * CH :], -1)
        gate = sigmoid(pre)
        hidden_2[row] = (pre * gate * inside(base, row - 3)).astype(BF16)
        if kept_row:
            slope_2[row - 2] = gate * (1.0 + pre * (1.0 - gate))

    loop(0, 2, functools.partial(second, kept_row=False))
    loop(2, 12, functools.partial(second, kept_row=True))
    loop(12, 14, functools.partial(second, kept_row=False))
    keep(hidden_2.at[2:12], hidden_2_out)
    keep(slope_2, slope_2_out)

    brought.wait()
    send[OWN:FAR_AT, :] = members[...].reshape(OWN, LON)
    for row in range(ROWS + 4):
        part = dot(w_out[...], hidden_2[row : row + 3].reshape(3 * CH, LON))
        both = turned(part[:16], 1) + part[16:32] + turned(part[32:], -1)
        log_scale = jnp.tanh(both[:HALF])
        field = wide(row + 3)
        moving = field[INPUTS : INPUTS + HALF]
        moved = moving * jnp.exp(log_scale) + both[8 : 8 + HALF]
        here = slice(row * HALF, (row + 1) * HALF)
        kept[0, here, :] = log_scale
        kept[1, here, :] = moving
        kept[2, here, :] = field[INPUTS + HALF : INPUTS + 2 * HALF]
        kept[3, here, :] = moved
        if 2 <= row < 2 + ROWS:
            send[(row - 2) * HALF : (row - 1) * HALF, :] = moved
            for var in range(HALF):
                pushed[HALF + var, row - 2 : row - 1, :] = moved[var : var + 1]
    keep(kept, kept_out)
    far_rows = jnp.where(odd, kept[3, WIDE - NEAR :, :], kept[3, :NEAR, :])
    send[FAR_AT:, :] = jnp.concatenate([far_rows, jnp.zeros((SENT - FAR_AT - NEAR, LON), F32)], 0)
    pushed[:HALF] = members[...]
    for copy in copies:
        copy.wait()


def folded(value):
    return sum(value[..., at : at + 128] for at in range(0, LON, 128))


def distance_kernel(lat, members, observed, fields, kept, swapped):
    me, odd = lax.axis_index("member"), lax.axis_index("core") == 1
    upper_lat = lat[NEAR : NEAR + OWN, :1]
    lower_lat = jnp.concatenate([lat[LAT_AT:, :1]] * HALF, 0)
    fixed_mine = members[:HALF].reshape(OWN, LON)
    mine = kept[3, NEAR : NEAR + OWN, :]

    def weighed(moved, fixed):
        upper = jnp.sum(folded(upper_lat * (mine - moved) ** 2), 0, keepdims=True)
        lower = jnp.sum(folded(lower_lat * (fixed_mine - fixed) ** 2), 0, keepdims=True)
        return upper + lower

    seen = kept[2, NEAR : NEAR + OWN, :]
    to_observed = weighed(seen, observed[:HALF].reshape(OWN, LON))
    rows = []
    for n in range(MEMBERS):
        first, last = fields[n, :NEAR], fields[n, OWN - NEAR : OWN]
        swapped[n * NEAR : (n + 1) * NEAR, :] = jnp.where(odd, first, last)
        rows.append(weighed(fields[n, :OWN], fields[n, OWN:FAR_AT]))
    all_rows = jnp.concatenate(rows, 0)
    spot = lax.broadcasted_iota(jnp.int32, (MEMBERS, 128), 0)
    swapped[MEMBERS * NEAR :, :128] = jnp.where(spot == me, to_observed, all_rows)
    swapped[MEMBERS * NEAR :, 128:] = jnp.zeros((MEMBERS, LON - 128), F32)


def started(pairs, sems):
    copies = [
        pltpu.make_async_copy(source, target, sems.at[at])
        for at, (source, target) in enumerate(pairs)
    ]
    for copy in copies:
        copy.start()
    return copies


def backward_kernel(
    lat, totals, near, fields_in, kept_in, stack_in, hidden_1_in, slope_1_in, hidden_2_in,
    slope_2_in, w_back_2_in, w_back_1_in,
    mine, theirs,
    fields, kept, stack, hidden_1, slope_1, hidden_2, slope_2, w_back_2, w_back_1,
    coupled, turned_2, by_row, sum_out, sum_mid, sum_in, packed, sems,
):
    sources = [kept_in, fields_in, w_back_2_in, slope_2_in]
    sources += [w_back_1_in, hidden_1_in, hidden_2_in, slope_1_in, stack_in]
    targets = [kept, fields, w_back_2, slope_2]
    targets += [w_back_1, hidden_1, hidden_2, slope_1, stack]
    copies = started(list(zip(sources, targets)), sems)
    me, base, core = lax.axis_index("member"), first_row(), lax.axis_index("core")
    sum_out[...] = jnp.zeros_like(sum_out)
    sum_mid[...] = jnp.zeros_like(sum_mid)
    sum_in[...] = jnp.zeros_like(sum_in)
    total = totals[0]
    for tile in range(1, RING):
        total = total + totals[tile]
    distances = jnp.sqrt(jnp.sum(total, 1, keepdims=True) / ENTRIES + EPSILON)
    is_me = lax.broadcasted_iota(jnp.int32, (MEMBERS, 1), 0) == me
    shares = jnp.where(is_me, distances / MEMBERS, -distances / (2.0 * MEMBERS * MEMBERS))
    share = jnp.sum(shares, 0, keepdims=True) / TILES
    weights = 1.0 / (jnp.where(is_me, MEMBERS, MEMBERS * MEMBERS) * distances)
    own_weight = jnp.sum(jnp.where(is_me, weights, 0.0), 0, keepdims=True)
    weights = jnp.where(is_me, 0.0, weights)
    copies[0].wait()
    log_scale, moving, observed, moved = kept[0], kept[1], kept[2], kept[3]
    inner = (moved - observed) * own_weight
    copies[1].wait()
    odd = core == 1
    first, last = moved[:NEAR], moved[WIDE - NEAR :]
    near_mine, far_mine = jnp.where(odd, first, last), jnp.where(odd, last, first)
    own_sum = jnp.zeros((OWN, LON), F32)
    near_sum = jnp.zeros((NEAR, LON), F32)
    far_sum = near_sum
    for n in range(MEMBERS):
        weight = weights[n : n + 1]
        own_sum += weight * (moved[NEAR : NEAR + OWN] - fields[n, :OWN])
        near_sum += weight * (near_mine - near[n * NEAR : (n + 1) * NEAR])
        far_sum += weight * (far_mine - fields[n, FAR_AT : FAR_AT + NEAR])
    first, last = jnp.where(odd, near_sum, far_sum), jnp.where(odd, far_sum, near_sum)
    inner = inner - jnp.concatenate([first, own_sum, last], 0)
    upper = lat[:WIDE, :1] * inner / math.sqrt(ENTRIES)
    scaled = upper * moving * jnp.exp(log_scale) * (1.0 - log_scale * log_scale)
    blank = jnp.zeros((8 - HALF, LON), F32)
    for row in range(ROWS + 4):
        here = slice(row * HALF, (row + 1) * HALF)
        field = jnp.concatenate([scaled[here], blank, upper[here], blank], 0)
        for shift in range(3):
            part = turned(field, shift - 1).astype(BF16)
            coupled[row, shift * 16 : (shift + 1) * 16, :] = part
    copies[2].wait()
    copies[3].wait()

    def second(row):
        back = dot(w_back_2[...], coupled[pl.ds(row, 3)].reshape(144, LON))
        grad = back * slope_2[row] * inside(base, row - 1)
        for shift in range(3):
            part = turned(grad, shift - 1).astype(BF16)
            turned_2[row, shift * CH : (shift + 1) * CH, :] = part

    loop(0, ROWS + 2, second)
    copies[4].wait()

    def across_rows(row):
        by_row[row] = dot(w_back_1[...], turned_2[row])

    loop(0, ROWS + 2, across_rows)
    copies[5].wait()

    def middle(row):
        near = hidden_1[pl.ds(row, 3)].reshape(3 * CH, LON)
        sum_mid[...] += dot_cells(turned_2[row + 1], near)

    loop(0, ROWS, middle)
    copies[6].wait()

    def outer(row):
        near = hidden_2[pl.ds(row, 3)].reshape(3 * CH, LON)
        sum_out[...] += dot_cells(coupled[row + 2], near)

    loop(0, ROWS, outer)
    copies[7].wait()
    copies[8].wait()

    def last(row):
        back = by_row[row + 2, :CH] + by_row[row + 1, CH : 2 * CH] + by_row[row, 2 * CH :]
        grad = (back * slope_1[row]).astype(BF16)
        near = stack[pl.ds(row, 3)].reshape(9 * FIELDS, LON)
        sum_in[...] += dot_cells(near, grad)

    loop(0, ROWS, last)
    packed[5 * CH :, :] = jnp.zeros((CH, 128), F32)
    packed[4 * CH : 5 * CH, CH:] = jnp.zeros((CH, CH), F32)
    for tap in range(9):
        a, b = tap // 3, tap % 3
        at, side = place_mid(tap)
        packed[at : at + CH, side] = sum_mid[b * CH : (b + 1) * CH, a * CH : (a + 1) * CH]
        at = 5 * CH + tap * VARS
        across = slice(a * CH, (a + 1) * CH)
        packed[at : at + HALF, :CH] = sum_out[b * 16 : b * 16 + HALF, across]
        packed[at + HALF : at + VARS, :CH] = sum_out[b * 16 + 8 : b * 16 + 8 + HALF, across]
        at = 4 * CH + tap * INPUTS
        packed[at : at + INPUTS, CH:] = sum_in[tap * FIELDS : tap * FIELDS + INPUTS]
    packed[6 * CH - 1 :, 127:] = share
    half = MEMBERS * CHUNK
    for copy in range(2):

        @pl.when(core == copy)
        def _():
            mine[...] = packed[copy * half : (copy + 1) * half, :]
            theirs[...] = packed[(1 - copy) * half : (2 - copy) * half, :]


def place_mid(tap):
    return (tap * CH, slice(0, CH)) if tap < 5 else ((tap - 5) * CH, slice(CH, 2 * CH))


def unpack_kernel(chunks, grad_in, grad_mid, grad_out, energy, packed):
    for member in range(MEMBERS):
        for half in range(2):
            at = (half * MEMBERS + member) * CHUNK
            packed[at : at + CHUNK, :] = chunks[member * 2 + half]
    for tap in range(9):
        at, side = place_mid(tap)
        grad_mid[tap] = packed[at : at + CH, side]
        at = 5 * CH + tap * VARS
        grad_out[tap] = packed[at : at + VARS, :CH]
        at = 4 * CH + tap * INPUTS
        grad_in[tap] = packed[at : at + INPUTS, CH:]
    energy[...] = packed[6 * CH - 1 :, 127:]


VMEM_LIMIT = 28 * 10**6
VMEM = pl.BlockSpec(memory_space=pltpu.VMEM)
HBM = pl.BlockSpec(memory_space=pltpu.HBM)


def call(kernel, ins, outs, scratch=(), copies=0, flops=10**6, vmem=VMEM_LIMIT):
    held = [pltpu.VMEM(shape, dtype) for shape, dtype in scratch]
    if copies > 0:
        held.append(pltpu.SemaphoreType.DMA((copies,)))
    shapes = [
        pltpu.HBM(shape, dtype) if spec is HBM else jax.ShapeDtypeStruct(shape, dtype)
        for shape, dtype, spec in outs
    ]
    run = pl.pallas_call(
        kernel,
        out_shape=shapes,
        in_specs=ins,
        out_specs=[spec for shape, dtype, spec in outs],
        scratch_shapes=held,
        compiler_params=pltpu.CompilerParams(vmem_limit_bytes=vmem),
        cost_estimate=pl.CostEstimate(flops=flops, bytes_accessed=10**6, transcendentals=0),
    )

    def placed(*arrays):
        return run(
            *[
                pltpu.with_memory_space_constraint(array, pltpu.HBM) if spec is HBM else array
                for array, spec in zip(arrays, ins)
            ]
        )

    return placed


def per_device(members, condition, observed, kernel_in, kernel_mid, kernel_out):
    members = members[0]
    tile = lax.axis_index(TILE)
    table = jnp.asarray(lat_table())
    lat = lax.dynamic_slice_in_dim(table, tile, 1, 0)[0]
    lat = jnp.broadcast_to(lat[:, None], (LAT_AT + ROWS, 128))
    edge = ((HALO + 1, FIELDS, LON), BF16, VMEM)
    own, edge_far, edge_near = call(
        pack_kernel,
        [HBM] * 3,
        [((ROWS, FIELDS, LON), F32, VMEM), edge, edge],
        [((VARS, ROWS, LON), F32), ((COND, ROWS, LON), F32), ((HALF, ROWS, LON), F32)],
        copies=3,
    )(members, condition, observed)
    across = [(i, i + 1) for i in range(1, TILES - 1, 2)]
    far = lax.ppermute(edge_far, TILE, across + [(j, i) for i, j in across])
    near = lax.ppermute(edge_near, "core", [(0, 1), (1, 0)])
    near, lat = lax.optimization_barrier((near, lat))
    w_shapes = [(CH, 9 * FIELDS), (3 * CH, 3 * CH), (48, 3 * CH), (CH, 144), (3 * CH, 3 * CH)]
    w_in, w_mid, w_out, w_back_2, w_back_1 = call(
        weights_kernel,
        [HBM] * 3,
        [(shape, BF16, VMEM) for shape in w_shapes[:3]]
        + [(shape, BF16, HBM) for shape in w_shapes[3:]],
        [((9, INPUTS, CH), BF16), ((9, CH, CH), BF16), ((9, VARS, CH), BF16)]
        + [(shape, F32) for shape in w_shapes]
        + [(shape, BF16) for shape in w_shapes[3:]],
        copies=5,
    )(kernel_in.transpose(0, 2, 1), kernel_mid, kernel_out)
    saved = [
        ((ROWS + 2, 3 * FIELDS, LON), BF16),
        ((ROWS + 2, CH, LON), BF16),
        ((ROWS, CH, LON), F32),
        ((ROWS + 2, CH, LON), BF16),
        ((ROWS + 2, CH, LON), F32),
    ]
    worked = [
        ((ROWS + 10, 3 * FIELDS, LON), BF16),
        ((ROWS + 8, CH, LON), BF16),
        ((ROWS, CH, LON), F32),
        ((ROWS + 6, CH, LON), BF16),
        ((ROWS + 2, CH, LON), F32),
    ]
    kept_shape = ((4, WIDE, LON), F32)
    send, pushed, kept, stack, hidden_1, slope_1, hidden_2, slope_2 = call(
        forward_kernel,
        [VMEM] * 3 + [HBM] + [VMEM] * 3,
        [((SENT, LON), F32, VMEM), ((VARS, ROWS, LON), F32, VMEM), kept_shape + (HBM,)]
        + [shape + (HBM,) for shape in saved],
        [kept_shape] + worked
        + [((2 * HALO, FIELDS, LON), F32), ((HALF, ROWS, LON), F32)],
        copies=7,
        flops=10**9,
    )(far, near, own, members, w_in, w_mid, w_out)
    fields = spread(send, "member", MEMBERS)
    fields_shape = ((MEMBERS, SENT, LON), F32)
    (swapped,) = call(
        distance_kernel,
        [VMEM] * 5,
        [((MEMBERS * (NEAR + 1), LON), F32, VMEM)],
        vmem=8 * 10**6,
    )(lat, members, observed, fields, kept)
    swap = [(0, 1), (1, 0)]
    beside = lax.ppermute(swapped, "core", swap)
    partials = swapped[MEMBERS * NEAR :, :128] + beside[MEMBERS * NEAR :, :128]
    totals = spread(partials, "ring", RING)
    mine, theirs = call(
        backward_kernel,
        [VMEM] * 3 + [HBM] * 9,
        [((MEMBERS * CHUNK, 128), F32, VMEM)] * 2,
        [fields_shape, kept_shape]
        + saved
        + [(shape, BF16) for shape in w_shapes[3:]]
        + [
            ((ROWS + 4, 48, LON), BF16),
            ((ROWS + 2, 3 * CH, LON), BF16),
            ((ROWS + 2, 3 * CH, LON), F32),
            ((48, 3 * CH), F32),
            ((3 * CH, 3 * CH), F32),
            ((9 * FIELDS, CH), F32),
            ((6 * CH, 128), F32),
        ],
        copies=9,
        flops=10**9,
    )(
        lat, totals, beside, fields, kept, stack, hidden_1, slope_1, hidden_2, slope_2,
        w_back_2, w_back_1,
    )
    mine = mine + lax.ppermute(theirs, "core", swap)
    chunk = jnp.sum(lax.all_to_all(mine.reshape(MEMBERS, CHUNK, 128), "member", 0, 0), 0)
    chunk = jnp.sum(spread(chunk, "ring", RING), 0)
    chunks = spread(chunk, ("member", "core"), 2 * MEMBERS)
    grad_in, grad_mid, grad_out, energy = call(
        unpack_kernel,
        [VMEM],
        [
            ((9, INPUTS, CH), F32, VMEM),
            ((9, CH, CH), F32, VMEM),
            ((9, VARS, CH), F32, VMEM),
            ((1, 1), F32, VMEM),
        ],
        [((6 * CH, 128), F32)],
        vmem=16 * 10**6,
    )(chunks)
    return (pushed[None], energy[0, 0], grad_in.transpose(0, 2, 1), grad_mid, grad_out)


def solution(mesh):
    fine = Mesh(mesh.devices.reshape(MEMBERS, -1, 2), ("member",) + TILE)
    in_specs = (
        P("member", None, TILE, None),
        P(None, TILE, None),
        P(None, TILE, None),
        P(),
        P(),
        P(),
    )
    out_specs = (P("member", None, TILE, None), P(), P(), P(), P())
    return jax.shard_map(
        per_device, mesh=fine, in_specs=in_specs, out_specs=out_specs, check_vma=False
    )
```

```python
import functools
import math

import jax
import jax.numpy as jnp
import numpy as np
from jax import lax
from jax.experimental import pallas as pl
from jax.experimental.pallas import tpu as pltpu
from jax.sharding import Mesh, PartitionSpec as P

EPSILON = 1e-06
MEMBERS, NLAT, LON, ROWS = 8, 256, 512, 8
VARS, HALF, COND, CH = 6, 3, 6, 64
TILES, RING = 32, 16
ENTRIES = VARS * NLAT * LON
HALO = 5
FIELDS = 16
INPUTS = HALF + COND
WIDE = (ROWS + 4) * HALF
LAT_AT = 40
OWN = ROWS * HALF
FAR_AT = 2 * OWN
NEAR = 2 * HALF
SENT = 56
CHUNK = 24
TILE = ("ring", "core")
F32, BF16 = jnp.float32, jnp.bfloat16


def spread(value, axes, count):
    copies = jnp.broadcast_to(value[None], (count,) + value.shape)
    return lax.all_to_all(copies, axes, 0, 0)


def lat_table():
    rows = np.arange(NLAT)
    cosine = np.cos((-90.0 + 180.0 * (rows + 0.5) / NLAT) * (np.pi / 180.0))
    lat = (cosine / cosine.mean()).astype(np.float32)
    padded = np.pad(lat, (2, 2))
    table = np.zeros((TILES, LAT_AT + ROWS), np.float32)
    for tile in range(TILES):
        wide = padded[tile * ROWS : tile * ROWS + ROWS + 4]
        table[tile, :WIDE] = np.repeat(wide, HALF)
        table[tile, LAT_AT:] = lat[tile * ROWS : (tile + 1) * ROWS]
    return table


def turned(value, step):
    return value if step == 0 else pltpu.roll(value, step % LON, 1)


def dot(left, right):
    return jnp.dot(left, right, preferred_element_type=F32)


def dot_cells(left, right):
    return lax.dot_general(left, right, (((1,), (1,)), ((), ())), preferred_element_type=F32)


def first_row():
    return lax.axis_index(TILE) * ROWS


def inside(base, row):
    row = base + row
    return jnp.where((row >= 0) & (row < NLAT), 1.0, 0.0).astype(F32)


def sigmoid(value):
    return 0.5 * jnp.tanh(0.5 * value) + 0.5


def loop(start, stop, body):
    lax.fori_loop(start, stop, lambda row, carry: (body(row), carry)[1], 0, unroll=True)


def pack_kernel(
    members_in, condition_in, observed_in, own, edge_far, edge_near,
    members, condition, observed, sems,
):
    pairs = [(members_in, members), (condition_in, condition)]
    pairs.append((observed_in.at[HALF:], observed))
    for copy in started(pairs, sems):
        copy.wait()
    for row in range(ROWS):
        own[row, :HALF, :] = members[:HALF, row, :]
        own[row, HALF:INPUTS, :] = condition[:, row, :]
        own[row, INPUTS : INPUTS + HALF, :] = members[HALF:, row, :]
        own[row, INPUTS + HALF : INPUTS + 2 * HALF, :] = observed[:, row, :]
        own[row, FIELDS - 1 :, :] = jnp.zeros((1, LON), F32)
    odd = lax.axis_index("core") == 1
    is_input = lax.broadcasted_iota(jnp.int32, (FIELDS, 1), 0) < INPUTS
    initial = in_parts(own[0], own[1])
    last = in_parts(own[ROWS - 2], own[ROWS - 1])
    for row in range(HALO + 1):
        at = min(row, HALO - 1)
        first = jnp.where(is_input, own[at], initial[row])
        final = jnp.where(is_input, own[ROWS - HALO + at], last[row])
        edge_far[row] = jnp.where(odd, final, first).astype(BF16)
        edge_near[row] = jnp.where(odd, first, final).astype(BF16)


def in_parts(row_a, row_b):
    parts = []
    for value in (row_a, row_b):
        high = value.astype(BF16).astype(F32)
        middle = (value - high).astype(BF16).astype(F32)
        parts.append((high, middle, value - high - middle))
    (high_a, middle_a, low_a), (high_b, middle_b, low_b) = parts
    return [high_a, high_b, middle_a, middle_b, low_a, low_b]


def weights_kernel(
    kernel_in_in, kernel_mid_in, kernel_out_in, w_in, w_mid, w_out, w_back_2, w_back_1,
    kernel_in, kernel_mid, kernel_out, flat_in, square, flat_out, back_2, back_1, held_2, held_1, sems,
):
    pairs = [(kernel_in_in, kernel_in), (kernel_mid_in, kernel_mid), (kernel_out_in, kernel_out)]
    copies = [
        pltpu.make_async_copy(source, target, sems.at[2 + at])
        for at, (source, target) in enumerate(pairs)
    ]
    for copy in copies:
        copy.start()
    flat_out[...] = jnp.zeros_like(flat_out)
    back_2[...] = jnp.zeros_like(back_2)
    for copy in copies:
        copy.wait()
    for tap in range(9):
        a, b = tap // 3, tap % 3
        back = 3 * (2 - a) + b
        first = kernel_in[tap].astype(F32)
        first = jnp.concatenate([first, jnp.zeros((FIELDS - INPUTS, CH), F32)], 0).T
        flat_in[:, tap * FIELDS : (tap + 1) * FIELDS] = first
        mid = kernel_mid[tap].astype(F32)
        square[b * CH : (b + 1) * CH, a * CH : (a + 1) * CH] = mid
        back_1[a * CH : (a + 1) * CH, b * CH : (b + 1) * CH] = mid.T
        out = kernel_out[tap].astype(F32)
        across = slice(a * CH, (a + 1) * CH)
        flat_out[b * 16 : b * 16 + HALF, across] = out[:HALF]
        flat_out[b * 16 + 8 : b * 16 + 8 + HALF, across] = out[HALF:]
        out = jnp.concatenate([out, jnp.zeros((8 - VARS, CH), F32)], 0).T
        back_2[:, back * 16 : back * 16 + HALF] = out[:, :HALF]
        back_2[:, back * 16 + 8 : back * 16 + 8 + HALF] = out[:, HALF:VARS]
    held_2[...] = back_2[...].astype(BF16)
    held_1[...] = back_1[...].astype(BF16)
    copies = [
        pltpu.make_async_copy(held_2, w_back_2, sems.at[0]),
        pltpu.make_async_copy(held_1, w_back_1, sems.at[1]),
    ]
    for copy in copies:
        copy.start()
    w_in[...] = flat_in[...].astype(BF16)
    w_mid[...] = square[...].astype(BF16)
    w_out[...] = flat_out[...].astype(BF16)
    for copy in copies:
        copy.wait()


def forward_kernel(
    far, near, own, members_in, w_in, w_mid, w_out,
    send, pushed, kept, stack, hidden_1, slope_1, hidden_2, slope_2, edges, members, sems,
):
    brought = pltpu.make_async_copy(members_in.at[:HALF], members, sems.at[0])
    brought.start()
    base, odd = first_row(), lax.axis_index("core") == 1
    is_input = lax.broadcasted_iota(jnp.int32, (FIELDS, 1), 0) < INPUTS
    for side in range(2):
        got = []
        for row in range(HALO + 1):
            one, other = far[row].astype(F32), near[row].astype(F32)
            got.append(jnp.where(odd == (side == 0), other, one))
        whole = [got[0] + got[2] + got[4], got[1] + got[3] + got[5]]
        for row in range(HALO):
            field = got[row]
            exact = row - (HALO - 2) if side == 0 else row
            if 0 <= exact < 2:
                field = jnp.where(is_input, field, whole[exact])
            edges[side * HALO + row] = field

    def wide(row):
        if row < HALO:
            return edges[row]
        return own[row - HALO] if row < HALO + ROWS else edges[row - ROWS]

    for row in range(ROWS + 2 * HALO):
        field = wide(row)
        for shift in range(3):
            part = turned(field, 1 - shift).astype(BF16)
            stack[row, shift * FIELDS : (shift + 1) * FIELDS, :] = part

    def first(row, kept_row):
        pre = dot(w_in[...], stack[pl.ds(row, 3)].reshape(9 * FIELDS, LON))
        gate = sigmoid(pre)
        hidden_1[row] = (pre * gate * inside(base, row - 4)).astype(BF16)
        if kept_row:
            slope_1[row - 4] = gate * (1.0 + pre * (1.0 - gate))

    loop(0, 4, functools.partial(first, kept_row=False))
    loop(4, 12, functools.partial(first, kept_row=True))
    loop(12, 16, functools.partial(first, kept_row=False))

    def second(row, kept_row):
        part = dot(w_mid[...], hidden_1[pl.ds(row, 3)].reshape(3 * CH, LON))
        pre = turned(part[:CH], 1) + part[CH : 2 * CH] + turned(part[2 * CH :], -1)
        gate = sigmoid(pre)
        hidden_2[row] = (pre * gate * inside(base, row - 3)).astype(BF16)
        if kept_row:
            slope_2[row - 2] = gate * (1.0 + pre * (1.0 - gate))

    loop(0, 2, functools.partial(second, kept_row=False))
    loop(2, 12, functools.partial(second, kept_row=True))
    loop(12, 14, functools.partial(second, kept_row=False))

    brought.wait()
    send[OWN:FAR_AT, :] = members[...].reshape(OWN, LON)
    for row in range(ROWS + 4):
        part = dot(w_out[...], hidden_2[row : row + 3].reshape(3 * CH, LON))
        both = turned(part[:16], 1) + part[16:32] + turned(part[32:], -1)
        log_scale = jnp.tanh(both[:HALF])
        field = wide(row + 3)
        moving = field[INPUTS : INPUTS + HALF]
        moved = moving * jnp.exp(log_scale) + both[8 : 8 + HALF]
        here = slice(row * HALF, (row + 1) * HALF)
        kept[0, here, :] = log_scale
        kept[1, here, :] = moving
        kept[2, here, :] = field[INPUTS + HALF : INPUTS + 2 * HALF]
        kept[3, here, :] = moved
        if 2 <= row < 2 + ROWS:
            send[(row - 2) * HALF : (row - 1) * HALF, :] = moved
            for var in range(HALF):
                pushed[HALF + var, row - 2 : row - 1, :] = moved[var : var + 1]
    far_rows = jnp.where(odd, kept[3, WIDE - NEAR :, :], kept[3, :NEAR, :])
    send[FAR_AT:, :] = jnp.concatenate([far_rows, jnp.zeros((SENT - FAR_AT - NEAR, LON), F32)], 0)
    pushed[:HALF] = members[...]


def folded(value):
    return sum(value[..., at : at + 128] for at in range(0, LON, 128))


def distance_kernel(lat, members, observed, fields, kept, swapped):
    me, odd = lax.axis_index("member"), lax.axis_index("core") == 1
    upper_lat = lat[NEAR : NEAR + OWN, :1]
    lower_lat = jnp.concatenate([lat[LAT_AT:, :1]] * HALF, 0)
    fixed_mine = members[:HALF].reshape(OWN, LON)
    mine = kept[3, NEAR : NEAR + OWN, :]

    def weighed(moved, fixed):
        upper = jnp.sum(folded(upper_lat * (mine - moved) ** 2), 0, keepdims=True)
        lower = jnp.sum(folded(lower_lat * (fixed_mine - fixed) ** 2), 0, keepdims=True)
        return upper + lower

    seen = kept[2, NEAR : NEAR + OWN, :]
    to_observed = weighed(seen, observed[:HALF].reshape(OWN, LON))
    rows = []
    for n in range(MEMBERS):
        first, last = fields[n, :NEAR], fields[n, OWN - NEAR : OWN]
        swapped[n * NEAR : (n + 1) * NEAR, :] = jnp.where(odd, first, last)
        rows.append(weighed(fields[n, :OWN], fields[n, OWN:FAR_AT]))
    all_rows = jnp.concatenate(rows, 0)
    spot = lax.broadcasted_iota(jnp.int32, (MEMBERS, 128), 0)
    swapped[MEMBERS * NEAR :, :128] = jnp.where(spot == me, to_observed, all_rows)
    swapped[MEMBERS * NEAR :, 128:] = jnp.zeros((MEMBERS, LON - 128), F32)


def started(pairs, sems):
    copies = [
        pltpu.make_async_copy(source, target, sems.at[at])
        for at, (source, target) in enumerate(pairs)
    ]
    for copy in copies:
        copy.start()
    return copies


def backward_kernel(
    lat, totals, near, fields, kept, stack, hidden_1, slope_1, hidden_2, slope_2, w_back_2_in, w_back_1_in,
    mine, theirs,
    w_back_2, w_back_1,
    coupled, turned_2, by_row, sum_out, sum_mid, sum_in, packed, sems,
):
    copies = started([(w_back_2_in, w_back_2), (w_back_1_in, w_back_1)], sems)
    me, base, core = lax.axis_index("member"), first_row(), lax.axis_index("core")
    sum_out[...] = jnp.zeros_like(sum_out)
    sum_mid[...] = jnp.zeros_like(sum_mid)
    sum_in[...] = jnp.zeros_like(sum_in)
    total = totals[0]
    for tile in range(1, RING):
        total = total + totals[tile]
    distances = jnp.sqrt(jnp.sum(total, 1, keepdims=True) / ENTRIES + EPSILON)
    is_me = lax.broadcasted_iota(jnp.int32, (MEMBERS, 1), 0) == me
    shares = jnp.where(is_me, distances / MEMBERS, -distances / (2.0 * MEMBERS * MEMBERS))
    share = jnp.sum(shares, 0, keepdims=True) / TILES
    weights = 1.0 / (jnp.where(is_me, MEMBERS, MEMBERS * MEMBERS) * distances)
    own_weight = jnp.sum(jnp.where(is_me, weights, 0.0), 0, keepdims=True)
    weights = jnp.where(is_me, 0.0, weights)
    log_scale, moving, observed, moved = kept[0], kept[1], kept[2], kept[3]
    inner = (moved - observed) * own_weight
    odd = core == 1
    first, last = moved[:NEAR], moved[WIDE - NEAR :]
    near_mine, far_mine = jnp.where(odd, first, last), jnp.where(odd, last, first)
    own_sum = jnp.zeros((OWN, LON), F32)
    near_sum = jnp.zeros((NEAR, LON), F32)
    far_sum = near_sum
    for n in range(MEMBERS):
        weight = weights[n : n + 1]
        own_sum += weight * (moved[NEAR : NEAR + OWN] - fields[n, :OWN])
        near_sum += weight * (near_mine - near[n * NEAR : (n + 1) * NEAR])
        far_sum += weight * (far_mine - fields[n, FAR_AT : FAR_AT + NEAR])
    first, last = jnp.where(odd, near_sum, far_sum), jnp.where(odd, far_sum, near_sum)
    inner = inner - jnp.concatenate([first, own_sum, last], 0)
    upper = lat[:WIDE, :1] * inner / math.sqrt(ENTRIES)
    scaled = upper * moving * jnp.exp(log_scale) * (1.0 - log_scale * log_scale)
    blank = jnp.zeros((8 - HALF, LON), F32)
    for row in range(ROWS + 4):
        here = slice(row * HALF, (row + 1) * HALF)
        field = jnp.concatenate([scaled[here], blank, upper[here], blank], 0)
        for shift in range(3):
            part = turned(field, shift - 1).astype(BF16)
            coupled[row, shift * 16 : (shift + 1) * 16, :] = part
    copies[0].wait()

    def second(row):
        back = dot(w_back_2[...], coupled[pl.ds(row, 3)].reshape(144, LON))
        grad = back * slope_2[row] * inside(base, row - 1)
        for shift in range(3):
            part = turned(grad, shift - 1).astype(BF16)
            turned_2[row, shift * CH : (shift + 1) * CH, :] = part

    loop(0, ROWS + 2, second)
    copies[1].wait()

    def across_rows(row):
        by_row[row] = dot(w_back_1[...], turned_2[row])

    loop(0, ROWS + 2, across_rows)

    def middle(row):
        near = hidden_1[pl.ds(row + 3, 3)].reshape(3 * CH, LON)
        sum_mid[...] += dot_cells(turned_2[row + 1], near)

    loop(0, ROWS, middle)

    def outer(row):
        near = hidden_2[pl.ds(row + 2, 3)].reshape(3 * CH, LON)
        sum_out[...] += dot_cells(coupled[row + 2], near)

    loop(0, ROWS, outer)

    def last(row):
        back = by_row[row + 2, :CH] + by_row[row + 1, CH : 2 * CH] + by_row[row, 2 * CH :]
        grad = (back * slope_1[row]).astype(BF16)
        near = stack[pl.ds(row + 4, 3)].reshape(9 * FIELDS, LON)
        sum_in[...] += dot_cells(near, grad)

    loop(0, ROWS, last)
    packed[5 * CH :, :] = jnp.zeros((CH, 128), F32)
    packed[4 * CH : 5 * CH, CH:] = jnp.zeros((CH, CH), F32)
    for tap in range(9):
        a, b = tap // 3, tap % 3
        at, side = place_mid(tap)
        packed[at : at + CH, side] = sum_mid[b * CH : (b + 1) * CH, a * CH : (a + 1) * CH]
        at = 5 * CH + tap * VARS
        across = slice(a * CH, (a + 1) * CH)
        packed[at : at + HALF, :CH] = sum_out[b * 16 : b * 16 + HALF, across]
        packed[at + HALF : at + VARS, :CH] = sum_out[b * 16 + 8 : b * 16 + 8 + HALF, across]
        at = 4 * CH + tap * INPUTS
        packed[at : at + INPUTS, CH:] = sum_in[tap * FIELDS : tap * FIELDS + INPUTS]
    packed[6 * CH - 1 :, 127:] = share
    half = MEMBERS * CHUNK
    for copy in range(2):

        @pl.when(core == copy)
        def _():
            mine[...] = packed[copy * half : (copy + 1) * half, :]
            theirs[...] = packed[(1 - copy) * half : (2 - copy) * half, :]


def place_mid(tap):
    return (tap * CH, slice(0, CH)) if tap < 5 else ((tap - 5) * CH, slice(CH, 2 * CH))


def unpack_kernel(chunks, grad_in, grad_mid, grad_out, energy, packed):
    core = lax.axis_index("core")
    for member in range(MEMBERS):
        first, second = chunks[member, 0], chunks[member, 1]
        at = member * CHUNK
        packed[at : at + CHUNK, :] = jnp.where(core == 0, first, second)
        at += MEMBERS * CHUNK
        packed[at : at + CHUNK, :] = jnp.where(core == 0, second, first)
    for tap in range(9):
        at, side = place_mid(tap)
        grad_mid[tap] = packed[at : at + CH, side]
        at = 5 * CH + tap * VARS
        grad_out[tap] = packed[at : at + VARS, :CH]
        at = 4 * CH + tap * INPUTS
        grad_in[tap] = packed[at : at + INPUTS, CH:]
    energy[...] = packed[6 * CH - 1 :, 127:]


VMEM_LIMIT = 28 * 10**6
VMEM = pl.BlockSpec(memory_space=pltpu.VMEM)
HBM = pl.BlockSpec(memory_space=pltpu.HBM)


def call(kernel, ins, outs, scratch=(), copies=0, flops=10**6, vmem=VMEM_LIMIT):
    held = [pltpu.VMEM(shape, dtype) for shape, dtype in scratch]
    if copies > 0:
        held.append(pltpu.SemaphoreType.DMA((copies,)))
    shapes = [
        pltpu.HBM(shape, dtype) if spec is HBM else jax.ShapeDtypeStruct(shape, dtype)
        for shape, dtype, spec in outs
    ]
    run = pl.pallas_call(
        kernel,
        out_shape=shapes,
        in_specs=ins,
        out_specs=[spec for shape, dtype, spec in outs],
        scratch_shapes=held,
        compiler_params=pltpu.CompilerParams(vmem_limit_bytes=vmem),
        cost_estimate=pl.CostEstimate(flops=flops, bytes_accessed=10**6, transcendentals=0),
    )

    def placed(*arrays):
        return run(
            *[
                pltpu.with_memory_space_constraint(array, pltpu.HBM) if spec is HBM else array
                for array, spec in zip(arrays, ins)
            ]
        )

    return placed


def per_device(members, condition, observed, kernel_in, kernel_mid, kernel_out):
    members = members[0]
    tile = lax.axis_index(TILE)
    table = jnp.asarray(lat_table())
    lat = lax.dynamic_slice_in_dim(table, tile, 1, 0)[0]
    lat = jnp.broadcast_to(lat[:, None], (LAT_AT + ROWS, 128))
    edge = ((HALO + 1, FIELDS, LON), BF16, VMEM)
    own, edge_far, edge_near = call(
        pack_kernel,
        [HBM] * 3,
        [((ROWS, FIELDS, LON), F32, VMEM), edge, edge],
        [((VARS, ROWS, LON), F32), ((COND, ROWS, LON), F32), ((HALF, ROWS, LON), F32)],
        copies=3,
    )(members, condition, observed)
    across = [(i, i + 1) for i in range(1, TILES - 1, 2)]
    far = lax.ppermute(edge_far, TILE, across + [(j, i) for i, j in across])
    near = lax.ppermute(edge_near, "core", [(0, 1), (1, 0)])
    near, lat = lax.optimization_barrier((near, lat))
    w_shapes = [(CH, 9 * FIELDS), (3 * CH, 3 * CH), (48, 3 * CH), (CH, 144), (3 * CH, 3 * CH)]
    w_in, w_mid, w_out, w_back_2, w_back_1 = call(
        weights_kernel,
        [HBM] * 3,
        [(shape, BF16, VMEM) for shape in w_shapes[:3]]
        + [(shape, BF16, HBM) for shape in w_shapes[3:]],
        [((9, INPUTS, CH), BF16), ((9, CH, CH), BF16), ((9, VARS, CH), BF16)]
        + [(shape, F32) for shape in w_shapes]
        + [(shape, BF16) for shape in w_shapes[3:]],
        copies=5,
    )(kernel_in.transpose(0, 2, 1), kernel_mid, kernel_out)
    saved = [
        ((ROWS + 10, 3 * FIELDS, LON), BF16),
        ((ROWS + 8, CH, LON), BF16),
        ((ROWS, CH, LON), F32),
        ((ROWS + 6, CH, LON), BF16),
        ((ROWS + 2, CH, LON), F32),
    ]
    kept_shape = ((4, WIDE, LON), F32)
    send, pushed, kept, stack, hidden_1, slope_1, hidden_2, slope_2 = call(
        forward_kernel,
        [VMEM] * 3 + [HBM] + [VMEM] * 3,
        [((SENT, LON), F32, VMEM), ((VARS, ROWS, LON), F32, VMEM), kept_shape + (VMEM,)]
        + [shape + (VMEM,) for shape in saved],
        [((2 * HALO, FIELDS, LON), F32), ((HALF, ROWS, LON), F32)],
        copies=1,
        flops=10**9,
    )(far, near, own, members, w_in, w_mid, w_out)
    fields = spread(send, "member", MEMBERS)
    (swapped,) = call(
        distance_kernel,
        [VMEM] * 5,
        [((MEMBERS * (NEAR + 1), LON), F32, VMEM)],
        vmem=8 * 10**6,
    )(lat, members, observed, fields, kept)
    swap = [(0, 1), (1, 0)]
    beside = lax.ppermute(swapped, "core", swap)
    partials = swapped[MEMBERS * NEAR :, :128] + beside[MEMBERS * NEAR :, :128]
    totals = spread(partials, "ring", RING)
    mine, theirs = call(
        backward_kernel,
        [VMEM] * 10 + [HBM] * 2,
        [((MEMBERS * CHUNK, 128), F32, VMEM)] * 2,
        [(shape, BF16) for shape in w_shapes[3:]]
        + [
            ((ROWS + 4, 48, LON), BF16),
            ((ROWS + 2, 3 * CH, LON), BF16),
            ((ROWS + 2, 3 * CH, LON), F32),
            ((48, 3 * CH), F32),
            ((3 * CH, 3 * CH), F32),
            ((9 * FIELDS, CH), F32),
            ((6 * CH, 128), F32),
        ],
        copies=2,
        flops=10**9,
    )(
        lat, totals, beside, fields, kept, stack, hidden_1, slope_1, hidden_2, slope_2,
        w_back_2, w_back_1,
    )
    mine = mine + lax.ppermute(theirs, "core", swap)
    chunk = jnp.sum(lax.all_to_all(mine.reshape(MEMBERS, CHUNK, 128), "member", 0, 0), 0)
    chunk = jnp.sum(spread(chunk, "ring", RING), 0)
    other = lax.ppermute(chunk, "core", swap)
    chunks = spread(jnp.stack([chunk, other]), "member", MEMBERS)
    grad_in, grad_mid, grad_out, energy = call(
        unpack_kernel,
        [VMEM],
        [
            ((9, INPUTS, CH), F32, VMEM),
            ((9, CH, CH), F32, VMEM),
            ((9, VARS, CH), F32, VMEM),
            ((1, 1), F32, VMEM),
        ],
        [((6 * CH, 128), F32)],
        vmem=16 * 10**6,
    )(chunks)
    return (pushed[None], energy[0, 0], grad_in.transpose(0, 2, 1), grad_mid, grad_out)


def solution(mesh):
    fine = Mesh(mesh.devices.reshape(MEMBERS, -1, 2), ("member",) + TILE)
    in_specs = (
        P("member", None, TILE, None),
        P(None, TILE, None),
        P(None, TILE, None),
        P(),
        P(),
        P(),
    )
    out_specs = (P("member", None, TILE, None), P(), P(), P(), P())
    return jax.shard_map(
        per_device, mesh=fine, in_specs=in_specs, out_specs=out_specs, check_vma=False
    )
```

```python
import functools
import math

import jax
import jax.numpy as jnp
import numpy as np
from jax import lax
from jax.experimental import pallas as pl
from jax.experimental.pallas import tpu as pltpu
from jax.sharding import Mesh, PartitionSpec as P

EPSILON = 1e-06
MEMBERS, NLAT, LON, ROWS = 8, 256, 512, 8
VARS, HALF, COND, CH = 6, 3, 6, 64
TILES, RING = 32, 16
ENTRIES = VARS * NLAT * LON
HALO = 5
FIELDS = 16
INPUTS = HALF + COND
WIDE = (ROWS + 4) * HALF
LAT_AT = 40
OWN = ROWS * HALF
FAR_AT = 2 * OWN
NEAR = 2 * HALF
SENT = 56
CHUNK = 24
TILE = ("ring", "core")
F32, BF16 = jnp.float32, jnp.bfloat16


def spread(value, axes, count):
    copies = jnp.broadcast_to(value[None], (count,) + value.shape)
    return lax.all_to_all(copies, axes, 0, 0)


def lat_table():
    rows = np.arange(NLAT)
    cosine = np.cos((-90.0 + 180.0 * (rows + 0.5) / NLAT) * (np.pi / 180.0))
    lat = (cosine / cosine.mean()).astype(np.float32)
    padded = np.pad(lat, (2, 2))
    table = np.zeros((TILES, LAT_AT + ROWS), np.float32)
    for tile in range(TILES):
        wide = padded[tile * ROWS : tile * ROWS + ROWS + 4]
        table[tile, :WIDE] = np.repeat(wide, HALF)
        table[tile, LAT_AT:] = lat[tile * ROWS : (tile + 1) * ROWS]
    return table


def turned(value, step):
    return value if step == 0 else pltpu.roll(value, step % LON, 1)


def dot(left, right):
    return jnp.dot(left, right, preferred_element_type=F32)


def dot_cells(left, right):
    return lax.dot_general(left, right, (((1,), (1,)), ((), ())), preferred_element_type=F32)


def first_row():
    return lax.axis_index(TILE) * ROWS


def inside(base, row):
    row = base + row
    return jnp.where((row >= 0) & (row < NLAT), 1.0, 0.0).astype(F32)


def sigmoid(value):
    return 0.5 * jnp.tanh(0.5 * value) + 0.5


def loop(start, stop, body):
    lax.fori_loop(start, stop, lambda row, carry: (body(row), carry)[1], 0, unroll=True)


def pack_kernel(
    members_in, condition_in, observed_in, own, edge_far, edge_near,
    members, condition, observed, sems,
):
    pairs = [(members_in, members), (condition_in, condition)]
    pairs.append((observed_in.at[HALF:], observed))
    for copy in started(pairs, sems):
        copy.wait()
    for row in range(ROWS):
        own[row, :HALF, :] = members[:HALF, row, :]
        own[row, HALF:INPUTS, :] = condition[:, row, :]
        own[row, INPUTS : INPUTS + HALF, :] = members[HALF:, row, :]
        own[row, INPUTS + HALF : INPUTS + 2 * HALF, :] = observed[:, row, :]
        own[row, FIELDS - 1 :, :] = jnp.zeros((1, LON), F32)
    odd = lax.axis_index("core") == 1
    is_input = lax.broadcasted_iota(jnp.int32, (FIELDS, 1), 0) < INPUTS
    initial = in_parts(own[0], own[1])
    last = in_parts(own[ROWS - 2], own[ROWS - 1])
    for row in range(HALO + 1):
        at = min(row, HALO - 1)
        first = jnp.where(is_input, own[at], initial[row])
        final = jnp.where(is_input, own[ROWS - HALO + at], last[row])
        edge_far[row] = jnp.where(odd, final, first).astype(BF16)
        edge_near[row] = jnp.where(odd, first, final).astype(BF16)


def in_parts(row_a, row_b):
    parts = []
    for value in (row_a, row_b):
        high = value.astype(BF16).astype(F32)
        middle = (value - high).astype(BF16).astype(F32)
        parts.append((high, middle, value - high - middle))
    (high_a, middle_a, low_a), (high_b, middle_b, low_b) = parts
    return [high_a, high_b, middle_a, middle_b, low_a, low_b]


def weights_kernel(
    kernel_in_in, kernel_mid_in, kernel_out_in, w_in, w_mid, w_out, w_back_2, w_back_1,
    kernel_in, kernel_mid, kernel_out, flat_in, square, flat_out, back_2, back_1, sems,
):
    pairs = [(kernel_in_in, kernel_in), (kernel_mid_in, kernel_mid), (kernel_out_in, kernel_out)]
    copies = started(pairs, sems)
    flat_out[...] = jnp.zeros_like(flat_out)
    back_2[...] = jnp.zeros_like(back_2)
    for copy in copies:
        copy.wait()
    for tap in range(9):
        a, b = tap // 3, tap % 3
        back = 3 * (2 - a) + b
        first = kernel_in[tap].astype(F32)
        first = jnp.concatenate([first, jnp.zeros((FIELDS - INPUTS, CH), F32)], 0).T
        flat_in[:, tap * FIELDS : (tap + 1) * FIELDS] = first
        mid = kernel_mid[tap].astype(F32)
        square[b * CH : (b + 1) * CH, a * CH : (a + 1) * CH] = mid
        back_1[a * CH : (a + 1) * CH, b * CH : (b + 1) * CH] = mid.T
        out = kernel_out[tap].astype(F32)
        across = slice(a * CH, (a + 1) * CH)
        flat_out[b * 16 : b * 16 + HALF, across] = out[:HALF]
        flat_out[b * 16 + 8 : b * 16 + 8 + HALF, across] = out[HALF:]
        out = jnp.concatenate([out, jnp.zeros((8 - VARS, CH), F32)], 0).T
        back_2[:, back * 16 : back * 16 + HALF] = out[:, :HALF]
        back_2[:, back * 16 + 8 : back * 16 + 8 + HALF] = out[:, HALF:VARS]
    w_back_2[...] = back_2[...].astype(BF16)
    w_back_1[...] = back_1[...].astype(BF16)
    w_in[...] = flat_in[...].astype(BF16)
    w_mid[...] = square[...].astype(BF16)
    w_out[...] = flat_out[...].astype(BF16)


def forward_kernel(
    far, near, own, members_in, w_in, w_mid, w_out,
    send, pushed, kept, stack, hidden_1, slope_1, hidden_2, slope_2, edges, members, sems,
):
    brought = pltpu.make_async_copy(members_in.at[:HALF], members, sems.at[0])
    brought.start()
    base, odd = first_row(), lax.axis_index("core") == 1
    is_input = lax.broadcasted_iota(jnp.int32, (FIELDS, 1), 0) < INPUTS
    for side in range(2):
        got = []
        for row in range(HALO + 1):
            one, other = far[row].astype(F32), near[row].astype(F32)
            got.append(jnp.where(odd == (side == 0), other, one))
        whole = [got[0] + got[2] + got[4], got[1] + got[3] + got[5]]
        for row in range(HALO):
            field = got[row]
            exact = row - (HALO - 2) if side == 0 else row
            if 0 <= exact < 2:
                field = jnp.where(is_input, field, whole[exact])
            edges[side * HALO + row] = field

    def wide(row):
        if row < HALO:
            return edges[row]
        return own[row - HALO] if row < HALO + ROWS else edges[row - ROWS]

    for row in range(ROWS + 2 * HALO):
        field = wide(row)
        for shift in range(3):
            part = turned(field, 1 - shift).astype(BF16)
            stack[row, shift * FIELDS : (shift + 1) * FIELDS, :] = part

    def first(row, kept_row):
        pre = dot(w_in[...], stack[pl.ds(row, 3)].reshape(9 * FIELDS, LON))
        gate = sigmoid(pre)
        hidden_1[row] = (pre * gate * inside(base, row - 4)).astype(BF16)
        if kept_row:
            slope_1[row - 4] = gate * (1.0 + pre * (1.0 - gate))

    loop(0, 4, functools.partial(first, kept_row=False))
    loop(4, 12, functools.partial(first, kept_row=True))
    loop(12, 16, functools.partial(first, kept_row=False))

    def second(row, kept_row):
        part = dot(w_mid[...], hidden_1[pl.ds(row, 3)].reshape(3 * CH, LON))
        pre = turned(part[:CH], 1) + part[CH : 2 * CH] + turned(part[2 * CH :], -1)
        gate = sigmoid(pre)
        hidden_2[row] = (pre * gate * inside(base, row - 3)).astype(BF16)
        if kept_row:
            slope_2[row - 2] = gate * (1.0 + pre * (1.0 - gate))

    loop(0, 2, functools.partial(second, kept_row=False))
    loop(2, 12, functools.partial(second, kept_row=True))
    loop(12, 14, functools.partial(second, kept_row=False))

    brought.wait()
    send[OWN:FAR_AT, :] = members[...].reshape(OWN, LON)
    for row in range(ROWS + 4):
        part = dot(w_out[...], hidden_2[row : row + 3].reshape(3 * CH, LON))
        both = turned(part[:16], 1) + part[16:32] + turned(part[32:], -1)
        log_scale = jnp.tanh(both[:HALF])
        field = wide(row + 3)
        moving = field[INPUTS : INPUTS + HALF]
        moved = moving * jnp.exp(log_scale) + both[8 : 8 + HALF]
        here = slice(row * HALF, (row + 1) * HALF)
        kept[0, here, :] = log_scale
        kept[1, here, :] = moving
        kept[2, here, :] = field[INPUTS + HALF : INPUTS + 2 * HALF]
        kept[3, here, :] = moved
        if 2 <= row < 2 + ROWS:
            send[(row - 2) * HALF : (row - 1) * HALF, :] = moved
            for var in range(HALF):
                pushed[HALF + var, row - 2 : row - 1, :] = moved[var : var + 1]
    far_rows = jnp.where(odd, kept[3, WIDE - NEAR :, :], kept[3, :NEAR, :])
    send[FAR_AT:, :] = jnp.concatenate([far_rows, jnp.zeros((SENT - FAR_AT - NEAR, LON), F32)], 0)
    pushed[:HALF] = members[...]


def folded(value):
    return sum(value[..., at : at + 128] for at in range(0, LON, 128))


def distance_kernel(lat, members, observed, fields, kept, swapped):
    me, odd = lax.axis_index("member"), lax.axis_index("core") == 1
    upper_lat = lat[NEAR : NEAR + OWN, :1]
    lower_lat = jnp.concatenate([lat[LAT_AT:, :1]] * HALF, 0)
    fixed_mine = members[:HALF].reshape(OWN, LON)
    mine = kept[3, NEAR : NEAR + OWN, :]

    def weighed(moved, fixed):
        upper = jnp.sum(folded(upper_lat * (mine - moved) ** 2), 0, keepdims=True)
        lower = jnp.sum(folded(lower_lat * (fixed_mine - fixed) ** 2), 0, keepdims=True)
        return upper + lower

    seen = kept[2, NEAR : NEAR + OWN, :]
    to_observed = weighed(seen, observed[:HALF].reshape(OWN, LON))
    rows = []
    for n in range(MEMBERS):
        first, last = fields[n, :NEAR], fields[n, OWN - NEAR : OWN]
        swapped[n * NEAR : (n + 1) * NEAR, :] = jnp.where(odd, first, last)
        rows.append(weighed(fields[n, :OWN], fields[n, OWN:FAR_AT]))
    all_rows = jnp.concatenate(rows, 0)
    spot = lax.broadcasted_iota(jnp.int32, (MEMBERS, 128), 0)
    swapped[MEMBERS * NEAR :, :128] = jnp.where(spot == me, to_observed, all_rows)
    swapped[MEMBERS * NEAR :, 128:] = jnp.zeros((MEMBERS, LON - 128), F32)


def started(pairs, sems):
    copies = [
        pltpu.make_async_copy(source, target, sems.at[at])
        for at, (source, target) in enumerate(pairs)
    ]
    for copy in copies:
        copy.start()
    return copies


def backward_kernel(
    lat, totals, near, fields, kept, stack, hidden_1, slope_1, hidden_2, slope_2, w_back_2, w_back_1,
    mine, theirs,
    coupled, turned_2, by_row, sum_out, sum_mid, sum_in, packed,
):
    me, base, core = lax.axis_index("member"), first_row(), lax.axis_index("core")
    sum_out[...] = jnp.zeros_like(sum_out)
    sum_mid[...] = jnp.zeros_like(sum_mid)
    sum_in[...] = jnp.zeros_like(sum_in)
    total = totals[0]
    for tile in range(1, RING):
        total = total + totals[tile]
    distances = jnp.sqrt(jnp.sum(total, 1, keepdims=True) / ENTRIES + EPSILON)
    is_me = lax.broadcasted_iota(jnp.int32, (MEMBERS, 1), 0) == me
    shares = jnp.where(is_me, distances / MEMBERS, -distances / (2.0 * MEMBERS * MEMBERS))
    share = jnp.sum(shares, 0, keepdims=True) / TILES
    weights = 1.0 / (jnp.where(is_me, MEMBERS, MEMBERS * MEMBERS) * distances)
    own_weight = jnp.sum(jnp.where(is_me, weights, 0.0), 0, keepdims=True)
    weights = jnp.where(is_me, 0.0, weights)
    log_scale, moving, observed, moved = kept[0], kept[1], kept[2], kept[3]
    inner = (moved - observed) * own_weight
    odd = core == 1
    first, last = moved[:NEAR], moved[WIDE - NEAR :]
    near_mine, far_mine = jnp.where(odd, first, last), jnp.where(odd, last, first)
    own_sum = jnp.zeros((OWN, LON), F32)
    near_sum = jnp.zeros((NEAR, LON), F32)
    far_sum = near_sum
    for n in range(MEMBERS):
        weight = weights[n : n + 1]
        own_sum += weight * (moved[NEAR : NEAR + OWN] - fields[n, :OWN])
        near_sum += weight * (near_mine - near[n * NEAR : (n + 1) * NEAR])
        far_sum += weight * (far_mine - fields[n, FAR_AT : FAR_AT + NEAR])
    first, last = jnp.where(odd, near_sum, far_sum), jnp.where(odd, far_sum, near_sum)
    inner = inner - jnp.concatenate([first, own_sum, last], 0)
    upper = lat[:WIDE, :1] * inner / math.sqrt(ENTRIES)
    scaled = upper * moving * jnp.exp(log_scale) * (1.0 - log_scale * log_scale)
    blank = jnp.zeros((8 - HALF, LON), F32)
    for row in range(ROWS + 4):
        here = slice(row * HALF, (row + 1) * HALF)
        field = jnp.concatenate([scaled[here], blank, upper[here], blank], 0)
        for shift in range(3):
            part = turned(field, shift - 1).astype(BF16)
            coupled[row, shift * 16 : (shift + 1) * 16, :] = part

    def second(row):
        back = dot(w_back_2[...], coupled[pl.ds(row, 3)].reshape(144, LON))
        grad = back * slope_2[row] * inside(base, row - 1)
        for shift in range(3):
            part = turned(grad, shift - 1).astype(BF16)
            turned_2[row, shift * CH : (shift + 1) * CH, :] = part

    loop(0, ROWS + 2, second)

    def across_rows(row):
        by_row[row] = dot(w_back_1[...], turned_2[row])

    loop(0, ROWS + 2, across_rows)

    def middle(row):
        near = hidden_1[pl.ds(row + 3, 3)].reshape(3 * CH, LON)
        sum_mid[...] += dot_cells(turned_2[row + 1], near)

    loop(0, ROWS, middle)

    def outer(row):
        near = hidden_2[pl.ds(row + 2, 3)].reshape(3 * CH, LON)
        sum_out[...] += dot_cells(coupled[row + 2], near)

    loop(0, ROWS, outer)

    def last(row):
        back = by_row[row + 2, :CH] + by_row[row + 1, CH : 2 * CH] + by_row[row, 2 * CH :]
        grad = (back * slope_1[row]).astype(BF16)
        near = stack[pl.ds(row + 4, 3)].reshape(9 * FIELDS, LON)
        sum_in[...] += dot_cells(near, grad)

    loop(0, ROWS, last)
    packed[5 * CH :, :] = jnp.zeros((CH, 128), F32)
    packed[4 * CH : 5 * CH, CH:] = jnp.zeros((CH, CH), F32)
    for tap in range(9):
        a, b = tap // 3, tap % 3
        at, side = place_mid(tap)
        packed[at : at + CH, side] = sum_mid[b * CH : (b + 1) * CH, a * CH : (a + 1) * CH]
        at = 5 * CH + tap * VARS
        across = slice(a * CH, (a + 1) * CH)
        packed[at : at + HALF, :CH] = sum_out[b * 16 : b * 16 + HALF, across]
        packed[at + HALF : at + VARS, :CH] = sum_out[b * 16 + 8 : b * 16 + 8 + HALF, across]
        at = 4 * CH + tap * INPUTS
        packed[at : at + INPUTS, CH:] = sum_in[tap * FIELDS : tap * FIELDS + INPUTS]
    packed[6 * CH - 1 :, 127:] = share
    half = MEMBERS * CHUNK
    for copy in range(2):

        @pl.when(core == copy)
        def _():
            mine[...] = packed[copy * half : (copy + 1) * half, :]
            theirs[...] = packed[(1 - copy) * half : (2 - copy) * half, :]


def place_mid(tap):
    return (tap * CH, slice(0, CH)) if tap < 5 else ((tap - 5) * CH, slice(CH, 2 * CH))


def unpack_kernel(chunks, grad_in, grad_mid, grad_out, energy, packed):
    core = lax.axis_index("core")
    for member in range(MEMBERS):
        first, second = chunks[member, 0], chunks[member, 1]
        at = member * CHUNK
        packed[at : at + CHUNK, :] = jnp.where(core == 0, first, second)
        at += MEMBERS * CHUNK
        packed[at : at + CHUNK, :] = jnp.where(core == 0, second, first)
    for tap in range(9):
        at, side = place_mid(tap)
        grad_mid[tap] = packed[at : at + CH, side]
        at = 5 * CH + tap * VARS
        grad_out[tap] = packed[at : at + VARS, :CH]
        at = 4 * CH + tap * INPUTS
        grad_in[tap] = packed[at : at + INPUTS, CH:]
    energy[...] = packed[6 * CH - 1 :, 127:]


VMEM_LIMIT = 28 * 10**6
VMEM = pl.BlockSpec(memory_space=pltpu.VMEM)
HBM = pl.BlockSpec(memory_space=pltpu.HBM)


def call(kernel, ins, outs, scratch=(), copies=0, flops=10**6, vmem=VMEM_LIMIT):
    held = [pltpu.VMEM(shape, dtype) for shape, dtype in scratch]
    if copies > 0:
        held.append(pltpu.SemaphoreType.DMA((copies,)))
    shapes = [
        pltpu.HBM(shape, dtype) if spec is HBM else jax.ShapeDtypeStruct(shape, dtype)
        for shape, dtype, spec in outs
    ]
    run = pl.pallas_call(
        kernel,
        out_shape=shapes,
        in_specs=ins,
        out_specs=[spec for shape, dtype, spec in outs],
        scratch_shapes=held,
        compiler_params=pltpu.CompilerParams(vmem_limit_bytes=vmem),
        cost_estimate=pl.CostEstimate(flops=flops, bytes_accessed=10**6, transcendentals=0),
    )

    def placed(*arrays):
        return run(
            *[
                pltpu.with_memory_space_constraint(array, pltpu.HBM) if spec is HBM else array
                for array, spec in zip(arrays, ins)
            ]
        )

    return placed


def per_device(members, condition, observed, kernel_in, kernel_mid, kernel_out):
    members = members[0]
    tile = lax.axis_index(TILE)
    table = jnp.asarray(lat_table())
    lat = lax.dynamic_slice_in_dim(table, tile, 1, 0)[0]
    lat = jnp.broadcast_to(lat[:, None], (LAT_AT + ROWS, 128))
    edge = ((HALO + 1, FIELDS, LON), BF16, VMEM)
    own, edge_far, edge_near = call(
        pack_kernel,
        [HBM] * 3,
        [((ROWS, FIELDS, LON), F32, VMEM), edge, edge],
        [((VARS, ROWS, LON), F32), ((COND, ROWS, LON), F32), ((HALF, ROWS, LON), F32)],
        copies=3,
    )(members, condition, observed)
    across = [(i, i + 1) for i in range(1, TILES - 1, 2)]
    far = lax.ppermute(edge_far, TILE, across + [(j, i) for i, j in across])
    near = lax.ppermute(edge_near, "core", [(0, 1), (1, 0)])
    near, lat = lax.optimization_barrier((near, lat))
    w_shapes = [(CH, 9 * FIELDS), (3 * CH, 3 * CH), (48, 3 * CH), (CH, 144), (3 * CH, 3 * CH)]
    w_in, w_mid, w_out, w_back_2, w_back_1 = call(
        weights_kernel,
        [HBM] * 3,
        [(shape, BF16, VMEM) for shape in w_shapes],
        [((9, INPUTS, CH), BF16), ((9, CH, CH), BF16), ((9, VARS, CH), BF16)]
        + [(shape, F32) for shape in w_shapes],
        copies=3,
    )(kernel_in.transpose(0, 2, 1), kernel_mid, kernel_out)
    saved = [
        ((ROWS + 10, 3 * FIELDS, LON), BF16),
        ((ROWS + 8, CH, LON), BF16),
        ((ROWS, CH, LON), F32),
        ((ROWS + 6, CH, LON), BF16),
        ((ROWS + 2, CH, LON), F32),
    ]
    kept_shape = ((4, WIDE, LON), F32)
    send, pushed, kept, stack, hidden_1, slope_1, hidden_2, slope_2 = call(
        forward_kernel,
        [VMEM] * 3 + [HBM] + [VMEM] * 3,
        [((SENT, LON), F32, VMEM), ((VARS, ROWS, LON), F32, VMEM), kept_shape + (VMEM,)]
        + [shape + (VMEM,) for shape in saved],
        [((2 * HALO, FIELDS, LON), F32), ((HALF, ROWS, LON), F32)],
        copies=1,
        flops=10**9,
    )(far, near, own, members, w_in, w_mid, w_out)
    fields = spread(send, "member", MEMBERS)
    (swapped,) = call(
        distance_kernel,
        [VMEM] * 5,
        [((MEMBERS * (NEAR + 1), LON), F32, VMEM)],
        vmem=8 * 10**6,
    )(lat, members, observed, fields, kept)
    swap = [(0, 1), (1, 0)]
    beside = lax.ppermute(swapped, "core", swap)
    partials = swapped[MEMBERS * NEAR :, :128] + beside[MEMBERS * NEAR :, :128]
    totals = spread(partials, "ring", RING)
    mine, theirs = call(
        backward_kernel,
        [VMEM] * 12,
        [((MEMBERS * CHUNK, 128), F32, VMEM)] * 2,
        [
            ((ROWS + 4, 48, LON), BF16),
            ((ROWS + 2, 3 * CH, LON), BF16),
            ((ROWS + 2, 3 * CH, LON), F32),
            ((48, 3 * CH), F32),
            ((3 * CH, 3 * CH), F32),
            ((9 * FIELDS, CH), F32),
            ((6 * CH, 128), F32),
        ],
        flops=10**9,
    )(
        lat, totals, beside, fields, kept, stack, hidden_1, slope_1, hidden_2, slope_2,
        w_back_2, w_back_1,
    )
    mine = mine + lax.ppermute(theirs, "core", swap)
    chunk = jnp.sum(lax.all_to_all(mine.reshape(MEMBERS, CHUNK, 128), "member", 0, 0), 0)
    chunk = jnp.sum(spread(chunk, "ring", RING), 0)
    other = lax.ppermute(chunk, "core", swap)
    chunks = spread(jnp.stack([chunk, other]), "member", MEMBERS)
    grad_in, grad_mid, grad_out, energy = call(
        unpack_kernel,
        [VMEM],
        [
            ((9, INPUTS, CH), F32, VMEM),
            ((9, CH, CH), F32, VMEM),
            ((9, VARS, CH), F32, VMEM),
            ((1, 1), F32, VMEM),
        ],
        [((6 * CH, 128), F32)],
        vmem=16 * 10**6,
    )(chunks)
    return (pushed[None], energy[0, 0], grad_in.transpose(0, 2, 1), grad_mid, grad_out)


def solution(mesh):
    fine = Mesh(mesh.devices.reshape(MEMBERS, -1, 2), ("member",) + TILE)
    in_specs = (
        P("member", None, TILE, None),
        P(None, TILE, None),
        P(None, TILE, None),
        P(),
        P(),
        P(),
    )
    out_specs = (P("member", None, TILE, None), P(), P(), P(), P())
    return jax.shard_map(
        per_device, mesh=fine, in_specs=in_specs, out_specs=out_specs, check_vma=False
    )
```

```python
import functools
import math

import jax
import jax.numpy as jnp
import numpy as np
from jax import lax
from jax.experimental import pallas as pl
from jax.experimental.pallas import tpu as pltpu
from jax.sharding import Mesh, PartitionSpec as P

EPSILON = 1e-06
MEMBERS, NLAT, LON, ROWS = 8, 256, 512, 8
VARS, HALF, COND, CH = 6, 3, 6, 64
TILES, RING = 32, 16
ENTRIES = VARS * NLAT * LON
HALO = 5
FIELDS = 16
INPUTS = HALF + COND
WIDE = (ROWS + 4) * HALF
LAT_AT = 40
OWN = ROWS * HALF
FAR_AT = 2 * OWN
NEAR = 2 * HALF
SENT = 56
CHUNK = 24
TILE = ("ring", "core")
F32, BF16 = jnp.float32, jnp.bfloat16


def spread(value, axes, count):
    copies = jnp.broadcast_to(value[None], (count,) + value.shape)
    return lax.all_to_all(copies, axes, 0, 0)


def lat_table():
    rows = np.arange(NLAT)
    cosine = np.cos((-90.0 + 180.0 * (rows + 0.5) / NLAT) * (np.pi / 180.0))
    lat = (cosine / cosine.mean()).astype(np.float32)
    padded = np.pad(lat, (2, 2))
    table = np.zeros((TILES, LAT_AT + ROWS), np.float32)
    for tile in range(TILES):
        wide = padded[tile * ROWS : tile * ROWS + ROWS + 4]
        table[tile, :WIDE] = np.repeat(wide, HALF)
        table[tile, LAT_AT:] = lat[tile * ROWS : (tile + 1) * ROWS]
    return table


def turned(value, step):
    return value if step == 0 else pltpu.roll(value, step % LON, 1)


def dot(left, right):
    return jnp.dot(left, right, preferred_element_type=F32)


def dot_cells(left, right):
    return lax.dot_general(left, right, (((1,), (1,)), ((), ())), preferred_element_type=F32)


def first_row():
    return lax.axis_index(TILE) * ROWS


def inside(base, row):
    row = base + row
    return jnp.where((row >= 0) & (row < NLAT), 1.0, 0.0).astype(F32)


def sigmoid(value):
    return 0.5 * jnp.tanh(0.5 * value) + 0.5


def loop(start, stop, body):
    lax.fori_loop(start, stop, lambda row, carry: (body(row), carry)[1], 0, unroll=True)


def pack_kernel(
    members_in, condition_in, observed_in, own, edge_far, edge_near,
    members, condition, observed, sems,
):
    pairs = [(members_in, members), (condition_in, condition)]
    pairs.append((observed_in.at[HALF:], observed))
    for copy in started(pairs, sems):
        copy.wait()
    for row in range(ROWS):
        own[row, :HALF, :] = members[:HALF, row, :]
        own[row, HALF:INPUTS, :] = condition[:, row, :]
        own[row, INPUTS : INPUTS + HALF, :] = members[HALF:, row, :]
        own[row, INPUTS + HALF : INPUTS + 2 * HALF, :] = observed[:, row, :]
        own[row, FIELDS - 1 :, :] = jnp.zeros((1, LON), F32)
    odd = lax.axis_index("core") == 1
    is_input = lax.broadcasted_iota(jnp.int32, (FIELDS, 1), 0) < INPUTS
    initial = in_parts(own[0], own[1])
    last = in_parts(own[ROWS - 2], own[ROWS - 1])
    for row in range(HALO + 1):
        at = min(row, HALO - 1)
        first = jnp.where(is_input, own[at], initial[row])
        final = jnp.where(is_input, own[ROWS - HALO + at], last[row])
        edge_far[row] = jnp.where(odd, final, first).astype(BF16)
        edge_near[row] = jnp.where(odd, first, final).astype(BF16)


def in_parts(row_a, row_b):
    parts = []
    for value in (row_a, row_b):
        high = value.astype(BF16).astype(F32)
        middle = (value - high).astype(BF16).astype(F32)
        parts.append((high, middle, value - high - middle))
    (high_a, middle_a, low_a), (high_b, middle_b, low_b) = parts
    return [high_a, high_b, middle_a, middle_b, low_a, low_b]


def weights_kernel(
    kernel_in_in, kernel_mid_in, kernel_out_in, w_in, w_mid, w_out, w_back_2, w_back_1,
    kernel_in, kernel_mid, kernel_out, flat_in, square, flat_out, back_2, back_1, sems,
):
    pairs = [(kernel_in_in, kernel_in), (kernel_mid_in, kernel_mid), (kernel_out_in, kernel_out)]
    copies = started(pairs, sems)
    flat_out[...] = jnp.zeros_like(flat_out)
    back_2[...] = jnp.zeros_like(back_2)
    for copy in copies:
        copy.wait()
    for tap in range(9):
        a, b = tap // 3, tap % 3
        back = 3 * (2 - a) + b
        first = kernel_in[tap].astype(F32)
        first = jnp.concatenate([first, jnp.zeros((FIELDS - INPUTS, CH), F32)], 0).T
        flat_in[:, tap * FIELDS : (tap + 1) * FIELDS] = first
        mid = kernel_mid[tap].astype(F32)
        square[b * CH : (b + 1) * CH, a * CH : (a + 1) * CH] = mid
        back_1[a * CH : (a + 1) * CH, b * CH : (b + 1) * CH] = mid.T
        out = kernel_out[tap].astype(F32)
        across = slice(a * CH, (a + 1) * CH)
        flat_out[b * 16 : b * 16 + HALF, across] = out[:HALF]
        flat_out[b * 16 + 8 : b * 16 + 8 + HALF, across] = out[HALF:]
        out = jnp.concatenate([out, jnp.zeros((8 - VARS, CH), F32)], 0).T
        back_2[:, back * 16 : back * 16 + HALF] = out[:, :HALF]
        back_2[:, back * 16 + 8 : back * 16 + 8 + HALF] = out[:, HALF:VARS]
    w_back_2[...] = back_2[...].astype(BF16)
    w_back_1[...] = back_1[...].astype(BF16)
    w_in[...] = flat_in[...].astype(BF16)
    w_mid[...] = square[...].astype(BF16)
    w_out[...] = flat_out[...].astype(BF16)


def forward_kernel(
    far, near, own, members_in, w_in, w_mid, w_out,
    send, pushed, kept, stack, hidden_1, slope_1, hidden_2, slope_2, edges, members, sems,
):
    brought = pltpu.make_async_copy(members_in.at[:HALF], members, sems.at[0])
    brought.start()
    base, odd = first_row(), lax.axis_index("core") == 1
    is_input = lax.broadcasted_iota(jnp.int32, (FIELDS, 1), 0) < INPUTS
    for side in range(2):
        got = []
        for row in range(HALO + 1):
            one, other = far[row].astype(F32), near[row].astype(F32)
            got.append(jnp.where(odd == (side == 0), other, one))
        whole = [got[0] + got[2] + got[4], got[1] + got[3] + got[5]]
        for row in range(HALO):
            field = got[row]
            exact = row - (HALO - 2) if side == 0 else row
            if 0 <= exact < 2:
                field = jnp.where(is_input, field, whole[exact])
            edges[side * HALO + row] = field

    def wide(row):
        if row < HALO:
            return edges[row]
        return own[row - HALO] if row < HALO + ROWS else edges[row - ROWS]

    for row in range(ROWS + 2 * HALO):
        field = wide(row)
        for shift in range(3):
            part = turned(field, 1 - shift).astype(BF16)
            stack[row, shift * FIELDS : (shift + 1) * FIELDS, :] = part

    def first(row, kept_row):
        pre = dot(w_in[...], stack[pl.ds(row, 3)].reshape(9 * FIELDS, LON))
        gate = sigmoid(pre)
        hidden_1[row] = (pre * gate * inside(base, row - 4)).astype(BF16)
        if kept_row:
            slope_1[row - 4] = gate * (1.0 + pre * (1.0 - gate))

    loop(0, 4, functools.partial(first, kept_row=False))
    loop(4, 12, functools.partial(first, kept_row=True))
    loop(12, 16, functools.partial(first, kept_row=False))

    def second(row, kept_row):
        part = dot(w_mid[...], hidden_1[pl.ds(row, 3)].reshape(3 * CH, LON))
        pre = turned(part[:CH], 1) + part[CH : 2 * CH] + turned(part[2 * CH :], -1)
        gate = sigmoid(pre)
        hidden_2[row] = (pre * gate * inside(base, row - 3)).astype(BF16)
        if kept_row:
            slope_2[row - 2] = gate * (1.0 + pre * (1.0 - gate))

    loop(0, 2, functools.partial(second, kept_row=False))
    loop(2, 12, functools.partial(second, kept_row=True))
    loop(12, 14, functools.partial(second, kept_row=False))

    brought.wait()
    send[OWN:FAR_AT, :] = members[...].reshape(OWN, LON)
    for row in range(ROWS + 4):
        part = dot(w_out[...], hidden_2[row : row + 3].reshape(3 * CH, LON))
        both = turned(part[:16], 1) + part[16:32] + turned(part[32:], -1)
        log_scale = jnp.tanh(both[:HALF])
        field = wide(row + 3)
        moving = field[INPUTS : INPUTS + HALF]
        moved = moving * jnp.exp(log_scale) + both[8 : 8 + HALF]
        here = slice(row * HALF, (row + 1) * HALF)
        kept[0, here, :] = log_scale
        kept[1, here, :] = moving
        kept[2, here, :] = field[INPUTS + HALF : INPUTS + 2 * HALF]
        kept[3, here, :] = moved
        if 2 <= row < 2 + ROWS:
            send[(row - 2) * HALF : (row - 1) * HALF, :] = moved
            for var in range(HALF):
                pushed[HALF + var, row - 2 : row - 1, :] = moved[var : var + 1]
    far_rows = jnp.where(odd, kept[3, WIDE - NEAR :, :], kept[3, :NEAR, :])
    send[FAR_AT:, :] = jnp.concatenate([far_rows, jnp.zeros((SENT - FAR_AT - NEAR, LON), F32)], 0)
    pushed[:HALF] = members[...]


def folded(value):
    return sum(value[..., at : at + 128] for at in range(0, LON, 128))


def distance_kernel(lat, members, observed, fields, kept, swapped):
    me, odd = lax.axis_index("member"), lax.axis_index("core") == 1
    upper_lat = lat[NEAR : NEAR + OWN, :1]
    lower_lat = jnp.concatenate([lat[LAT_AT:, :1]] * HALF, 0)
    fixed_mine = members[:HALF].reshape(OWN, LON)
    mine = kept[3, NEAR : NEAR + OWN, :]

    def weighed(moved, fixed):
        upper = jnp.sum(folded(upper_lat * (mine - moved) ** 2), 0, keepdims=True)
        lower = jnp.sum(folded(lower_lat * (fixed_mine - fixed) ** 2), 0, keepdims=True)
        return upper + lower

    seen = kept[2, NEAR : NEAR + OWN, :]
    to_observed = weighed(seen, observed[:HALF].reshape(OWN, LON))
    rows = []
    for n in range(MEMBERS):
        first, last = fields[n, :NEAR], fields[n, OWN - NEAR : OWN]
        swapped[n * NEAR : (n + 1) * NEAR, :] = jnp.where(odd, first, last)
        rows.append(weighed(fields[n, :OWN], fields[n, OWN:FAR_AT]))
    all_rows = jnp.concatenate(rows, 0)
    spot = lax.broadcasted_iota(jnp.int32, (MEMBERS, 128), 0)
    swapped[MEMBERS * NEAR :, :128] = jnp.where(spot == me, to_observed, all_rows)
    swapped[MEMBERS * NEAR :, 128:] = jnp.zeros((MEMBERS, LON - 128), F32)


def started(pairs, sems):
    copies = [
        pltpu.make_async_copy(source, target, sems.at[at])
        for at, (source, target) in enumerate(pairs)
    ]
    for copy in copies:
        copy.start()
    return copies


def backward_kernel(
    lat, totals, near, fields, kept, stack, hidden_1, slope_1, hidden_2, slope_2, w_back_2, w_back_1,
    mine, theirs,
    coupled, turned_2, by_row, sum_out, sum_mid, sum_in, packed,
):
    me, base, core = lax.axis_index("member"), first_row(), lax.axis_index("core")
    sum_out[...] = jnp.zeros_like(sum_out)
    sum_mid[...] = jnp.zeros_like(sum_mid)
    sum_in[...] = jnp.zeros_like(sum_in)
    total = totals[0]
    for tile in range(1, RING):
        total = total + totals[tile]
    distances = jnp.sqrt(jnp.sum(total, 1, keepdims=True) / ENTRIES + EPSILON)
    is_me = lax.broadcasted_iota(jnp.int32, (MEMBERS, 1), 0) == me
    shares = jnp.where(is_me, distances / MEMBERS, -distances / (2.0 * MEMBERS * MEMBERS))
    share = jnp.sum(shares, 0, keepdims=True) / TILES
    weights = 1.0 / (jnp.where(is_me, MEMBERS, MEMBERS * MEMBERS) * distances)
    own_weight = jnp.sum(jnp.where(is_me, weights, 0.0), 0, keepdims=True)
    weights = jnp.where(is_me, 0.0, weights)
    log_scale, moving, observed, moved = kept[0], kept[1], kept[2], kept[3]
    inner = (moved - observed) * own_weight
    odd = core == 1
    first, last = moved[:NEAR], moved[WIDE - NEAR :]
    near_mine, far_mine = jnp.where(odd, first, last), jnp.where(odd, last, first)
    own_sum = jnp.zeros((OWN, LON), F32)
    near_sum = jnp.zeros((NEAR, LON), F32)
    far_sum = near_sum
    for n in range(MEMBERS):
        weight = weights[n : n + 1]
        own_sum += weight * (moved[NEAR : NEAR + OWN] - fields[n, :OWN])
        near_sum += weight * (near_mine - near[n * NEAR : (n + 1) * NEAR])
        far_sum += weight * (far_mine - fields[n, FAR_AT : FAR_AT + NEAR])
    first, last = jnp.where(odd, near_sum, far_sum), jnp.where(odd, far_sum, near_sum)
    inner = inner - jnp.concatenate([first, own_sum, last], 0)
    upper = lat[:WIDE, :1] * inner / math.sqrt(ENTRIES)
    scaled = upper * moving * jnp.exp(log_scale) * (1.0 - log_scale * log_scale)
    blank = jnp.zeros((8 - HALF, LON), F32)
    for row in range(ROWS + 4):
        here = slice(row * HALF, (row + 1) * HALF)
        field = jnp.concatenate([scaled[here], blank, upper[here], blank], 0)
        for shift in range(3):
            part = turned(field, shift - 1).astype(BF16)
            coupled[row, shift * 16 : (shift + 1) * 16, :] = part

    def second(row):
        back = dot(w_back_2[...], coupled[pl.ds(row, 3)].reshape(144, LON))
        grad = back * slope_2[row] * inside(base, row - 1)
        for shift in range(3):
            part = turned(grad, shift - 1).astype(BF16)
            turned_2[row, shift * CH : (shift + 1) * CH, :] = part

    loop(0, ROWS + 2, second)

    def across_rows(row):
        by_row[row] = dot(w_back_1[...], turned_2[row])

    loop(0, ROWS + 2, across_rows)

    def middle(row):
        near = hidden_1[pl.ds(row + 3, 3)].reshape(3 * CH, LON)
        sum_mid[...] += dot_cells(turned_2[row + 1], near)

    loop(0, ROWS, middle)

    def outer(row):
        near = hidden_2[pl.ds(row + 2, 3)].reshape(3 * CH, LON)
        sum_out[...] += dot_cells(coupled[row + 2], near)

    loop(0, ROWS, outer)

    def last(row):
        back = by_row[row + 2, :CH] + by_row[row + 1, CH : 2 * CH] + by_row[row, 2 * CH :]
        grad = (back * slope_1[row]).astype(BF16)
        near = stack[pl.ds(row + 4, 3)].reshape(9 * FIELDS, LON)
        sum_in[...] += dot_cells(near, grad)

    loop(0, ROWS, last)
    packed[5 * CH :, :] = jnp.zeros((CH, 128), F32)
    packed[4 * CH : 5 * CH, CH:] = jnp.zeros((CH, CH), F32)
    for tap in range(9):
        a, b = tap // 3, tap % 3
        at, side = place_mid(tap)
        packed[at : at + CH, side] = sum_mid[b * CH : (b + 1) * CH, a * CH : (a + 1) * CH]
        at = 5 * CH + tap * VARS
        across = slice(a * CH, (a + 1) * CH)
        packed[at : at + HALF, :CH] = sum_out[b * 16 : b * 16 + HALF, across]
        packed[at + HALF : at + VARS, :CH] = sum_out[b * 16 + 8 : b * 16 + 8 + HALF, across]
        at = 4 * CH + tap * INPUTS
        packed[at : at + INPUTS, CH:] = sum_in[tap * FIELDS : tap * FIELDS + INPUTS]
    packed[6 * CH - 1 :, 127:] = share
    half = MEMBERS * CHUNK
    for copy in range(2):

        @pl.when(core == copy)
        def _():
            mine[...] = packed[copy * half : (copy + 1) * half, :]
            theirs[...] = packed[(1 - copy) * half : (2 - copy) * half, :]


def place_mid(tap):
    return (tap * CH, slice(0, CH)) if tap < 5 else ((tap - 5) * CH, slice(CH, 2 * CH))


def unpack_kernel(chunks, grad_in, grad_mid, grad_out, energy, packed):
    for member in range(MEMBERS):
        for half in range(2):
            at = (half * MEMBERS + member) * CHUNK
            packed[at : at + CHUNK, :] = chunks[member * 2 + half]
    for tap in range(9):
        at, side = place_mid(tap)
        grad_mid[tap] = packed[at : at + CH, side]
        at = 5 * CH + tap * VARS
        grad_out[tap] = packed[at : at + VARS, :CH]
        at = 4 * CH + tap * INPUTS
        grad_in[tap] = packed[at : at + INPUTS, CH:]
    energy[...] = packed[6 * CH - 1 :, 127:]


VMEM_LIMIT = 28 * 10**6
VMEM = pl.BlockSpec(memory_space=pltpu.VMEM)
HBM = pl.BlockSpec(memory_space=pltpu.HBM)


def call(kernel, ins, outs, scratch=(), copies=0, flops=10**6, vmem=VMEM_LIMIT):
    held = [pltpu.VMEM(shape, dtype) for shape, dtype in scratch]
    if copies > 0:
        held.append(pltpu.SemaphoreType.DMA((copies,)))
    shapes = [
        pltpu.HBM(shape, dtype) if spec is HBM else jax.ShapeDtypeStruct(shape, dtype)
        for shape, dtype, spec in outs
    ]
    run = pl.pallas_call(
        kernel,
        out_shape=shapes,
        in_specs=ins,
        out_specs=[spec for shape, dtype, spec in outs],
        scratch_shapes=held,
        compiler_params=pltpu.CompilerParams(vmem_limit_bytes=vmem),
        cost_estimate=pl.CostEstimate(flops=flops, bytes_accessed=10**6, transcendentals=0),
    )

    def placed(*arrays):
        return run(
            *[
                pltpu.with_memory_space_constraint(array, pltpu.HBM) if spec is HBM else array
                for array, spec in zip(arrays, ins)
            ]
        )

    return placed


def per_device(members, condition, observed, kernel_in, kernel_mid, kernel_out):
    members = members[0]
    tile = lax.axis_index(TILE)
    table = jnp.asarray(lat_table())
    lat = lax.dynamic_slice_in_dim(table, tile, 1, 0)[0]
    lat = jnp.broadcast_to(lat[:, None], (LAT_AT + ROWS, 128))
    edge = ((HALO + 1, FIELDS, LON), BF16, VMEM)
    own, edge_far, edge_near = call(
        pack_kernel,
        [HBM] * 3,
        [((ROWS, FIELDS, LON), F32, VMEM), edge, edge],
        [((VARS, ROWS, LON), F32), ((COND, ROWS, LON), F32), ((HALF, ROWS, LON), F32)],
        copies=3,
    )(members, condition, observed)
    across = [(i, i + 1) for i in range(1, TILES - 1, 2)]
    far = lax.ppermute(edge_far, TILE, across + [(j, i) for i, j in across])
    near = lax.ppermute(edge_near, "core", [(0, 1), (1, 0)])
    near, lat = lax.optimization_barrier((near, lat))
    w_shapes = [(CH, 9 * FIELDS), (3 * CH, 3 * CH), (48, 3 * CH), (CH, 144), (3 * CH, 3 * CH)]
    w_in, w_mid, w_out, w_back_2, w_back_1 = call(
        weights_kernel,
        [HBM] * 3,
        [(shape, BF16, VMEM) for shape in w_shapes],
        [((9, INPUTS, CH), BF16), ((9, CH, CH), BF16), ((9, VARS, CH), BF16)]
        + [(shape, F32) for shape in w_shapes],
        copies=3,
    )(kernel_in.transpose(0, 2, 1), kernel_mid, kernel_out)
    saved = [
        ((ROWS + 10, 3 * FIELDS, LON), BF16),
        ((ROWS + 8, CH, LON), BF16),
        ((ROWS, CH, LON), F32),
        ((ROWS + 6, CH, LON), BF16),
        ((ROWS + 2, CH, LON), F32),
    ]
    kept_shape = ((4, WIDE, LON), F32)
    send, pushed, kept, stack, hidden_1, slope_1, hidden_2, slope_2 = call(
        forward_kernel,
        [VMEM] * 3 + [HBM] + [VMEM] * 3,
        [((SENT, LON), F32, VMEM), ((VARS, ROWS, LON), F32, VMEM), kept_shape + (VMEM,)]
        + [shape + (VMEM,) for shape in saved],
        [((2 * HALO, FIELDS, LON), F32), ((HALF, ROWS, LON), F32)],
        copies=1,
        flops=10**9,
    )(far, near, own, members, w_in, w_mid, w_out)
    fields = spread(send, "member", MEMBERS)
    (swapped,) = call(
        distance_kernel,
        [VMEM] * 5,
        [((MEMBERS * (NEAR + 1), LON), F32, VMEM)],
        vmem=8 * 10**6,
    )(lat, members, observed, fields, kept)
    swap = [(0, 1), (1, 0)]
    beside = lax.ppermute(swapped, "core", swap)
    partials = swapped[MEMBERS * NEAR :, :128] + beside[MEMBERS * NEAR :, :128]
    totals = spread(partials, "ring", RING)
    mine, theirs = call(
        backward_kernel,
        [VMEM] * 12,
        [((MEMBERS * CHUNK, 128), F32, VMEM)] * 2,
        [
            ((ROWS + 4, 48, LON), BF16),
            ((ROWS + 2, 3 * CH, LON), BF16),
            ((ROWS + 2, 3 * CH, LON), F32),
            ((48, 3 * CH), F32),
            ((3 * CH, 3 * CH), F32),
            ((9 * FIELDS, CH), F32),
            ((6 * CH, 128), F32),
        ],
        flops=10**9,
    )(
        lat, totals, beside, fields, kept, stack, hidden_1, slope_1, hidden_2, slope_2,
        w_back_2, w_back_1,
    )
    mine = mine + lax.ppermute(theirs, "core", swap)
    chunk = jnp.sum(lax.all_to_all(mine.reshape(MEMBERS, CHUNK, 128), "member", 0, 0), 0)
    chunk = jnp.sum(spread(chunk, "ring", RING), 0)
    chunks = spread(chunk, ("member", "core"), 2 * MEMBERS)
    grad_in, grad_mid, grad_out, energy = call(
        unpack_kernel,
        [VMEM],
        [
            ((9, INPUTS, CH), F32, VMEM),
            ((9, CH, CH), F32, VMEM),
            ((9, VARS, CH), F32, VMEM),
            ((1, 1), F32, VMEM),
        ],
        [((6 * CH, 128), F32)],
        vmem=16 * 10**6,
    )(chunks)
    return (pushed[None], energy[0, 0], grad_in.transpose(0, 2, 1), grad_mid, grad_out)


def solution(mesh):
    fine = Mesh(mesh.devices.reshape(MEMBERS, -1, 2), ("member",) + TILE)
    in_specs = (
        P("member", None, TILE, None),
        P(None, TILE, None),
        P(None, TILE, None),
        P(),
        P(),
        P(),
    )
    out_specs = (P("member", None, TILE, None), P(), P(), P(), P())
    return jax.shard_map(
        per_device, mesh=fine, in_specs=in_specs, out_specs=out_specs, check_vma=False
    )
```
